128 devices in a mesh: section: 4 (over y), space: 32 (over z, x, core).
Axes of the slice: x: 4, y: 4, z: 4, core: 2. Of those that a mesh axis runs over, the one named last changes fastest.
Arguments:
- features: bfloat16 [4, 256, 512, 96], P('section', 'space'), may hold values from -6 to 6
- occupancy: int32 [4, 256, 512], P('section', 'space'), may hold values 0 or 1
- neighbors: int32 [6, 256], P(None, 'space'), may hold values from -1 to 255, as said below
- routes: int32 [4, 16384, 1], P('section', 'space'), may hold values from 0 to 63; in each aligned block of 512 rows (0 to 511, 512 to 1023, ..., all dimensions but the last counted through in order) at most 16 rows name the same one
- cotangent: float32 [4, 64, 8, 192], P('section', 'space'), may hold values from -6 to 6
- conv_weight: bfloat16 [2592, 192], replicated, may hold values from -0.125 to 0.125
- conv_bias: float32 [192], replicated, may hold values from -3 to 3
- key_weight: float32 [192, 192], replicated, may hold values from -0.4375 to 0.4375
- value_weight: float32 [192, 192], replicated, may hold values from -0.4375 to 0.4375
- queries: float32 [8, 192], replicated, may hold values from -6 to 6
Outputs:
- pooled: float32 [4, 64, 8, 192], P('section', 'space')
- d_features: bfloat16 [4, 256, 512, 96], P('section', 'space')
- d_conv_weight: float32 [2592, 192], replicated
- d_conv_bias: float32 [192], replicated
- d_key_weight: float32 [192, 192], replicated
- d_value_weight: float32 [192, 192], replicated
- d_queries: float32 [8, 192], replicated
The draws below stay inside these ranges and needn't reach their ends.
Inputs may be any that keep to these rules, and one draw needn't show every extreme that they name: `neighbors`: blocks sit on a map of 8 x 4 tiles, one tile of 2 x 2 x 2 blocks (x, y, z) on each index d of space, tile (d % 8, d // 8). The block beside a block along x lies on the same index or on the next one, along y on the same index or 8 indices away, along z on the same index. Rows 0 to 2 and 3 to 5 are mutual: if the +x block of s is t then the -x block of t is s. `routes`: among one index's rows of one scene, at most 16 name one group, and some group has exactly 16.
All inputs are finite; a program needn't handle non-finite values. No bound on the sum of `occupancy` on one device may be relied on, other than what follows from the above.
Results may differ from the reference program's by a relative error of at most 0.0075.
Values may be sent and summed in bfloat16 or wider, within the bound.
No kernel may reach another device: no remote copies, remote signals or barrier semaphores. Data moves between devices by JAX's collectives and lax.ppermute only.
A program may use at most 128 MiB of HBM per device.

```python
import math
import jax
import jax.numpy as jnp
import numpy as np
from jax import lax

CIN = 96
COUT = 192
NB_DEV = 8
NQ = 8
TILES_Y = 4
TILES_X = 8
SLOTS = 256
ROWS_DEV = 512
ROWS = 16384
GROUPS = 64
CAP = 16
KDIM = 2592
N_SECTION = 4
N_SPACE = 32


def draw_neighbors(key, part):
    key = jax.random.fold_in(key, 11)
    device_keys = jax.random.split(key, N_SPACE)
    orders = jax.vmap(lambda single: jax.random.permutation(single, NB_DEV))(device_keys).astype(jnp.int32)
    device_rows = jnp.arange(N_SPACE, dtype=jnp.int32)[:, None] * jnp.ones((1, NB_DEV), jnp.int32)
    inverse = jnp.zeros((N_SPACE, NB_DEV), jnp.int32).at[device_rows, orders].set(jnp.arange(NB_DEV, dtype=jnp.int32)[None, :] * jnp.ones((N_SPACE, 1), jnp.int32))
    slots = jnp.arange(SLOTS, dtype=jnp.int32)
    device = slots // NB_DEV
    local_slot = slots % NB_DEV
    position = inverse[device, local_slot]
    pos_x = position % 2
    pos_y = position // 2 % 2
    pos_z = position // 4
    height = NB_DEV // 4
    tile_x = device % TILES_X
    tile_y = device // TILES_X

    def locate(valid, other_device, new_x, new_y, new_z):
        safe_device = jnp.clip(other_device, 0, N_SPACE - 1)
        new_position = jnp.clip((new_z * 2 + new_y) * 2 + new_x, 0, NB_DEV - 1)
        found = safe_device * NB_DEV + orders[safe_device, new_position]
        return jnp.where(valid, found, -1)
    plus_x = locate((pos_x < 1) | (tile_x < TILES_X - 1), jnp.where(pos_x < 1, device, device + 1), 1 - pos_x, pos_y, pos_z)
    plus_y = locate((pos_y < 1) | (tile_y < TILES_Y - 1), jnp.where(pos_y < 1, device, device + TILES_X), pos_x, 1 - pos_y, pos_z)
    plus_z = locate(pos_z < height - 1, device, pos_x, pos_y, pos_z + 1)
    minus_x = locate((pos_x > 0) | (tile_x > 0), jnp.where(pos_x > 0, device, device - 1), 1 - pos_x, pos_y, pos_z)
    minus_y = locate((pos_y > 0) | (tile_y > 0), jnp.where(pos_y > 0, device, device - TILES_X), pos_x, 1 - pos_y, pos_z)
    minus_z = locate(pos_z > 0, device, pos_x, pos_y, pos_z - 1)
    return jnp.stack([plus_x, plus_y, plus_z, minus_x, minus_y, minus_z], axis=0).astype(jnp.int32)


def plant(result, rng, smallest, high):
    place = [jax.random.randint(jax.random.fold_in(rng, axis), (), 0, length) for axis, length in enumerate(result.shape)]
    widest = result.shape.index(max(result.shape))
    next_to = place[:widest] + [(place[widest] + 1) % result.shape[widest]] + place[widest + 1:]
    return result.at[tuple(place)].set(smallest).at[tuple(next_to)].set(high)


def block_levels(own_key, dims, cuts, smallest, top_value):
    loudness, own = 1.0, jax.random.fold_in(own_key, 6)
    for dim, blocks in cuts:
        draws = jnp.exp(jax.random.uniform(jax.random.fold_in(own, dim), (blocks,), jnp.float32, smallest / len(cuts), top_value / len(cuts)))
        loudness = loudness * jnp.repeat(draws, dims[dim] // blocks).reshape([-1 if axis == dim else 1 for axis in range(len(dims))])
    return loudness


def routed_block(stream_key, own, number, rows, number_of, top, most, slope):
    sequence = jax.random.permutation(stream_key, number_of)
    heavy_load, usual = portions_of(number_of, rows * top, most, slope, True), portions_of(number_of, rows * top, most, slope, False)
    places = jnp.arange(number_of)

    def named(lengths, turn):
        used = int((lengths > 0).sum())
        fixed = max(1, used // 4)
        shifted = fixed + (places - fixed + turn * (used - fixed)) % max(1, number_of - fixed)
        return jnp.zeros((number_of,), jnp.int32).at[sequence[jnp.where(places < fixed, places, shifted)]].set(jnp.asarray(lengths, jnp.int32))

    lengths = jnp.where(number % 4 == 0, named(heavy_load, number // 4), named(usual, number - number // 4 - 1))
    mixed = jax.random.permutation(jax.random.fold_in(own, 3), number_of)
    giver, sink = mixed[0:number_of // 2 * 2:2], mixed[1:number_of // 2 * 2:2]
    room = jnp.minimum(lengths[giver] - 1, most - lengths[sink]) // 2
    room = jnp.where((giver == sequence[0]) | (sink == sequence[0]) | (lengths[sink] == 0), 0, jnp.maximum(room, 0))
    shifted = jax.random.randint(jax.random.fold_in(own, 4), (number_of // 2,), 0, 1 << 20) % (room + 1)
    lengths = lengths.at[giver].add(-shifted).at[sink].add(shifted)
    items = jnp.searchsorted(jnp.cumsum(lengths), jnp.arange(rows * top), side="right").astype(jnp.int32)
    grid = items.reshape(top, rows).T
    grid = grid[jax.random.permutation(jax.random.fold_in(own, 1), rows)]
    turn = jax.random.randint(jax.random.fold_in(own, 2), (rows, 1), 0, top)
    return jnp.take_along_axis(grid, (jnp.arange(top)[None, :] + turn) % top, axis=1)


def portions_of(count, total, most, lean, full):
    weights = [(1 << 20) // math.isqrt(standing ** lean) + 1 for standing in range(1, count + 1)]
    largest = most if full else min(most, max(-(-total // count), total * weights[0] // sum(weights)))
    least = 1 if total - largest >= count - 1 else 0
    holding, rest = [largest] + [least] * (count - 1), total - largest - least * (count - 1)
    while rest > 0:
        free = [i for i in range(1, count) if holding[i] < largest] or [i for i in range(1, count) if holding[i] < most]
        mass, budget = sum([weights[i] for i in free]), rest
        for i in free:
            more = min(most - holding[i], max(1, budget * weights[i] // mass), rest)
            holding[i] = holding[i] + more
            rest = rest - more
    return np.array(holding)


def centred(key, extent, deviation, limit, cuts=(), kind=jnp.bfloat16):
    result = jax.random.normal(key, extent, jnp.float32) * deviation
    if len(cuts) > 0:
        result = block_levels(key, extent, cuts, -0.22, 0.18) * result
    return jnp.clip(result, min=-limit, max=limit).astype(kind)


def setup_inputs(seed: int = 0) -> dict:
    key_of = jax.random.split(jax.random.key(seed), 11)
    features = centred(key_of[0], (N_SECTION, SLOTS, 512, CIN), 1.0, 6.0, ((0, 4), (1, 32)))
    occupancy = plant((jax.random.randint(key_of[1], (N_SECTION, SLOTS, 512), 0, 2) < 1).astype(jnp.int32), jax.random.fold_in(key_of[1], 1), 0, 1)
    neighbors = draw_neighbors(jax.random.fold_in(key_of[10], 71), 0)
    routes_keys = jax.random.split(jax.random.fold_in(key_of[3], 1), N_SECTION * ROWS // ROWS_DEV)
    routes_turns = jax.random.permutation(jax.random.fold_in(key_of[3], 3), N_SECTION * ROWS // ROWS_DEV)
    routes = jax.vmap(lambda own, number: routed_block(jax.random.fold_in(key_of[3], 2), own, number, ROWS_DEV, GROUPS, 1, CAP, 2))(routes_keys, routes_turns).reshape((N_SECTION, ROWS, 1))
    cotangent = centred(key_of[4], (N_SECTION, GROUPS, NQ, COUT), 1.0, 6.0, ((0, 4), (1, 32)), jnp.float32)
    conv_weight = centred(key_of[5], (KDIM, COUT), KDIM ** -0.5, 0.125)
    conv_bias = centred(key_of[6], (COUT,), 0.5, 3.0, (), jnp.float32)
    key_weight = centred(key_of[7], (COUT, COUT), COUT ** -0.5, 0.4375, (), jnp.float32)
    value_weight = centred(key_of[8], (COUT, COUT), COUT ** -0.5, 0.4375, (), jnp.float32)
    queries = centred(key_of[9], (NQ, COUT), 1.0, 6.0, (), jnp.float32)
    return {"features": features, "occupancy": occupancy, "neighbors": neighbors, "routes": routes, "cotangent": cotangent, "conv_weight": conv_weight, "conv_bias": conv_bias, "key_weight": key_weight, "value_weight": value_weight, "queries": queries}


EPS = 1e-06
TEMPER = 8.0

def extract(blocks):
    amount = blocks.shape[0]
    channels = blocks.shape[-1]
    volume = blocks.reshape(amount, 8, 8, 8, channels)
    padded = jnp.pad(volume, ((0, 0), (1, 2), (1, 2), (1, 2), (0, 0)))
    pieces = []
    for offset_x in range(3):
        for offset_y in range(3):
            for offset_z in range(3):
                pieces.append(padded[:, offset_x:offset_x + 9:2, offset_y:offset_y + 9:2, offset_z:offset_z + 9:2, :])
    stacked = jnp.stack(pieces, axis=4)
    return stacked.reshape(amount, 125, 27 * channels)

def take_plane(plane, source):
    present = source >= 0
    picked = plane[jnp.maximum(source, 0)]
    shaped = present.reshape((-1,) + (1,) * (plane.ndim - 1))
    return jnp.where(shaped, picked, jnp.zeros_like(picked))

def rim_sum(partial_value, lower):
    across_x = partial_value[:, 0:4].at[:, 0].add(take_plane(partial_value[:, 4], lower[0]))
    across_y = across_x[:, :, 0:4].at[:, :, 0].add(take_plane(across_x[:, :, 4], lower[1]))
    across_z = across_y[:, :, :, 0:4].at[:, :, :, 0].add(take_plane(across_y[:, :, :, 4], lower[2]))
    return across_z

def head_terms(inputs, key_weight, value_weight, queries):
    highest = lax.Precision.HIGHEST
    key_rows = jnp.dot(inputs, key_weight, precision=highest)
    value_rows = jnp.dot(inputs, value_weight, precision=highest)
    key_unit = key_rows * lax.rsqrt(lax.optimization_barrier(jnp.sum(key_rows * key_rows, axis=-1, keepdims=True)) + EPS)
    query_unit = queries * lax.rsqrt(lax.optimization_barrier(jnp.sum(queries * queries, axis=-1, keepdims=True)) + EPS)
    weights = jnp.exp(TEMPER * jnp.dot(key_unit, query_unit.T, precision=highest))
    return (weights, value_rows)

def group_sums(inputs, key_weight, value_weight, queries, member):
    highest = lax.Precision.HIGHEST
    weights, value_rows = head_terms(inputs, key_weight, value_weight, queries)
    amount = inputs.shape[0]
    outer = (weights[:, :, None] * value_rows[:, None, :]).reshape(amount, -1)
    numerator = jnp.dot(member.T, outer, precision=highest).reshape(member.shape[1], weights.shape[1], -1)
    mass_sum = jnp.dot(member.T, weights, precision=highest)
    return (numerator, mass_sum)

def scene(features, occupancy, routes, cotangent, neighbors, conv_weight, conv_bias, key_weight, value_weight, queries):
    masked = jnp.where(occupancy[..., None] > 0, features, jnp.zeros_like(features))
    patches = extract(masked)
    blocks_all = patches.shape[0]
    flat = patches.reshape(blocks_all * 125, -1)
    partial_value = jnp.dot(flat, conv_weight, preferred_element_type=jnp.float32).reshape(blocks_all, 5, 5, 5, -1)
    lower = neighbors[3:6]
    summed = rim_sum(partial_value, lower).reshape(blocks_all * 64, -1)
    before = summed + conv_bias
    hidden = lax.optimization_barrier(jax.nn.gelu(before).astype(jnp.bfloat16))
    member = (routes[:, 0][:, None] == jnp.arange(GROUPS)[None, :]).astype(jnp.float32)

    def head(inputs, key_w, value_w, query_w):
        numerator, mass_sum = group_sums(inputs, key_w, value_w, query_w, member)
        return numerator / (1.0 + mass_sum)[:, :, None]
    pooled, head_back = jax.vjp(head, hidden.astype(jnp.float32), key_weight, value_weight, queries)
    d_hidden, d_key, d_value, d_query = head_back(cotangent)
    _, gelu_back = jax.vjp(jax.nn.gelu, before)
    d_before = gelu_back(d_hidden)[0]
    d_bias = lax.optimization_barrier(jnp.sum(d_before, axis=0))
    _, rim_back = jax.vjp(lambda part: rim_sum(part, lower), partial_value)
    d_partial = rim_back(d_before.reshape(blocks_all, 4, 4, 4, -1))[0]
    d_partial = d_partial.astype(jnp.bfloat16).reshape(blocks_all * 125, -1)
    d_weight = jnp.dot(flat.T, d_partial, preferred_element_type=jnp.float32)
    d_patches = jnp.dot(d_partial, conv_weight.T, preferred_element_type=jnp.float32).reshape(blocks_all, 125, -1)
    _, extract_back = jax.vjp(extract, masked.astype(jnp.float32))
    d_masked = extract_back(d_patches)[0]
    d_features = jnp.where(occupancy[..., None] > 0, d_masked, jnp.zeros_like(d_masked)).astype(jnp.bfloat16)
    return (pooled, d_features, d_weight, d_bias, d_key, d_value, d_query)

def reference(features, occupancy, neighbors, routes, cotangent, conv_weight, conv_bias, key_weight, value_weight, queries):

    def single(items):
        feats, occ, route_rows, cot = items
        return scene(feats, occ, route_rows, cot, neighbors, conv_weight, conv_bias, key_weight, value_weight, queries)
    pooled, d_features, d_weight, d_bias, d_key, d_value, d_query = lax.map(single, (features, occupancy, routes, cotangent))
    return (pooled, d_features, lax.optimization_barrier(jnp.sum(d_weight, axis=0)), lax.optimization_barrier(jnp.sum(d_bias, axis=0)), lax.optimization_barrier(jnp.sum(d_key, axis=0)), lax.optimization_barrier(jnp.sum(d_value, axis=0)), lax.optimization_barrier(jnp.sum(d_query, axis=0)))
```

```python
import functools

import jax
import jax.numpy as jnp
from jax import lax
from jax.experimental import pallas as pl
from jax.experimental.pallas import tpu as pltpu
from jax.sharding import Mesh, PartitionSpec as P

EPS = 1e-06
TEMPER = 8.0
CIN, COUT = 96, 192
LANES = 128
SLOTS9 = 9 * LANES
GROUPS, NQ = 64, 8
SHARD = 24
HALF = 64 * SHARD
F32, BF16 = jnp.float32, jnp.bfloat16
SPACE = ("chip", "core")
CHIPS = ("section", "chip")
VMEM_LIMIT = 44 * 1024 * 1024


def params():
    return pltpu.CompilerParams(vmem_limit_bytes=VMEM_LIMIT)


def nn(a, b):
    return lax.dot_general(a, b, (((1,), (0,)), ((), ())), preferred_element_type=F32)


def nt(a, b):
    return lax.dot_general(a, b, (((1,), (1,)), ((), ())), preferred_element_type=F32)


def tn(a, b):
    return lax.dot_general(a, b, (((0,), (0,)), ((), ())), preferred_element_type=F32)


def split(a):
    high = a.astype(BF16)
    return high, (a - high.astype(F32)).astype(BF16)


def find_slots(near_ref, slot_ref):
    here = lax.axis_index("chip") * 2 + lax.axis_index("core")
    for place in range(8):
        slot_ref[place] = 0
    for slot in range(8):
        place = 0
        for axis in range(3):
            beside = near_ref[axis, slot]
            inner = jnp.logical_and(beside >= 0, lax.shift_right_arithmetic(beside, 3) == here)
            place = place + jnp.where(inner, 0, 1 << axis)
        slot_ref[place] = slot


def placed_occupancy(occ_ref, slot_ref):
    rows = [occ_ref[pl.ds(slot_ref[p], 1), :] for p in range(8)]
    return jnp.concatenate(rows, axis=0).astype(F32).T


def place_kernel(near_ref, feat_ref, occ_ref, v_ref, xs_ref, ys_ref, rows_ref, slot_ref):
    find_slots(near_ref, slot_ref)
    occ = placed_occupancy(occ_ref, slot_ref)
    rows_ref[...] = jnp.zeros_like(rows_ref)
    for by in range(2):
        for bx in range(2):
            pair = []
            for bz in range(2):
                place = bx + 2 * by + 4 * bz
                block = feat_ref[slot_ref[place]].astype(F32)
                block = jnp.where(occ[:, place : place + 1] > 0, block, 0.0)
                pair.append(block.reshape(64, 8, CIN))
            rows_ref[:, 0:CIN] = jnp.stack(pair, axis=1).reshape(1024, CIN)
            for pz in range(2):
                part = rows_ref[pl.ds(pz, 512, stride=2), :].reshape(8, 4, 2, 8, LANES)
                for py in range(2):
                    piece = part[:, :, py].reshape(8, 32, LANES).astype(BF16)
                    v_ref[pl.ds(8 * bx, 8), 2 * py + pz, pl.ds(32 * by, 32), :] = piece
            if by == 1:
                edge = [
                    rows_ref[pl.ds(pz, 512, stride=2), :].reshape(8, 8, 8, LANES)[:, 7]
                    for pz in range(2)
                ]
                ys_ref[pl.ds(128 * bx, 128), :] = (
                    jnp.stack(edge, axis=1).reshape(128, LANES).astype(BF16)
                )
    xs_ref[...] = v_ref[15].reshape(256, LANES)


def forward_kernel(
    near_ref, v_ref, xr_ref, yr_ref, xyr_ref, w_ref, bias_ref, key_ref, val_ref, query_ref,
    routes_ref, cot_ref,
    podd_ref, peven_ref, wp_ref, slope_ref, hid_ref, ku_ref, kn_ref, wt_ref, tt_ref, rr_ref,
    send_ref, slot_ref,
):
    find_slots(near_ref, slot_ref)
    wp_ref[...] = jnp.zeros_like(wp_ref)
    for tap in range(27):
        wp_ref[pl.ds(tap * LANES, CIN), :] = w_ref[pl.ds(tap * CIN, CIN), :]
    first = lax.broadcasted_iota(jnp.int32, (64, LANES), 0) % 8 == 0
    for x in range(-1, 16):
        if x < 0:
            planes = xr_ref[...].astype(F32).reshape(4, 64, LANES)
            edge = xyr_ref[...].astype(F32)
        else:
            planes = v_ref[x].astype(F32)
            edge = yr_ref[pl.ds(16 * x, 16), :].astype(F32)
        if x % 2 == 0:
            out_ref, row = peven_ref, 32 * x
        else:
            out_ref, row = podd_ref, 32 * (x + 1)
        for b in range(3):
            for c in range(3):
                py, pz = (b + 1) % 2, (c + 1) % 2
                piece = planes[2 * py + pz]
                if b == 0:
                    piece = jnp.concatenate([edge[8 * pz : 8 * pz + 8], piece[0:56]], axis=0)
                if c == 0:
                    piece = jnp.where(first, 0.0, pltpu.roll(piece, 1, 0))
                column = (3 * b + c) * LANES
                out_ref[pl.ds(row, 64), pl.ds(column, LANES)] = piece.astype(BF16)
    before = (
        nn(podd_ref[0:512, :], wp_ref[0:SLOTS9, :])
        + nn(peven_ref[...], wp_ref[SLOTS9 : 2 * SLOTS9, :])
        + nn(podd_ref[64:576, :], wp_ref[2 * SLOTS9 : 3 * SLOTS9, :])
        + bias_ref[...]
    )
    root = 0.7978845608028654
    square = before * before
    tanh = jnp.tanh(root * before * (1.0 + 0.044715 * square))
    hidden = (0.5 * before * (1.0 + tanh)).astype(BF16)
    slope_ref[...] = 0.5 * (1.0 + tanh) + 0.5 * before * (1.0 - tanh * tanh) * root * (
        1.0 + 3.0 * 0.044715 * square
    )
    hid_ref[...] = hidden

    kh, kl = split(key_ref[...])
    vh, vl = split(val_ref[...])
    keys = nn(hidden, kh) + nn(hidden, kl)
    values = nn(hidden, vh) + nn(hidden, vl)
    key_norm = lax.rsqrt(jnp.sum(keys * keys, axis=-1, keepdims=True) + EPS)
    ku = keys * key_norm
    ku_ref[...] = ku
    kn_ref[...] = key_norm
    queries = query_ref[...]
    qu = queries * lax.rsqrt(jnp.sum(queries * queries, axis=-1, keepdims=True) + EPS)
    uh, ul = split(ku)
    qh, ql = split(qu)
    weights = jnp.exp(TEMPER * (nt(qh, uh) + nt(ql, uh) + nt(qh, ul)))
    wt_ref[...] = weights

    routes = jnp.concatenate(
        [routes_ref[pl.ds(slot_ref[p], 1), :] for p in range(8)], axis=0
    ).astype(BF16)
    row = lax.broadcasted_iota(jnp.int32, (64, 512), 1)
    inside = ((row >> 6) & 3) * 16 + ((row >> 3) & 3) * 4 + (row & 3)
    pick = (inside == lax.broadcasted_iota(jnp.int32, (64, 512), 0)).astype(F32).astype(BF16)
    spread = nn(routes, pick)
    row = lax.broadcasted_iota(jnp.int32, (8, 512), 1)
    place = (row >> 8) + ((row >> 5) & 1) * 2 + ((row >> 2) & 1) * 4
    here = place == lax.broadcasted_iota(jnp.int32, (8, 512), 0)
    group = jnp.sum(jnp.where(here, spread, 0.0), axis=0, keepdims=True)
    group = jnp.broadcast_to(group, (8, 512))
    rr_ref[...] = group

    shares = jnp.concatenate(
        [jnp.where(group == float(g), weights, 0.0) for g in range(GROUPS)], axis=0
    ).astype(BF16)
    vb = values.astype(BF16)
    sums = nn(shares, jnp.concatenate([vb, jnp.ones((512, 64), BF16)], axis=1))
    cot = cot_ref[...]
    inner = jnp.sum(sums[:, 0:COUT] * cot.astype(F32), axis=-1, keepdims=True)
    lane = lax.broadcasted_iota(jnp.int32, (8, 64), 1)
    mass = jnp.zeros((8, 64), F32)
    dots = jnp.zeros((8, 64), F32)
    for g in range(GROUPS):
        mass = jnp.where(lane == g, sums[8 * g : 8 * g + 8, COUT:256], mass)
        dots = jnp.where(lane == g, inner[8 * g : 8 * g + 8], dots)
    table = jnp.concatenate([mass, dots], axis=0)
    send_ref[:, 0:COUT] = sums[:, 0:COUT]
    send_ref[:, COUT:256] = jnp.concatenate([table] * 32, axis=0)

    meets = nt(cot, vb)
    total = jnp.zeros((8, 512), F32)
    for g in range(GROUPS):
        total = total + jnp.where(group == float(g), meets[8 * g : 8 * g + 8], 0.0)
    tt_ref[...] = total


def backward_kernel(
    recv_ref, podd_ref, peven_ref, slope_ref, hid_ref, ku_ref, kn_ref, wt_ref, tt_ref, rr_ref,
    cot_ref, key_ref, val_ref, query_ref,
    pooled_ref, db_ref, xs_ref, ys_ref, keep_ref, give_ref, sum_ref,
):
    got = recv_ref[0:16, :]
    for source in range(1, 32):
        got = got + recv_ref[16 * source : 16 * source + 16, :]
    mass = got[0:8, COUT:256]
    dots = got[8:16, COUT:256]
    here = lax.axis_index("chip") * 2 + lax.axis_index("core")
    lane = lax.broadcasted_iota(jnp.int32, (8, 64), 1)
    own = [
        jnp.sum(jnp.where(lane == 2 * here + i, mass, 0.0), axis=-1, keepdims=True)
        for i in range(2)
    ]
    pooled_ref[...] = got[:, 0:COUT] / (1.0 + jnp.concatenate(own, axis=0))

    inverse = 1.0 / (1.0 + mass)
    d_mass = -dots * inverse * inverse
    ih, il = split(inverse)
    mh, ml = split(d_mass)
    group = rr_ref[...]
    member = (
        lax.broadcasted_iota(jnp.int32, (64, 512), 0).astype(F32)
        == jnp.broadcast_to(group[0:1], (64, 512))
    ).astype(F32).astype(BF16)
    inv_row = nn(ih, member) + nn(il, member)
    dm_row = nn(mh, member) + nn(ml, member)
    weights = wt_ref[...]
    d_cos = TEMPER * weights * (tt_ref[...] * inv_row + dm_row)
    scaled = weights * inv_row
    shares = jnp.concatenate(
        [jnp.where(group == float(g), scaled, 0.0) for g in range(GROUPS)], axis=0
    ).astype(BF16)
    d_value = tn(shares, cot_ref[...]).astype(BF16)

    queries = query_ref[...]
    qn = lax.rsqrt(jnp.sum(queries * queries, axis=-1, keepdims=True) + EPS)
    qu = queries * qn
    ku = ku_ref[...]
    dc = d_cos.astype(BF16)
    d_ku = tn(dc, qu.astype(BF16))
    d_key = kn_ref[...] * (d_ku - ku * jnp.sum(ku * d_ku, axis=-1, keepdims=True))
    d_key = d_key.astype(BF16)
    d_qu = nn(dc, ku.astype(BF16))
    d_query = qn * (d_qu - qu * jnp.sum(qu * d_qu, axis=-1, keepdims=True))

    d_hidden = nt(d_key, key_ref[...].astype(BF16)) + nt(d_value, val_ref[...].astype(BF16))
    d_before = d_hidden * slope_ref[...]
    db = d_before.astype(BF16)
    db_ref[...] = db
    xs_ref[...] = db[0:64]
    ys_ref[...] = d_before.reshape(8, 64, COUT)[:, 0:8].reshape(64, COUT).astype(BF16)

    hid = hid_ref[...]
    parts = (podd_ref[0:512, :], peven_ref[...], podd_ref[64:576, :])
    for a in range(3):
        grad = tn(parts[a], db)
        for tap in range(9):
            sum_ref[pl.ds((9 * a + tap) * CIN, CIN), :] = grad[tap * LANES : tap * LANES + CIN]
    base = 27 * CIN
    sum_ref[pl.ds(base, COUT), :] = tn(hid, d_key)
    sum_ref[pl.ds(base + COUT, COUT), :] = tn(hid, d_value)
    sum_ref[pl.ds(base + 2 * COUT, 8), :] = d_query
    bias = jnp.sum(d_before, axis=0, keepdims=True)
    sum_ref[pl.ds(base + 2 * COUT + 8, 8), :] = jnp.broadcast_to(bias, (8, COUT))
    end = base + 2 * COUT + 16
    sum_ref[pl.ds(end, 2 * HALF - end), :] = jnp.zeros((2 * HALF - end, COUT), F32)
    core = lax.axis_index("core")
    keep_ref[...] = sum_ref[pl.ds(pl.multiple_of(core * HALF, HALF), HALF), :].astype(BF16)
    give_ref[...] = sum_ref[pl.ds(pl.multiple_of((1 - core) * HALF, HALF), HALF), :].astype(BF16)


def add_kernel(a_ref, b_ref, out_ref):
    out_ref[...] = (a_ref[...].astype(F32) + b_ref[...].astype(F32)).astype(BF16)


def total_kernel(recv_ref, out_ref):
    total = jnp.sum(recv_ref[...].astype(F32), axis=0).astype(BF16)
    out_ref[...] = jnp.broadcast_to(total[None], out_ref.shape)


def final_kernel(mine_ref, other_ref, dw_ref, dk_ref, dv_ref, dq_ref, dbias_ref, all_ref):
    core = lax.axis_index("core")
    all_ref[pl.ds(pl.multiple_of(core * HALF, HALF), HALF), :] = mine_ref[...].astype(F32)
    all_ref[pl.ds(pl.multiple_of((1 - core) * HALF, HALF), HALF), :] = other_ref[...].astype(F32)
    base = 27 * CIN
    dw_ref[...] = all_ref[0:base, :]
    dk_ref[...] = all_ref[base : base + COUT, :]
    dv_ref[...] = all_ref[base + COUT : base + 2 * COUT, :]
    dq_ref[...] = all_ref[base + 2 * COUT : base + 2 * COUT + 8, :]
    dbias_ref[...] = all_ref[base + 2 * COUT + 8 : base + 2 * COUT + 9, :]


def spread_kernel(
    near_ref, db_ref, xr_ref, yr_ref, xyr_ref, wp_ref, occ_ref, out_ref,
    ext_ref, even_ref, odd_ref, rows_ref, slot_ref,
):
    find_slots(near_ref, slot_ref)
    occ = placed_occupancy(occ_ref, slot_ref)
    edge = yr_ref[...].astype(F32)
    for jx in range(8):
        ext_ref[pl.ds(72 * jx, 64), :] = db_ref[pl.ds(64 * jx, 64), :].astype(F32)
        ext_ref[pl.ds(72 * jx + 64, 8), :] = edge[8 * jx : 8 * jx + 8]
    ext_ref[pl.ds(576, 64), :] = xr_ref[...].astype(F32)
    ext_ref[pl.ds(640, 8), :] = xyr_ref[...].astype(F32)[0:8]
    low = ext_ref[0:576, :].astype(BF16)
    high = ext_ref[72:648, :].astype(BF16)
    even_ref[...] = nt(low, wp_ref[SLOTS9 : 2 * SLOTS9, :])
    odd_ref[...] = nt(low, wp_ref[2 * SLOTS9 : 3 * SLOTS9, :]) + nt(high, wp_ref[0:SLOTS9, :])
    last = lax.broadcasted_iota(jnp.int32, (32, LANES), 0) % 8 == 7

    def up(piece):
        return jnp.where(last, 0.0, pltpu.roll(piece, 31, 0))

    for by in range(2):
        for bx in range(2):
            for xl in range(8):
                x = 8 * bx + xl
                src_ref = even_ref if x % 2 == 0 else odd_ref
                start = 72 * (x // 2) + 32 * by

                def tap(b, c, later, src_ref=src_ref, start=start):
                    return src_ref[pl.ds(start + 8 * later, 32), pl.ds((3 * b + c) * LANES, LANES)]

                e00 = tap(1, 1, 0)
                e01 = tap(1, 2, 0) + up(tap(1, 0, 0))
                e10 = tap(2, 1, 0) + tap(0, 1, 1)
                e11 = tap(2, 2, 0) + tap(0, 2, 1) + up(tap(2, 0, 0) + tap(0, 0, 1))
                for pz, (ye, yo) in enumerate(((e00, e10), (e01, e11))):
                    both = jnp.stack([ye.reshape(4, 8, LANES), yo.reshape(4, 8, LANES)], axis=1)
                    rows_ref[pl.ds(128 * xl + pz, 64, stride=2), :] = both.reshape(64, LANES)
            tile = rows_ref[...].reshape(64, 2, 8, LANES)
            for bz in range(2):
                place = bx + 2 * by + 4 * bz
                block = tile[:, bz].reshape(512, LANES)[:, 0:CIN]
                block = jnp.where(occ[:, place : place + 1] > 0, block, 0.0)
                out_ref[slot_ref[place]] = block.astype(BF16)


def vm():
    return pl.BlockSpec(memory_space=pltpu.VMEM)


def sm():
    return pl.BlockSpec(memory_space=pltpu.SMEM)


def like(shape, dtype=F32):
    return jax.ShapeDtypeStruct(shape, dtype)


def call(kernel, first_scalar, outs, scratch, *args):
    in_specs = [sm() if i == 0 and first_scalar else vm() for i in range(len(args))]
    return pl.pallas_call(
        kernel,
        out_shape=outs,
        in_specs=in_specs,
        out_specs=jax.tree.map(lambda _: vm(), outs),
        scratch_shapes=scratch,
        compiler_params=params(),
        name=kernel.__name__,
    )(*args)


def shift(shard, by_x, by_y):
    pairs = []
    for index in range(32):
        tx, ty = index % 8 + by_x, index // 8 + by_y
        if 0 <= tx < 8 and 0 <= ty < 4:
            pairs.append((index, ty * 8 + tx))
    return lax.ppermute(shard, SPACE, pairs)


def on_device(
    features, occupancy, neighbors, routes, cotangent, conv_weight, conv_bias,
    key_weight, value_weight, queries,
):
    features, occupancy = features[0], occupancy[0]
    slots = pltpu.SMEM((8,), jnp.int32)
    cot = cotangent[0].astype(BF16).reshape(1, 16, COUT)
    cot_all = lax.all_to_all(jnp.broadcast_to(cot, (32, 16, COUT)), SPACE, 0, 0, tiled=True)
    cot_all = cot_all.reshape(512, COUT)

    v, xs, ys = call(
        place_kernel, True,
        [like((16, 4, 64, LANES), BF16), like((256, LANES), BF16), like((256, LANES), BF16)],
        [pltpu.VMEM((1024, LANES), F32), slots],
        neighbors, features, occupancy,
    )
    xr = shift(xs, 1, 0)
    yr = shift(ys, 0, 1)
    xyr = shift(ys[240:256], 1, 1)
    podd, peven, wp, slope, hid, ku, kn, wt, tt, rr, send = call(
        forward_kernel, True,
        [
            like((576, SLOTS9), BF16), like((512, SLOTS9), BF16), like((27 * LANES, COUT), BF16),
            like((512, COUT)), like((512, COUT), BF16), like((512, COUT)), like((512, 1)),
            like((8, 512)), like((8, 512)), like((8, 512)), like((512, 256)),
        ],
        [slots],
        neighbors, v, xr, yr, xyr, conv_weight, conv_bias.reshape(1, COUT), key_weight,
        value_weight, queries, routes.reshape(8, 64), cot_all,
    )
    recv = lax.all_to_all(send.reshape(32, 16, 256), SPACE, 0, 0, tiled=True).reshape(512, 256)
    pooled, db, bxs, bys, keep, give = call(
        backward_kernel, False,
        [
            like((16, COUT)), like((512, COUT), BF16), like((64, COUT), BF16),
            like((64, COUT), BF16), like((HALF, COUT), BF16), like((HALF, COUT), BF16),
        ],
        [pltpu.VMEM((2 * HALF, COUT), F32)],
        recv, podd, peven, slope, hid, ku, kn, wt, tt, rr, cot_all, key_weight, value_weight,
        queries,
    )
    swap = [(0, 1), (1, 0)]
    taken = lax.ppermute(give, "core", swap)
    half = call(add_kernel, False, like((HALF, COUT), BF16), [], keep, taken)
    pieces = lax.all_to_all(half.reshape(64, SHARD, COUT), CHIPS, 0, 0, tiled=True)
    bxr = shift(bxs, -1, 0)
    byr = shift(bys, 0, -1)
    bxyr = shift(bys[0:16], -1, -1)
    d_features = call(
        spread_kernel, True, like((8, 512, CIN), BF16),
        [
            pltpu.VMEM((648, COUT), F32), pltpu.VMEM((576, SLOTS9), F32),
            pltpu.VMEM((576, SLOTS9), F32), pltpu.VMEM((1024, LANES), F32), slots,
        ],
        neighbors, db, bxr, byr, bxyr, wp, occupancy,
    )
    copies = call(total_kernel, False, like((64, SHARD, COUT), BF16), [], pieces)
    mine = lax.all_to_all(copies, CHIPS, 0, 0, tiled=True).reshape(HALF, COUT)
    other = lax.ppermute(mine, "core", swap)
    d_weight, d_key, d_value, d_query, d_bias = call(
        final_kernel, False,
        [
            like((27 * CIN, COUT)), like((COUT, COUT)), like((COUT, COUT)), like((NQ, COUT)),
            like((1, COUT)),
        ],
        [pltpu.VMEM((2 * HALF, COUT), F32)],
        mine, other,
    )
    return (
        pooled.reshape(1, 2, NQ, COUT), d_features[None], d_weight, d_bias.reshape(COUT),
        d_key, d_value, d_query,
    )


def solution(mesh):
    fine = Mesh(mesh.devices.reshape(4, 16, 2), ("section", "chip", "core"))
    in_specs = (
        P("section", SPACE, None, None),
        P("section", SPACE, None),
        P(None, SPACE),
        P("section", SPACE, None),
        P("section", SPACE, None, None),
        P(),
        P(),
        P(),
        P(),
        P(),
    )
    out_specs = (
        P("section", SPACE, None, None),
        P("section", SPACE, None, None),
        P(),
        P(),
        P(),
        P(),
        P(),
    )
    return jax.shard_map(
        on_device, mesh=fine, in_specs=in_specs, out_specs=out_specs, check_vma=False
    )
```

```python
import functools

import jax
import jax.numpy as jnp
from jax import lax
from jax.experimental import pallas as pl
from jax.experimental.pallas import tpu as pltpu
from jax.sharding import Mesh, PartitionSpec as P

EPS = 1e-06
TEMPER = 8.0
CIN, COUT = 96, 192
LANES = 128
SLOTS9 = 9 * LANES
GROUPS, NQ = 64, 8
KDIM = 27 * CIN
SHARD = 40
HALF = 64 * SHARD
WIDE = 24 * LANES
F32, BF16 = jnp.float32, jnp.bfloat16
SPACE = ("chip", "core")
CHIPS = ("section", "chip")
VMEM_LIMIT = 44 * 1024 * 1024


def params():
    return pltpu.CompilerParams(vmem_limit_bytes=VMEM_LIMIT)


def nn(a, b):
    return lax.dot_general(a, b, (((1,), (0,)), ((), ())), preferred_element_type=F32)


def nt(a, b):
    return lax.dot_general(a, b, (((1,), (1,)), ((), ())), preferred_element_type=F32)


def tn(a, b):
    return lax.dot_general(a, b, (((0,), (0,)), ((), ())), preferred_element_type=F32)


def split(a):
    high = a.astype(BF16)
    return high, (a - high.astype(F32)).astype(BF16)


def find_slots(near_ref, slot_ref):
    here = lax.axis_index("chip") * 2 + lax.axis_index("core")
    for place in range(8):
        slot_ref[place] = 0
    for slot in range(8):
        place = 0
        for axis in range(3):
            beside = near_ref[axis, slot]
            inner = jnp.logical_and(beside >= 0, lax.shift_right_arithmetic(beside, 3) == here)
            place = place + jnp.where(inner, 0, 1 << axis)
        slot_ref[place] = slot


def place_kernel(
    near_ref, feat_ref, occ_ref, cot_ref, v_ref, xs_ref, ys_ref, early_ref, rows_ref, slot_ref
):
    find_slots(near_ref, slot_ref)
    rows_ref[...] = jnp.zeros_like(rows_ref)
    for by in range(2):
        for bx in range(2):
            pair = []
            for bz in range(2):
                place = bx + 2 * by + 4 * bz
                slot = slot_ref[place]
                block = feat_ref[slot].astype(F32)
                block = jnp.where(occ_ref[pl.ds(slot, 1), :] > 0, block, 0.0).T
                pair.append(block.reshape(64, 8, CIN))
            rows_ref[:, 0:CIN] = jnp.stack(pair, axis=1).reshape(1024, CIN)
            for pz in range(2):
                part = rows_ref[pl.ds(pz, 512, stride=2), :].reshape(8, 4, 2, 8, LANES)
                for py in range(2):
                    piece = part[:, :, py].reshape(8, 32, LANES).astype(BF16)
                    v_ref[pl.ds(8 * bx, 8), 2 * py + pz, pl.ds(32 * by, 32), :] = piece
            if by == 1:
                edge = [
                    rows_ref[pl.ds(pz, 512, stride=2), :].reshape(8, 8, 8, LANES)[:, 7]
                    for pz in range(2)
                ]
                ys_ref[pl.ds(128 * bx, 128), :] = (
                    jnp.stack(edge, axis=1).reshape(128, LANES).astype(BF16)
                )
    xs_ref[...] = v_ref[15].reshape(256, LANES)
    early = jnp.concatenate(
        [cot_ref[...].astype(BF16), jnp.zeros((16, 64), BF16), ys_ref[240:256, :]], axis=1
    )
    early_ref[...] = jnp.broadcast_to(early[None], early_ref.shape)


def forward_kernel(
    near_ref, v_ref, xr_ref, yr_ref, w_ref, bias_ref, key_ref, val_ref, query_ref,
    routes_ref, early_ref,
    podd_ref, peven_ref, wp_ref, slope_ref, hid_ref, ku_ref, kn_ref, wt_ref, tt_ref, rr_ref,
    send_ref, slot_ref, routes8_ref,
):
    find_slots(near_ref, slot_ref)
    wp_ref[...] = jnp.zeros_like(wp_ref)
    for tap in range(27):
        wp_ref[:, pl.ds(tap * LANES, CIN)] = w_ref[:, pl.ds(tap * CIN, CIN)]
    here = lax.axis_index("chip") * 2 + lax.axis_index("core")
    inner = jnp.logical_and(here >= 8, lax.rem(here, 8) > 0)
    corner = early_ref[pl.ds(pl.multiple_of(16 * jnp.maximum(here - 9, 0), 16), 16), 256:384]
    corner = jnp.where(inner, corner.astype(F32), 0.0)
    first = lax.broadcasted_iota(jnp.int32, (64, LANES), 0) % 8 == 0
    for x in range(-1, 16):
        if x < 0:
            planes = xr_ref[...].astype(F32).reshape(4, 64, LANES)
            edge = corner
        else:
            planes = v_ref[x].astype(F32)
            edge = yr_ref[pl.ds(16 * x, 16), :].astype(F32)
        if x % 2 == 0:
            out_ref, row = peven_ref, 32 * x
        else:
            out_ref, row = podd_ref, 32 * (x + 1)
        for b in range(3):
            for c in range(3):
                py, pz = (b + 1) % 2, (c + 1) % 2
                piece = planes[2 * py + pz]
                if b == 0:
                    piece = jnp.concatenate([edge[8 * pz : 8 * pz + 8], piece[0:56]], axis=0)
                if c == 0:
                    piece = jnp.where(first, 0.0, pltpu.roll(piece, 1, 0))
                column = (3 * b + c) * LANES
                out_ref[pl.ds(row, 64), pl.ds(column, LANES)] = piece.astype(BF16)
    before = (
        nt(podd_ref[0:512, :], wp_ref[:, 0:SLOTS9])
        + nt(peven_ref[...], wp_ref[:, SLOTS9 : 2 * SLOTS9])
        + nt(podd_ref[64:576, :], wp_ref[:, 2 * SLOTS9 : 3 * SLOTS9])
        + bias_ref[...]
    )
    root = 0.7978845608028654
    square = before * before
    tanh = jnp.tanh(root * before * (1.0 + 0.044715 * square))
    hidden = (0.5 * before * (1.0 + tanh)).astype(BF16)
    slope_ref[...] = 0.5 * (1.0 + tanh) + 0.5 * before * (1.0 - tanh * tanh) * root * (
        1.0 + 3.0 * 0.044715 * square
    )
    hid_ref[...] = hidden

    kh, kl = split(key_ref[...])
    vh, vl = split(val_ref[...])
    keys = nn(hidden, kh) + nn(hidden, kl)
    values = nn(hidden, vh) + nn(hidden, vl)
    key_norm = lax.rsqrt(jnp.sum(keys * keys, axis=-1, keepdims=True) + EPS)
    ku = keys * key_norm
    ku_ref[...] = ku
    kn_ref[...] = key_norm
    queries = query_ref[...]
    qu = queries * lax.rsqrt(jnp.sum(queries * queries, axis=-1, keepdims=True) + EPS)
    uh, ul = split(ku)
    qh, ql = split(qu)
    weights = jnp.exp(TEMPER * (nt(qh, uh) + nt(ql, uh) + nt(qh, ul)))
    wt_ref[...] = weights

    for slot in range(8):
        routes8_ref[slot : slot + 1, :] = routes_ref[:, 64 * slot : 64 * slot + 64]
    routes = jnp.concatenate(
        [routes8_ref[pl.ds(slot_ref[p], 1), :] for p in range(8)], axis=0
    ).astype(BF16)
    row = lax.broadcasted_iota(jnp.int32, (64, 512), 1)
    inside = ((row >> 6) & 3) * 16 + ((row >> 3) & 3) * 4 + (row & 3)
    pick = (inside == lax.broadcasted_iota(jnp.int32, (64, 512), 0)).astype(F32).astype(BF16)
    spread = nn(routes, pick)
    row = lax.broadcasted_iota(jnp.int32, (8, 512), 1)
    place = (row >> 8) + ((row >> 5) & 1) * 2 + ((row >> 2) & 1) * 4
    here = place == lax.broadcasted_iota(jnp.int32, (8, 512), 0)
    group = jnp.sum(jnp.where(here, spread, 0.0), axis=0, keepdims=True)
    group = jnp.broadcast_to(group, (8, 512))
    rr_ref[...] = group

    shares = jnp.concatenate(
        [jnp.where(group == float(g), weights, 0.0) for g in range(GROUPS)], axis=0
    ).astype(BF16)
    vb = values.astype(BF16)
    sums = nn(shares, jnp.concatenate([vb, jnp.ones((512, 64), BF16)], axis=1))
    cot = early_ref[:, 0:COUT]
    inner = jnp.sum(sums[:, 0:COUT] * cot.astype(F32), axis=-1, keepdims=True)
    lane = lax.broadcasted_iota(jnp.int32, (8, 64), 1)
    mass = jnp.zeros((8, 64), F32)
    dots = jnp.zeros((8, 64), F32)
    for g in range(GROUPS):
        mass = jnp.where(lane == g, sums[8 * g : 8 * g + 8, COUT:256], mass)
        dots = jnp.where(lane == g, inner[8 * g : 8 * g + 8], dots)
    table = jnp.concatenate([mass, dots], axis=0)
    send_ref[:, 0:COUT] = sums[:, 0:COUT].astype(BF16)
    send_ref[:, COUT:256] = jnp.concatenate([table.astype(BF16)] * 32, axis=0)

    meets = nt(cot, vb)
    total = jnp.zeros((8, 512), F32)
    for g in range(GROUPS):
        total = total + jnp.where(group == float(g), meets[8 * g : 8 * g + 8], 0.0)
    tt_ref[...] = total


def backward_kernel(
    recv_ref, podd_ref, peven_ref, slope_ref, hid_ref, ku_ref, kn_ref, wt_ref, tt_ref, rr_ref,
    early_ref, key_ref, val_ref, query_ref,
    pooled_ref, db_ref, xs_ref, ys_ref, keep_ref, give_ref, sum_ref,
):
    got = jnp.sum(recv_ref[...].reshape(32, 16, 256).astype(F32), axis=0)
    mass = got[0:8, COUT:256]
    dots = got[8:16, COUT:256]
    here = lax.axis_index("chip") * 2 + lax.axis_index("core")
    lane = lax.broadcasted_iota(jnp.int32, (8, 64), 1)
    own = [
        jnp.sum(jnp.where(lane == 2 * here + i, mass, 0.0), axis=-1, keepdims=True)
        for i in range(2)
    ]
    pooled_ref[...] = got[:, 0:COUT] / (1.0 + jnp.concatenate(own, axis=0))

    inverse = 1.0 / (1.0 + mass)
    d_mass = -dots * inverse * inverse
    ih, il = split(inverse)
    mh, ml = split(d_mass)
    group = rr_ref[...]
    member = (
        lax.broadcasted_iota(jnp.int32, (64, 512), 0).astype(F32)
        == jnp.broadcast_to(group[0:1], (64, 512))
    ).astype(F32).astype(BF16)
    inv_row = nn(ih, member) + nn(il, member)
    dm_row = nn(mh, member) + nn(ml, member)
    weights = wt_ref[...]
    d_cos = TEMPER * weights * (tt_ref[...] * inv_row + dm_row)
    scaled = weights * inv_row
    shares = jnp.concatenate(
        [jnp.where(group == float(g), scaled, 0.0) for g in range(GROUPS)], axis=0
    ).astype(BF16)
    d_value = tn(shares, early_ref[:, 0:COUT]).astype(BF16)

    queries = query_ref[...]
    qn = lax.rsqrt(jnp.sum(queries * queries, axis=-1, keepdims=True) + EPS)
    qu = queries * qn
    ku = ku_ref[...]
    dc = d_cos.astype(BF16)
    d_ku = tn(dc, qu.astype(BF16))
    d_key = kn_ref[...] * (d_ku - ku * jnp.sum(ku * d_ku, axis=-1, keepdims=True))
    d_key = d_key.astype(BF16)
    d_qu = nn(dc, ku.astype(BF16))
    d_query = qn * (d_qu - qu * jnp.sum(qu * d_qu, axis=-1, keepdims=True))

    d_hidden = nt(d_key, key_ref[...].astype(BF16)) + nt(d_value, val_ref[...].astype(BF16))
    d_before = d_hidden * slope_ref[...]
    db = d_before.astype(BF16)
    db_ref[...] = db
    xs_ref[...] = db[0:64]
    ys_ref[...] = d_before.reshape(8, 64, COUT)[:, 0:8].reshape(64, COUT).astype(BF16)

    hid = hid_ref[...]
    parts = (podd_ref[0:512, :], peven_ref[...], podd_ref[64:576, :])
    for a in range(3):
        grad = tn(db, parts[a])
        for tap in range(9):
            piece = grad[:, tap * LANES : tap * LANES + CIN]
            sum_ref[:, pl.ds((9 * a + tap) * CIN, CIN)] = piece
    sum_ref[:, KDIM : KDIM + COUT] = tn(hid, d_key)
    sum_ref[:, KDIM + COUT : KDIM + 2 * COUT] = tn(hid, d_value)
    bias = jnp.broadcast_to(jnp.sum(d_before, axis=0, keepdims=True), (8, COUT))
    small = [d_query[:, 0:CIN], d_query[:, CIN:COUT], bias[:, 0:CIN], bias[:, CIN:COUT]]
    small = jnp.concatenate(small + [jnp.zeros((COUT - 32, CIN), F32)], axis=0)
    sum_ref[:, KDIM + 2 * COUT : WIDE] = small
    low = lax.axis_index("core") == 0
    for t in range(12):
        left = sum_ref[:, LANES * t : LANES * (t + 1)]
        right = sum_ref[:, LANES * (t + 12) : LANES * (t + 13)]
        keep_ref[COUT * t : COUT * (t + 1), :] = jnp.where(low, left, right)
        give_ref[COUT * t : COUT * (t + 1), :] = jnp.where(low, right, left).astype(BF16)
    rest = HALF - 12 * COUT
    keep_ref[12 * COUT : HALF, :] = jnp.zeros((rest, LANES), F32)
    give_ref[12 * COUT : HALF, :] = jnp.zeros((rest, LANES), BF16)


def add_kernel(a_ref, b_ref, out_ref):
    out_ref[...] = (a_ref[...] + b_ref[...].astype(F32)).astype(BF16)


def total_kernel(recv_ref, out_ref):
    total = jnp.sum(recv_ref[...].astype(F32), axis=0).astype(BF16)
    out_ref[...] = jnp.broadcast_to(total[None], out_ref.shape)


def final_kernel(mine_ref, other_ref, dw_ref, dk_ref, dv_ref, dq_ref, dbias_ref, all_ref):
    low = lax.axis_index("core") == 0
    for t in range(12):
        mine = mine_ref[COUT * t : COUT * (t + 1), :].astype(F32)
        other = other_ref[COUT * t : COUT * (t + 1), :].astype(F32)
        all_ref[:, LANES * t : LANES * (t + 1)] = jnp.where(low, mine, other)
        all_ref[:, LANES * (t + 12) : LANES * (t + 13)] = jnp.where(low, other, mine)
    dw_ref[...] = all_ref[:, 0:KDIM]
    dk_ref[...] = all_ref[:, KDIM : KDIM + COUT]
    dv_ref[...] = all_ref[:, KDIM + COUT : KDIM + 2 * COUT]
    small = all_ref[0:32, KDIM + 2 * COUT : WIDE]
    dq_ref[...] = jnp.concatenate([small[0:8], small[8:16]], axis=1)
    dbias_ref[...] = jnp.concatenate([small[16:17], small[24:25]], axis=1)


def spread_kernel(
    near_ref, db_ref, xr_ref, yr_ref, xyr_ref, wp_ref, occ_ref, out_ref,
    ext_ref, even_ref, odd_ref, rows_ref, slot_ref,
):
    find_slots(near_ref, slot_ref)
    edge = yr_ref[...].astype(F32)
    for jx in range(8):
        ext_ref[pl.ds(72 * jx, 64), :] = db_ref[pl.ds(64 * jx, 64), :].astype(F32)
        ext_ref[pl.ds(72 * jx + 64, 8), :] = edge[8 * jx : 8 * jx + 8]
    ext_ref[pl.ds(576, 64), :] = xr_ref[...].astype(F32)
    ext_ref[pl.ds(640, 8), :] = xyr_ref[...].astype(F32)[0:8]
    low = ext_ref[0:576, :].astype(BF16)
    high = ext_ref[72:648, :].astype(BF16)
    even_ref[...] = nn(low, wp_ref[:, SLOTS9 : 2 * SLOTS9])
    odd_ref[...] = nn(low, wp_ref[:, 2 * SLOTS9 : 3 * SLOTS9]) + nn(high, wp_ref[:, 0:SLOTS9])
    last = lax.broadcasted_iota(jnp.int32, (32, LANES), 0) % 8 == 7

    def up(piece):
        return jnp.where(last, 0.0, pltpu.roll(piece, 31, 0))

    for by in range(2):
        for bx in range(2):
            for xl in range(8):
                x = 8 * bx + xl
                src_ref = even_ref if x % 2 == 0 else odd_ref
                start = 72 * (x // 2) + 32 * by

                def tap(b, c, later, src_ref=src_ref, start=start):
                    return src_ref[pl.ds(start + 8 * later, 32), pl.ds((3 * b + c) * LANES, LANES)]

                e00 = tap(1, 1, 0)
                e01 = tap(1, 2, 0) + up(tap(1, 0, 0))
                e10 = tap(2, 1, 0) + tap(0, 1, 1)
                e11 = tap(2, 2, 0) + tap(0, 2, 1) + up(tap(2, 0, 0) + tap(0, 0, 1))
                for pz, (ye, yo) in enumerate(((e00, e10), (e01, e11))):
                    both = jnp.stack([ye.reshape(4, 8, LANES), yo.reshape(4, 8, LANES)], axis=1)
                    rows_ref[pl.ds(128 * xl + pz, 64, stride=2), :] = both.reshape(64, LANES)
            tile = rows_ref[...].reshape(64, 2, 8, LANES)
            for bz in range(2):
                place = bx + 2 * by + 4 * bz
                slot = slot_ref[place]
                block = tile[:, bz].reshape(512, LANES).T[0:CIN]
                block = jnp.where(occ_ref[pl.ds(slot, 1), :] > 0, block, 0.0)
                out_ref[slot] = block.astype(BF16)


def vm():
    return pl.BlockSpec(memory_space=pltpu.VMEM)


def sm():
    return pl.BlockSpec(memory_space=pltpu.SMEM)


def like(shape, dtype=F32):
    return jax.ShapeDtypeStruct(shape, dtype)


def call(kernel, first_scalar, outs, scratch, *args):
    in_specs = [sm() if i == 0 and first_scalar else vm() for i in range(len(args))]
    return pl.pallas_call(
        kernel,
        out_shape=outs,
        in_specs=in_specs,
        out_specs=jax.tree.map(lambda _: vm(), outs),
        scratch_shapes=scratch,
        compiler_params=params(),
        name=kernel.__name__,
    )(*args)


def shift(shard, by_x, by_y):
    pairs = []
    for index in range(32):
        tx, ty = index % 8 + by_x, index // 8 + by_y
        if 0 <= tx < 8 and 0 <= ty < 4:
            pairs.append((index, ty * 8 + tx))
    return lax.ppermute(shard, SPACE, pairs)


def on_device(
    features, occupancy, neighbors, routes, cotangent, conv_weight, conv_bias,
    key_weight, value_weight, queries,
):
    features, occupancy = jnp.swapaxes(features[0], 1, 2), occupancy[0]
    slots = pltpu.SMEM((8,), jnp.int32)
    v, xs, ys, early = call(
        place_kernel, True,
        [
            like((16, 4, 64, LANES), BF16), like((256, LANES), BF16), like((256, LANES), BF16),
            like((32, 16, 3 * LANES), BF16),
        ],
        [pltpu.VMEM((1024, LANES), F32), slots],
        neighbors, features, occupancy, cotangent.reshape(16, COUT),
    )
    early = lax.all_to_all(early, SPACE, 0, 0, tiled=True).reshape(512, 3 * LANES)
    xr = shift(xs, 1, 0)
    yr = shift(ys, 0, 1)
    podd, peven, wp, slope, hid, ku, kn, wt, tt, rr, send = call(
        forward_kernel, True,
        [
            like((576, SLOTS9), BF16), like((512, SLOTS9), BF16), like((COUT, 27 * LANES), BF16),
            like((512, COUT)), like((512, COUT), BF16), like((512, COUT)), like((512, 1)),
            like((8, 512)), like((8, 512)), like((8, 512)), like((512, 256), BF16),
        ],
        [slots, pltpu.VMEM((8, 64), jnp.int32)],
        neighbors, v, xr, yr, conv_weight.T, conv_bias.reshape(1, COUT), key_weight,
        value_weight, queries, routes.reshape(1, 512), early,
    )
    recv = lax.all_to_all(send.reshape(32, 16, 256), SPACE, 0, 0, tiled=True).reshape(512, 256)
    pooled, db, bxs, bys, keep, give = call(
        backward_kernel, False,
        [
            like((16, COUT)), like((512, COUT), BF16), like((64, COUT), BF16),
            like((64, COUT), BF16), like((HALF, LANES)), like((HALF, LANES), BF16),
        ],
        [pltpu.VMEM((COUT, WIDE), F32)],
        recv, podd, peven, slope, hid, ku, kn, wt, tt, rr, early, key_weight, value_weight,
        queries,
    )
    swap = [(0, 1), (1, 0)]
    taken = lax.ppermute(give, "core", swap)
    half = call(add_kernel, False, like((HALF, LANES), BF16), [], keep, taken)
    pieces = lax.all_to_all(half.reshape(64, SHARD, LANES), CHIPS, 0, 0, tiled=True)
    bxr = shift(bxs, -1, 0)
    byr = shift(bys, 0, -1)
    bxyr = shift(bys[0:16], -1, -1)
    d_features = call(
        spread_kernel, True, like((8, CIN, 512), BF16),
        [
            pltpu.VMEM((648, COUT), F32), pltpu.VMEM((576, SLOTS9), F32),
            pltpu.VMEM((576, SLOTS9), F32), pltpu.VMEM((1024, LANES), F32), slots,
        ],
        neighbors, db, bxr, byr, bxyr, wp, occupancy,
    )
    pieces, d_features = lax.optimization_barrier((pieces, d_features))
    copies = call(total_kernel, False, like((64, SHARD, LANES), BF16), [], pieces)
    mine = lax.all_to_all(copies, CHIPS, 0, 0, tiled=True).reshape(HALF, LANES)
    other = lax.ppermute(mine, "core", swap)
    d_weight, d_key, d_value, d_query, d_bias = call(
        final_kernel, False,
        [
            like((COUT, KDIM)), like((COUT, COUT)), like((COUT, COUT)), like((NQ, COUT)),
            like((1, COUT)),
        ],
        [pltpu.VMEM((COUT, WIDE), F32)],
        mine, other,
    )
    return (
        pooled.reshape(1, 2, NQ, COUT), jnp.swapaxes(d_features, 1, 2)[None], d_weight.T,
        d_bias.reshape(COUT), d_key, d_value, d_query,
    )


def solution(mesh):
    fine = Mesh(mesh.devices.reshape(4, 16, 2), ("section", "chip", "core"))
    in_specs = (
        P("section", SPACE, None, None),
        P("section", SPACE, None),
        P(None, SPACE),
        P("section", SPACE, None),
        P("section", SPACE, None, None),
        P(),
        P(),
        P(),
        P(),
        P(),
    )
    out_specs = (
        P("section", SPACE, None, None),
        P("section", SPACE, None, None),
        P(),
        P(),
        P(),
        P(),
        P(),
    )
    return jax.shard_map(
        on_device, mesh=fine, in_specs=in_specs, out_specs=out_specs, check_vma=False
    )
```

```python
import functools

import jax
import jax.numpy as jnp
from jax import lax
from jax.experimental import pallas as pl
from jax.experimental.pallas import tpu as pltpu
from jax.sharding import Mesh, PartitionSpec as P

EPS = 1e-06
TEMPER = 8.0
CIN, COUT = 96, 192
LANES = 128
SLOTS9 = 9 * LANES
GROUPS, NQ = 64, 8
KDIM = 27 * CIN
SHARD = 40
HALF = 64 * SHARD
WIDE = 24 * LANES
F32, BF16 = jnp.float32, jnp.bfloat16
SPACE = ("chip", "core")
CHIPS = ("section", "chip")
VMEM_LIMIT = 44 * 1024 * 1024


def params():
    return pltpu.CompilerParams(vmem_limit_bytes=VMEM_LIMIT)


def nn(a, b):
    return lax.dot_general(a, b, (((1,), (0,)), ((), ())), preferred_element_type=F32)


def nt(a, b):
    return lax.dot_general(a, b, (((1,), (1,)), ((), ())), preferred_element_type=F32)


def tn(a, b):
    return lax.dot_general(a, b, (((0,), (0,)), ((), ())), preferred_element_type=F32)


def split(a):
    high = a.astype(BF16)
    return high, (a - high.astype(F32)).astype(BF16)


def find_slots(near_ref, slot_ref):
    here = lax.axis_index("chip") * 2 + lax.axis_index("core")
    for place in range(8):
        slot_ref[place] = 0
    for slot in range(8):
        place = 0
        for axis in range(3):
            beside = near_ref[axis, slot]
            inner = jnp.logical_and(beside >= 0, lax.shift_right_arithmetic(beside, 3) == here)
            place = place + jnp.where(inner, 0, 1 << axis)
        slot_ref[place] = slot


def place_kernel(
    near_hbm, feat_hbm, occ_hbm, cot_hbm, v_ref, xs_ref, ys_ref, early_ref,
    near_ref, feat_ref, occ_ref, cot_ref, rows_ref, slot_ref, sems,
):
    copies = [
        pltpu.make_async_copy(source, target, sems.at[i])
        for i, (source, target) in enumerate(
            (
                (near_hbm, near_ref), (feat_hbm, feat_ref), (occ_hbm, occ_ref), (cot_hbm, cot_ref),
            )
        )
    ]
    for copy in copies:
        copy.start()
    rows_ref[...] = jnp.zeros_like(rows_ref)
    for copy in copies:
        copy.wait()
    find_slots(near_ref, slot_ref)
    for by in range(2):
        for bx in range(2):
            pair = []
            for bz in range(2):
                place = bx + 2 * by + 4 * bz
                slot = slot_ref[place]
                block = feat_ref[slot].astype(F32)
                block = jnp.where(occ_ref[pl.ds(slot, 1), :] > 0, block, 0.0).T
                pair.append(block.reshape(64, 8, CIN))
            rows_ref[:, 0:CIN] = jnp.stack(pair, axis=1).reshape(1024, CIN)
            for pz in range(2):
                part = rows_ref[pl.ds(pz, 512, stride=2), :].reshape(8, 4, 2, 8, LANES)
                for py in range(2):
                    piece = part[:, :, py].reshape(8, 32, LANES).astype(BF16)
                    v_ref[pl.ds(8 * bx, 8), 2 * py + pz, pl.ds(32 * by, 32), :] = piece
            if by == 1:
                edge = [
                    rows_ref[pl.ds(pz, 512, stride=2), :].reshape(8, 8, 8, LANES)[:, 7]
                    for pz in range(2)
                ]
                ys_ref[pl.ds(128 * bx, 128), :] = (
                    jnp.stack(edge, axis=1).reshape(128, LANES).astype(BF16)
                )
    xs_ref[...] = v_ref[15].reshape(256, LANES)
    early = jnp.concatenate(
        [cot_ref[...].astype(BF16), jnp.zeros((16, 64), BF16), ys_ref[240:256, :]], axis=1
    )
    early_ref[...] = jnp.broadcast_to(early[None], early_ref.shape)


def forward_kernel(
    near_ref, w_hbm, v_ref, xr_ref, yr_ref, bias_ref, key_ref, val_ref, query_ref,
    routes_ref, early_ref,
    podd_ref, peven_ref, wp_ref, slope_ref, hid_ref, ku_ref, kn_ref, wt_ref, tt_ref, rr_ref,
    send_ref, slot_ref, routes8_ref, w_ref, sem,
):
    fetch = pltpu.make_async_copy(w_hbm, w_ref, sem)
    fetch.start()
    find_slots(near_ref, slot_ref)
    wp_ref[...] = jnp.zeros_like(wp_ref)
    here = lax.axis_index("chip") * 2 + lax.axis_index("core")
    inner = jnp.logical_and(here >= 8, lax.rem(here, 8) > 0)
    corner = early_ref[pl.ds(pl.multiple_of(16 * jnp.maximum(here - 9, 0), 16), 16), 256:384]
    corner = jnp.where(inner, corner.astype(F32), 0.0)
    first = lax.broadcasted_iota(jnp.int32, (64, LANES), 0) % 8 == 0
    for x in range(-1, 16):
        if x < 0:
            planes = xr_ref[...].astype(F32).reshape(4, 64, LANES)
            edge = corner
        else:
            planes = v_ref[x].astype(F32)
            edge = yr_ref[pl.ds(16 * x, 16), :].astype(F32)
        if x % 2 == 0:
            out_ref, row = peven_ref, 32 * x
        else:
            out_ref, row = podd_ref, 32 * (x + 1)
        for b in range(3):
            for c in range(3):
                py, pz = (b + 1) % 2, (c + 1) % 2
                piece = planes[2 * py + pz]
                if b == 0:
                    piece = jnp.concatenate([edge[8 * pz : 8 * pz + 8], piece[0:56]], axis=0)
                if c == 0:
                    piece = jnp.where(first, 0.0, pltpu.roll(piece, 1, 0))
                column = (3 * b + c) * LANES
                out_ref[pl.ds(row, 64), pl.ds(column, LANES)] = piece.astype(BF16)
    fetch.wait()
    for tap in range(27):
        wp_ref[:, pl.ds(tap * LANES, CIN)] = w_ref[:, pl.ds(tap * CIN, CIN)]
    before = (
        nt(podd_ref[0:512, :], wp_ref[:, 0:SLOTS9])
        + nt(peven_ref[...], wp_ref[:, SLOTS9 : 2 * SLOTS9])
        + nt(podd_ref[64:576, :], wp_ref[:, 2 * SLOTS9 : 3 * SLOTS9])
        + bias_ref[...]
    )
    root = 0.7978845608028654
    square = before * before
    tanh = jnp.tanh(root * before * (1.0 + 0.044715 * square))
    hidden = (0.5 * before * (1.0 + tanh)).astype(BF16)
    slope_ref[...] = 0.5 * (1.0 + tanh) + 0.5 * before * (1.0 - tanh * tanh) * root * (
        1.0 + 3.0 * 0.044715 * square
    )
    hid_ref[...] = hidden

    kh, kl = split(key_ref[...])
    vh, vl = split(val_ref[...])
    keys = nn(hidden, kh) + nn(hidden, kl)
    values = nn(hidden, vh) + nn(hidden, vl)
    key_norm = lax.rsqrt(jnp.sum(keys * keys, axis=-1, keepdims=True) + EPS)
    ku = keys * key_norm
    ku_ref[...] = ku
    kn_ref[...] = key_norm
    queries = query_ref[...]
    qu = queries * lax.rsqrt(jnp.sum(queries * queries, axis=-1, keepdims=True) + EPS)
    uh, ul = split(ku)
    qh, ql = split(qu)
    weights = jnp.exp(TEMPER * (nt(qh, uh) + nt(ql, uh) + nt(qh, ul)))
    wt_ref[...] = weights

    for slot in range(8):
        routes8_ref[slot : slot + 1, :] = routes_ref[:, 64 * slot : 64 * slot + 64]
    routes = jnp.concatenate(
        [routes8_ref[pl.ds(slot_ref[p], 1), :] for p in range(8)], axis=0
    ).astype(BF16)
    row = lax.broadcasted_iota(jnp.int32, (64, 512), 1)
    inside = ((row >> 6) & 3) * 16 + ((row >> 3) & 3) * 4 + (row & 3)
    pick = (inside == lax.broadcasted_iota(jnp.int32, (64, 512), 0)).astype(F32).astype(BF16)
    spread = nn(routes, pick)
    row = lax.broadcasted_iota(jnp.int32, (8, 512), 1)
    place = (row >> 8) + ((row >> 5) & 1) * 2 + ((row >> 2) & 1) * 4
    here = place == lax.broadcasted_iota(jnp.int32, (8, 512), 0)
    group = jnp.sum(jnp.where(here, spread, 0.0), axis=0, keepdims=True)
    group = jnp.broadcast_to(group, (8, 512))
    rr_ref[...] = group

    shares = jnp.concatenate(
        [jnp.where(group == float(g), weights, 0.0) for g in range(GROUPS)], axis=0
    ).astype(BF16)
    vb = values.astype(BF16)
    sums = nn(shares, jnp.concatenate([vb, jnp.ones((512, 64), BF16)], axis=1))
    cot = early_ref[:, 0:COUT]
    inner = jnp.sum(sums[:, 0:COUT] * cot.astype(F32), axis=-1, keepdims=True)
    lane = lax.broadcasted_iota(jnp.int32, (8, 64), 1)
    mass = jnp.zeros((8, 64), F32)
    dots = jnp.zeros((8, 64), F32)
    for g in range(GROUPS):
        mass = jnp.where(lane == g, sums[8 * g : 8 * g + 8, COUT:256], mass)
        dots = jnp.where(lane == g, inner[8 * g : 8 * g + 8], dots)
    table = jnp.concatenate([mass, dots], axis=0)
    send_ref[:, 0:COUT] = sums[:, 0:COUT].astype(BF16)
    send_ref[:, COUT:256] = jnp.concatenate([table.astype(BF16)] * 32, axis=0)

    meets = nt(cot, vb)
    total = jnp.zeros((8, 512), F32)
    for g in range(GROUPS):
        total = total + jnp.where(group == float(g), meets[8 * g : 8 * g + 8], 0.0)
    tt_ref[...] = total


def backward_kernel(
    recv_ref, podd_ref, peven_ref, slope_ref, hid_ref, ku_ref, kn_ref, wt_ref, tt_ref, rr_ref,
    early_ref, key_ref, val_ref, query_ref,
    pooled_ref, db_ref, xs_ref, ys_ref, keep_ref, give_ref, sum_ref,
):
    got = jnp.sum(recv_ref[...].reshape(32, 16, 256).astype(F32), axis=0)
    mass = got[0:8, COUT:256]
    dots = got[8:16, COUT:256]
    here = lax.axis_index("chip") * 2 + lax.axis_index("core")
    lane = lax.broadcasted_iota(jnp.int32, (8, 64), 1)
    own = [
        jnp.sum(jnp.where(lane == 2 * here + i, mass, 0.0), axis=-1, keepdims=True)
        for i in range(2)
    ]
    pooled_ref[...] = got[:, 0:COUT] / (1.0 + jnp.concatenate(own, axis=0))

    inverse = 1.0 / (1.0 + mass)
    d_mass = -dots * inverse * inverse
    ih, il = split(inverse)
    mh, ml = split(d_mass)
    group = rr_ref[...]
    member = (
        lax.broadcasted_iota(jnp.int32, (64, 512), 0).astype(F32)
        == jnp.broadcast_to(group[0:1], (64, 512))
    ).astype(F32).astype(BF16)
    inv_row = nn(ih, member) + nn(il, member)
    dm_row = nn(mh, member) + nn(ml, member)
    weights = wt_ref[...]
    d_cos = TEMPER * weights * (tt_ref[...] * inv_row + dm_row)
    scaled = weights * inv_row
    shares = jnp.concatenate(
        [jnp.where(group == float(g), scaled, 0.0) for g in range(GROUPS)], axis=0
    ).astype(BF16)
    d_value = tn(shares, early_ref[:, 0:COUT]).astype(BF16)

    queries = query_ref[...]
    qn = lax.rsqrt(jnp.sum(queries * queries, axis=-1, keepdims=True) + EPS)
    qu = queries * qn
    ku = ku_ref[...]
    dc = d_cos.astype(BF16)
    d_ku = tn(dc, qu.astype(BF16))
    d_key = kn_ref[...] * (d_ku - ku * jnp.sum(ku * d_ku, axis=-1, keepdims=True))
    d_key = d_key.astype(BF16)
    d_qu = nn(dc, ku.astype(BF16))
    d_query = qn * (d_qu - qu * jnp.sum(qu * d_qu, axis=-1, keepdims=True))

    d_hidden = nt(d_key, key_ref[...].astype(BF16)) + nt(d_value, val_ref[...].astype(BF16))
    d_before = d_hidden * slope_ref[...]
    db = d_before.astype(BF16)
    db_ref[...] = db
    xs_ref[...] = db[0:64]
    ys_ref[...] = d_before.reshape(8, 64, COUT)[:, 0:8].reshape(64, COUT).astype(BF16)

    hid = hid_ref[...]
    parts = (podd_ref[0:512, :], peven_ref[...], podd_ref[64:576, :])
    for a in range(3):
        grad = tn(db, parts[a])
        for tap in range(9):
            piece = grad[:, tap * LANES : tap * LANES + CIN]
            sum_ref[:, pl.ds((9 * a + tap) * CIN, CIN)] = piece
    sum_ref[:, KDIM : KDIM + COUT] = tn(hid, d_key)
    sum_ref[:, KDIM + COUT : KDIM + 2 * COUT] = tn(hid, d_value)
    bias = jnp.broadcast_to(jnp.sum(d_before, axis=0, keepdims=True), (8, COUT))
    small = [d_query[:, 0:CIN], d_query[:, CIN:COUT], bias[:, 0:CIN], bias[:, CIN:COUT]]
    small = jnp.concatenate(small + [jnp.zeros((COUT - 32, CIN), F32)], axis=0)
    sum_ref[:, KDIM + 2 * COUT : WIDE] = small
    low = lax.axis_index("core") == 0
    for t in range(12):
        left = sum_ref[:, LANES * t : LANES * (t + 1)]
        right = sum_ref[:, LANES * (t + 12) : LANES * (t + 13)]
        keep_ref[COUT * t : COUT * (t + 1), :] = jnp.where(low, left, right)
        give_ref[COUT * t : COUT * (t + 1), :] = jnp.where(low, right, left).astype(BF16)
    rest = HALF - 12 * COUT
    keep_ref[12 * COUT : HALF, :] = jnp.zeros((rest, LANES), F32)
    give_ref[12 * COUT : HALF, :] = jnp.zeros((rest, LANES), BF16)


def add_kernel(a_ref, b_ref, out_ref):
    out_ref[...] = (a_ref[...] + b_ref[...].astype(F32)).astype(BF16)


def total_kernel(recv_ref, out_ref):
    total = jnp.sum(recv_ref[...].astype(F32), axis=0).astype(BF16)
    out_ref[...] = jnp.broadcast_to(total[None], out_ref.shape)


def final_kernel(mine_ref, other_ref, dw_ref, dk_ref, dv_ref, dq_ref, dbias_ref, all_ref):
    low = lax.axis_index("core") == 0
    for t in range(12):
        mine = mine_ref[COUT * t : COUT * (t + 1), :].astype(F32)
        other = other_ref[COUT * t : COUT * (t + 1), :].astype(F32)
        all_ref[:, LANES * t : LANES * (t + 1)] = jnp.where(low, mine, other)
        all_ref[:, LANES * (t + 12) : LANES * (t + 13)] = jnp.where(low, other, mine)
    dw_ref[...] = all_ref[:, 0:KDIM]
    dk_ref[...] = all_ref[:, KDIM : KDIM + COUT]
    dv_ref[...] = all_ref[:, KDIM + COUT : KDIM + 2 * COUT]
    small = all_ref[0:32, KDIM + 2 * COUT : WIDE]
    dq_ref[...] = jnp.concatenate([small[0:8], small[8:16]], axis=1)
    dbias_ref[...] = jnp.concatenate([small[16:17], small[24:25]], axis=1)


def spread_kernel(
    near_ref, db_ref, xr_ref, yr_ref, xyr_ref, wp_ref, occ_ref, out_ref,
    ext_ref, even_ref, odd_ref, rows_ref, slot_ref,
):
    find_slots(near_ref, slot_ref)
    edge = yr_ref[...].astype(F32)
    for jx in range(8):
        ext_ref[pl.ds(72 * jx, 64), :] = db_ref[pl.ds(64 * jx, 64), :].astype(F32)
        ext_ref[pl.ds(72 * jx + 64, 8), :] = edge[8 * jx : 8 * jx + 8]
    ext_ref[pl.ds(576, 64), :] = xr_ref[...].astype(F32)
    ext_ref[pl.ds(640, 8), :] = xyr_ref[...].astype(F32)[0:8]
    low = ext_ref[0:576, :].astype(BF16)
    high = ext_ref[72:648, :].astype(BF16)
    even_ref[...] = nn(low, wp_ref[:, SLOTS9 : 2 * SLOTS9])
    odd_ref[...] = nn(low, wp_ref[:, 2 * SLOTS9 : 3 * SLOTS9]) + nn(high, wp_ref[:, 0:SLOTS9])
    last = lax.broadcasted_iota(jnp.int32, (32, LANES), 0) % 8 == 7

    def up(piece):
        return jnp.where(last, 0.0, pltpu.roll(piece, 31, 0))

    for by in range(2):
        for bx in range(2):
            for xl in range(8):
                x = 8 * bx + xl
                src_ref = even_ref if x % 2 == 0 else odd_ref
                start = 72 * (x // 2) + 32 * by

                def tap(b, c, later, src_ref=src_ref, start=start):
                    return src_ref[pl.ds(start + 8 * later, 32), pl.ds((3 * b + c) * LANES, LANES)]

                e00 = tap(1, 1, 0)
                e01 = tap(1, 2, 0) + up(tap(1, 0, 0))
                e10 = tap(2, 1, 0) + tap(0, 1, 1)
                e11 = tap(2, 2, 0) + tap(0, 2, 1) + up(tap(2, 0, 0) + tap(0, 0, 1))
                for pz, (ye, yo) in enumerate(((e00, e10), (e01, e11))):
                    both = jnp.stack([ye.reshape(4, 8, LANES), yo.reshape(4, 8, LANES)], axis=1)
                    rows_ref[pl.ds(128 * xl + pz, 64, stride=2), :] = both.reshape(64, LANES)
            tile = rows_ref[...].reshape(64, 2, 8, LANES)
            for bz in range(2):
                place = bx + 2 * by + 4 * bz
                slot = slot_ref[place]
                block = tile[:, bz].reshape(512, LANES).T[0:CIN]
                block = jnp.where(occ_ref[pl.ds(slot, 1), :] > 0, block, 0.0)
                out_ref[slot] = block.astype(BF16)


def vm():
    return pl.BlockSpec(memory_space=pltpu.VMEM)


def like(shape, dtype=F32):
    return jax.ShapeDtypeStruct(shape, dtype)


def call(kernel, kinds, outs, scratch, *args):
    spaces = {"s": pltpu.SMEM, "h": pltpu.HBM, "v": pltpu.VMEM}
    kinds = kinds + "v" * (len(args) - len(kinds))
    in_specs = [pl.BlockSpec(memory_space=spaces[kind]) for kind in kinds]
    args = [
        pltpu.with_memory_space_constraint(arg, pltpu.HBM) if kind == "h" else arg
        for arg, kind in zip(args, kinds, strict=True)
    ]
    return pl.pallas_call(
        kernel,
        out_shape=outs,
        in_specs=in_specs,
        out_specs=jax.tree.map(lambda _: vm(), outs),
        scratch_shapes=scratch,
        compiler_params=params(),
        name=kernel.__name__,
    )(*args)


def shift(shard, by_x, by_y):
    pairs = []
    for index in range(32):
        tx, ty = index % 8 + by_x, index // 8 + by_y
        if 0 <= tx < 8 and 0 <= ty < 4:
            pairs.append((index, ty * 8 + tx))
    return lax.ppermute(shard, SPACE, pairs)


def on_device(
    features, occupancy, neighbors, routes, cotangent, conv_weight, conv_bias,
    key_weight, value_weight, queries,
):
    features, occupancy = jnp.swapaxes(features[0], 1, 2), occupancy[0]
    slots = pltpu.SMEM((8,), jnp.int32)
    v, xs, ys, early = call(
        place_kernel, "hhhh",
        [
            like((16, 4, 64, LANES), BF16), like((256, LANES), BF16), like((256, LANES), BF16),
            like((32, 16, 3 * LANES), BF16),
        ],
        [
            pltpu.SMEM((6, 8), jnp.int32), pltpu.VMEM((8, CIN, 512), BF16),
            pltpu.VMEM((8, 512), jnp.int32), pltpu.VMEM((16, COUT), F32),
            pltpu.VMEM((1024, LANES), F32), slots, pltpu.SemaphoreType.DMA((4,)),
        ],
        neighbors, features, occupancy, cotangent.reshape(16, COUT),
    )
    early = lax.all_to_all(early, SPACE, 0, 0, tiled=True).reshape(512, 3 * LANES)
    xr = shift(xs, 1, 0)
    yr = shift(ys, 0, 1)
    podd, peven, wp, slope, hid, ku, kn, wt, tt, rr, send = call(
        forward_kernel, "sh",
        [
            like((576, SLOTS9), BF16), like((512, SLOTS9), BF16), like((COUT, 27 * LANES), BF16),
            like((512, COUT)), like((512, COUT), BF16), like((512, COUT)), like((512, 1)),
            like((8, 512)), like((8, 512)), like((8, 512)), like((512, 256), BF16),
        ],
        [
            slots, pltpu.VMEM((8, 64), jnp.int32), pltpu.VMEM((COUT, KDIM), BF16),
            pltpu.SemaphoreType.DMA,
        ],
        neighbors, conv_weight.T, v, xr, yr, conv_bias.reshape(1, COUT), key_weight,
        value_weight, queries, routes.reshape(1, 512), early,
    )
    recv = lax.all_to_all(send.reshape(32, 16, 256), SPACE, 0, 0, tiled=True).reshape(512, 256)
    pooled, db, bxs, bys, keep, give = call(
        backward_kernel, "",
        [
            like((16, COUT)), like((512, COUT), BF16), like((64, COUT), BF16),
            like((64, COUT), BF16), like((HALF, LANES)), like((HALF, LANES), BF16),
        ],
        [pltpu.VMEM((COUT, WIDE), F32)],
        recv, podd, peven, slope, hid, ku, kn, wt, tt, rr, early, key_weight, value_weight,
        queries,
    )
    swap = [(0, 1), (1, 0)]
    taken = lax.ppermute(give, "core", swap)
    half = call(add_kernel, "", like((HALF, LANES), BF16), [], keep, taken)
    pieces = lax.all_to_all(half.reshape(64, SHARD, LANES), CHIPS, 0, 0, tiled=True)
    bxr = shift(bxs, -1, 0)
    byr = shift(bys, 0, -1)
    bxyr = shift(bys[0:16], -1, -1)
    copies = call(total_kernel, "", like((64, SHARD, LANES), BF16), [], pieces)
    bxr, byr, bxyr, copies = lax.optimization_barrier((bxr, byr, bxyr, copies))
    mine = lax.all_to_all(copies, CHIPS, 0, 0, tiled=True).reshape(HALF, LANES)
    d_features = call(
        spread_kernel, "s", like((8, CIN, 512), BF16),
        [
            pltpu.VMEM((648, COUT), F32), pltpu.VMEM((576, SLOTS9), F32),
            pltpu.VMEM((576, SLOTS9), F32), pltpu.VMEM((1024, LANES), F32), slots,
        ],
        neighbors, db, bxr, byr, bxyr, wp, occupancy,
    )
    mine, d_features = lax.optimization_barrier((mine, d_features))
    other = lax.ppermute(mine, "core", swap)
    d_weight, d_key, d_value, d_query, d_bias = call(
        final_kernel, "",
        [
            like((COUT, KDIM)), like((COUT, COUT)), like((COUT, COUT)), like((NQ, COUT)),
            like((1, COUT)),
        ],
        [pltpu.VMEM((COUT, WIDE), F32)],
        mine, other,
    )
    return (
        pooled.reshape(1, 2, NQ, COUT), jnp.swapaxes(d_features, 1, 2)[None], d_weight.T,
        d_bias.reshape(COUT), d_key, d_value, d_query,
    )


def solution(mesh):
    fine = Mesh(mesh.devices.reshape(4, 16, 2), ("section", "chip", "core"))
    in_specs = (
        P("section", SPACE, None, None),
        P("section", SPACE, None),
        P(None, SPACE),
        P("section", SPACE, None),
        P("section", SPACE, None, None),
        P(),
        P(),
        P(),
        P(),
        P(),
    )
    out_specs = (
        P("section", SPACE, None, None),
        P("section", SPACE, None, None),
        P(),
        P(),
        P(),
        P(),
        P(),
    )
    return jax.shard_map(
        on_device, mesh=fine, in_specs=in_specs, out_specs=out_specs, check_vma=False
    )
```

```python
import functools

import jax
import jax.numpy as jnp
from jax import lax
from jax.experimental import pallas as pl
from jax.experimental.pallas import tpu as pltpu
from jax.sharding import Mesh, PartitionSpec as P

EPS = 1e-06
TEMPER = 8.0
CIN, COUT = 96, 192
LANES = 128
SLOTS9 = 9 * LANES
GROUPS, NQ = 64, 8
KDIM = 27 * CIN
SHARD = 40
HALF = 64 * SHARD
WIDE = 24 * LANES
F32, BF16 = jnp.float32, jnp.bfloat16
SPACE = ("chip", "core")
CHIPS = ("section", "chip")
ROOT, CUBIC = 0.7978845608028654, 0.044715
VMEM_LIMIT = 44 * 1024 * 1024


def params():
    return pltpu.CompilerParams(vmem_limit_bytes=VMEM_LIMIT)


def nn(a, b):
    return lax.dot_general(a, b, (((1,), (0,)), ((), ())), preferred_element_type=F32)


def nt(a, b):
    return lax.dot_general(a, b, (((1,), (1,)), ((), ())), preferred_element_type=F32)


def tn(a, b):
    return lax.dot_general(a, b, (((0,), (0,)), ((), ())), preferred_element_type=F32)


def split(a):
    high = a.astype(BF16)
    return high, (a - high.astype(F32)).astype(BF16)


def find_slots(near_ref, slot_ref):
    here = lax.axis_index("chip") * 2 + lax.axis_index("core")
    for place in range(8):
        slot_ref[place] = 0
    for slot in range(8):
        place = 0
        for axis in range(3):
            beside = near_ref[axis, slot]
            inner = jnp.logical_and(beside >= 0, lax.shift_right_arithmetic(beside, 3) == here)
            place = place + jnp.where(inner, 0, 1 << axis)
        slot_ref[place] = slot


def place_kernel(
    near_hbm, feat_hbm, occ_hbm, cot_hbm, v_ref, xs_ref, ys_ref, early_ref,
    near_ref, feat_ref, occ_ref, cot_ref, rows_ref, slot_ref, sems,
):
    copies = [
        pltpu.make_async_copy(source, target, sems.at[i])
        for i, (source, target) in enumerate(
            (
                (near_hbm, near_ref), (feat_hbm, feat_ref), (occ_hbm, occ_ref), (cot_hbm, cot_ref),
            )
        )
    ]
    for copy in copies:
        copy.start()
    rows_ref[...] = jnp.zeros_like(rows_ref)
    for copy in copies:
        copy.wait()
    find_slots(near_ref, slot_ref)
    for by in range(2):
        for bx in range(2):
            pair = []
            for bz in range(2):
                place = bx + 2 * by + 4 * bz
                slot = slot_ref[place]
                block = feat_ref[slot].astype(F32)
                block = jnp.where(occ_ref[pl.ds(slot, 1), :] > 0, block, 0.0).T
                pair.append(block.reshape(64, 8, CIN))
            rows_ref[:, 0:CIN] = jnp.stack(pair, axis=1).reshape(1024, CIN)
            for pz in range(2):
                part = rows_ref[pl.ds(pz, 512, stride=2), :].reshape(8, 4, 2, 8, LANES)
                for py in range(2):
                    piece = part[:, :, py].reshape(8, 32, LANES).astype(BF16)
                    v_ref[pl.ds(8 * bx, 8), 2 * py + pz, pl.ds(32 * by, 32), :] = piece
            if by == 1:
                edge = [
                    rows_ref[pl.ds(pz, 512, stride=2), :].reshape(8, 8, 8, LANES)[:, 7]
                    for pz in range(2)
                ]
                ys_ref[pl.ds(128 * bx, 128), :] = (
                    jnp.stack(edge, axis=1).reshape(128, LANES).astype(BF16)
                )
    xs_ref[...] = v_ref[15].reshape(256, LANES)
    early = jnp.concatenate(
        [cot_ref[...].astype(BF16), jnp.zeros((16, 64), BF16), ys_ref[240:256, :]], axis=1
    )
    early_ref[...] = jnp.broadcast_to(early[None], early_ref.shape)


def prepare_kernel(
    near_ref, w_hbm, routes_ref,
    wp_ref, group_ref,
    slot_ref, routes8_ref, w_ref, sem,
):
    fetch = pltpu.make_async_copy(w_hbm, w_ref, sem)
    fetch.start()
    find_slots(near_ref, slot_ref)
    wp_ref[...] = jnp.zeros_like(wp_ref)
    for slot in range(8):
        routes8_ref[slot : slot + 1, :] = routes_ref[:, 64 * slot : 64 * slot + 64]
    routes = jnp.concatenate(
        [routes8_ref[pl.ds(slot_ref[p], 1), :] for p in range(8)], axis=0
    ).astype(BF16)
    row = lax.broadcasted_iota(jnp.int32, (64, 512), 1)
    inside = ((row >> 6) & 3) * 16 + ((row >> 3) & 3) * 4 + (row & 3)
    pick = (inside == lax.broadcasted_iota(jnp.int32, (64, 512), 0)).astype(F32).astype(BF16)
    spread = nn(routes, pick)
    row = lax.broadcasted_iota(jnp.int32, (8, 512), 1)
    place = (row >> 8) + ((row >> 5) & 1) * 2 + ((row >> 2) & 1) * 4
    mine = place == lax.broadcasted_iota(jnp.int32, (8, 512), 0)
    group = jnp.sum(jnp.where(mine, spread, 0.0), axis=0, keepdims=True)
    group_ref[...] = jnp.broadcast_to(group, (8, 512))

    fetch.wait()
    for tap in range(27):
        wp_ref[:, pl.ds(tap * LANES, CIN)] = w_ref[:, pl.ds(tap * CIN, CIN)]


def shared_out(group, amounts):
    return jnp.concatenate(
        [jnp.where(group == float(g), amounts, 0.0) for g in range(GROUPS)], axis=0
    ).astype(BF16)


def forward_kernel(
    key_hbm, val_hbm, query_hbm, v_ref, xr_ref, yr_ref, bias_ref, wp_ref, group_ref, early_ref,
    podd_ref, peven_ref, slope_ref, hidt_ref, cott_ref, kut_ref, knt_ref, wt_ref, tt_ref, kt_ref,
    vw_ref, send_ref,
    key_ref, val_ref, query_ref, sems,
):
    copies = [
        pltpu.make_async_copy(source, target, sems.at[i])
        for i, (source, target) in enumerate(
            ((key_hbm, key_ref), (val_hbm, val_ref), (query_hbm, query_ref))
        )
    ]
    for copy in copies:
        copy.start()
    here = lax.axis_index("chip") * 2 + lax.axis_index("core")
    inner = jnp.logical_and(here >= 8, lax.rem(here, 8) > 0)
    corner = early_ref[pl.ds(pl.multiple_of(16 * jnp.maximum(here - 9, 0), 16), 16), 256:384]
    corner = jnp.where(inner, corner.astype(F32), 0.0)
    first = lax.broadcasted_iota(jnp.int32, (64, LANES), 0) % 8 == 0
    for x in range(-1, 16):
        if x < 0:
            planes, edge = xr_ref[...].astype(F32).reshape(4, 64, LANES), corner
        else:
            planes, edge = v_ref[x].astype(F32), yr_ref[pl.ds(16 * x, 16), :].astype(F32)
        if x % 2 == 0:
            out_ref, row = peven_ref, 32 * x
        else:
            out_ref, row = podd_ref, 32 * (x + 1)
        for b in range(3):
            for c in range(3):
                py, pz = (b + 1) % 2, (c + 1) % 2
                piece = planes[2 * py + pz]
                if b == 0:
                    piece = jnp.concatenate([edge[8 * pz : 8 * pz + 8], piece[0:56]], axis=0)
                if c == 0:
                    piece = jnp.where(first, 0.0, pltpu.roll(piece, 1, 0))
                column = (3 * b + c) * LANES
                out_ref[pl.ds(row, 64), pl.ds(column, LANES)] = piece.astype(BF16)
    before = (
        nt(podd_ref[0:512, :], wp_ref[:, 0:SLOTS9])
        + nt(peven_ref[...], wp_ref[:, SLOTS9 : 2 * SLOTS9])
        + nt(podd_ref[64:576, :], wp_ref[:, 2 * SLOTS9 : 3 * SLOTS9])
        + bias_ref[...]
    )
    square = before * before
    tanh = jnp.tanh(ROOT * before * (1.0 + CUBIC * square))
    hidden = (0.5 * before * (1.0 + tanh)).astype(BF16)
    slope = 0.5 * (1.0 + tanh) + 0.5 * before * (1.0 - tanh * tanh) * ROOT * (
        1.0 + 3.0 * CUBIC * square
    )
    slope_ref[...] = slope.T
    hidt_ref[...] = hidden.astype(F32).T.astype(BF16)

    for copy in copies:
        copy.wait()
    kh, kl = split(key_ref[...].T)
    vh, vl = split(val_ref[...])
    kt_ref[0:COUT, :] = kh
    kt_ref[COUT : 2 * COUT, :] = kl
    vw_ref[0:COUT, :] = vh
    vw_ref[COUT : 2 * COUT, :] = vl
    keys = nt(kh, hidden) + nt(kl, hidden)
    values = nn(hidden, vh) + nn(hidden, vl)
    queries = query_ref[...]
    qu = queries * lax.rsqrt(jnp.sum(queries * queries, axis=-1, keepdims=True) + EPS)
    key_norm = lax.rsqrt(jnp.sum(keys * keys, axis=0, keepdims=True) + EPS)
    kut = keys * key_norm
    kut_ref[...] = kut
    knt_ref[...] = jnp.broadcast_to(key_norm, (8, 512))
    uh, ul = split(kut)
    qh, ql = split(qu)
    weights = jnp.exp(TEMPER * (nn(qh, uh) + nn(ql, uh) + nn(qh, ul)))
    wt_ref[...] = weights
    group = group_ref[...]
    shares = shared_out(group, weights)
    vb = values.astype(BF16)
    sums = nn(shares, jnp.concatenate([vb, jnp.ones((512, 64), BF16)], axis=1))
    cot = early_ref[:, 0:COUT]
    cott_ref[...] = cot.astype(F32).T.astype(BF16)
    meets = nt(cot, vb)
    total = jnp.zeros((8, 512), F32)
    for g in range(GROUPS):
        total = total + jnp.where(group == float(g), meets[8 * g : 8 * g + 8], 0.0)
    tt_ref[...] = total
    inner = jnp.sum(sums[:, 0:COUT] * cot.astype(F32), axis=-1, keepdims=True)
    lane = lax.broadcasted_iota(jnp.int32, (8, 64), 1)
    mass = jnp.zeros((8, 64), F32)
    dots = jnp.zeros((8, 64), F32)
    for g in range(GROUPS):
        mass = jnp.where(lane == g, sums[8 * g : 8 * g + 8, COUT:256], mass)
        dots = jnp.where(lane == g, inner[8 * g : 8 * g + 8], dots)
    table = jnp.concatenate([mass, dots], axis=0)
    send_ref[:, 0:COUT] = sums[:, 0:COUT].astype(BF16)
    send_ref[:, COUT:256] = jnp.concatenate([table.astype(BF16)] * 32, axis=0)


def backward_kernel(
    recv_ref, podd_ref, peven_ref, slope_ref, hidt_ref, kut_ref, knt_ref, wt_ref, tt_ref,
    group_ref, cott_ref, kt_ref, vw_ref, query_ref,
    pooled_ref, db_ref, xs_ref, ys_ref, keep_ref, give_ref, sum_ref,
):
    got = jnp.sum(recv_ref[...].reshape(32, 16, 256).astype(F32), axis=0)
    mass = got[0:8, COUT:256]
    dots = got[8:16, COUT:256]
    here = lax.axis_index("chip") * 2 + lax.axis_index("core")
    lane = lax.broadcasted_iota(jnp.int32, (8, 64), 1)
    own = [
        jnp.sum(jnp.where(lane == 2 * here + i, mass, 0.0), axis=-1, keepdims=True)
        for i in range(2)
    ]
    pooled_ref[...] = got[:, 0:COUT] / (1.0 + jnp.concatenate(own, axis=0))

    inverse = 1.0 / (1.0 + mass)
    d_mass = -dots * inverse * inverse
    ih, il = split(inverse)
    mh, ml = split(d_mass)
    group = group_ref[...]
    rows = lax.broadcasted_iota(jnp.int32, (64, 512), 0).astype(F32)
    member = (rows == jnp.broadcast_to(group[0:1], (64, 512))).astype(F32).astype(BF16)
    inv_row = nn(ih, member) + nn(il, member)
    dm_row = nn(mh, member) + nn(ml, member)
    weights = wt_ref[...]
    d_cos = TEMPER * weights * (tt_ref[...] * inv_row + dm_row)
    d_value = nn(cott_ref[...], shared_out(group, weights * inv_row))

    kut = kut_ref[...]
    queries = query_ref[...]
    qn = lax.rsqrt(jnp.sum(queries * queries, axis=-1, keepdims=True) + EPS)
    qu = queries * qn
    ch, cl = split(d_cos)
    qh, ql = split(qu.T)
    d_ku = nn(qh, ch) + nn(ql, ch) + nn(qh, cl)
    d_key = knt_ref[0:1, :] * (d_ku - kut * jnp.sum(kut * d_ku, axis=0, keepdims=True))
    d_qu = nt(ch, kut.astype(BF16))
    d_query = qn * (d_qu - qu * jnp.sum(qu * d_qu, axis=-1, keepdims=True))

    kh, kl = split(d_key)
    vh, vl = split(d_value)
    d_hidden = tn(kt_ref[0:COUT, :], kh) + tn(kt_ref[COUT : 2 * COUT, :], kh)
    d_hidden = d_hidden + tn(kt_ref[0:COUT, :], kl) + nn(vw_ref[0:COUT, :], vl)
    d_hidden = d_hidden + nn(vw_ref[0:COUT, :], vh) + nn(vw_ref[COUT : 2 * COUT, :], vh)
    d_before = d_hidden * slope_ref[...]
    dbt = d_before.astype(BF16)
    d_rows = d_before.T
    db = d_rows.astype(BF16)
    db_ref[...] = db
    xs_ref[...] = db[0:64]
    ys_ref[...] = d_rows.reshape(8, 64, COUT)[:, 0:8].reshape(64, COUT).astype(BF16)

    parts = (podd_ref[0:512, :], peven_ref[...], podd_ref[64:576, :])
    for a in range(3):
        grad = nn(dbt, parts[a])
        for tap in range(9):
            piece = grad[:, tap * LANES : tap * LANES + CIN]
            sum_ref[:, pl.ds((9 * a + tap) * CIN, CIN)] = piece
    sum_ref[:, KDIM : KDIM + COUT] = nt(hidt_ref[...], kh)
    sum_ref[:, KDIM + COUT : KDIM + 2 * COUT] = nt(hidt_ref[...], vh)
    bias = jnp.broadcast_to(jnp.sum(d_rows, axis=0, keepdims=True), (8, COUT))
    small = [d_query[:, 0:CIN], d_query[:, CIN:COUT], bias[:, 0:CIN], bias[:, CIN:COUT]]
    small = jnp.concatenate(small + [jnp.zeros((COUT - 32, CIN), F32)], axis=0)
    sum_ref[:, KDIM + 2 * COUT : WIDE] = small
    low = lax.axis_index("core") == 0
    for t in range(12):
        left = sum_ref[:, LANES * t : LANES * (t + 1)]
        right = sum_ref[:, LANES * (t + 12) : LANES * (t + 13)]
        keep_ref[COUT * t : COUT * (t + 1), :] = jnp.where(low, left, right)
        give_ref[COUT * t : COUT * (t + 1), :] = jnp.where(low, right, left).astype(BF16)
    rest = HALF - 12 * COUT
    keep_ref[12 * COUT : HALF, :] = jnp.zeros((rest, LANES), F32)
    give_ref[12 * COUT : HALF, :] = jnp.zeros((rest, LANES), BF16)


def add_kernel(a_ref, b_ref, out_ref):
    out_ref[...] = (a_ref[...] + b_ref[...].astype(F32)).astype(BF16)


def total_kernel(recv_ref, out_ref):
    total = jnp.sum(recv_ref[...].astype(F32), axis=0).astype(BF16)
    out_ref[...] = jnp.broadcast_to(total[None], out_ref.shape)


def final_kernel(mine_ref, other_ref, dw_ref, dk_ref, dv_ref, dq_ref, dbias_ref, all_ref):
    low = lax.axis_index("core") == 0
    for t in range(12):
        mine = mine_ref[COUT * t : COUT * (t + 1), :].astype(F32)
        other = other_ref[COUT * t : COUT * (t + 1), :].astype(F32)
        all_ref[:, LANES * t : LANES * (t + 1)] = jnp.where(low, mine, other)
        all_ref[:, LANES * (t + 12) : LANES * (t + 13)] = jnp.where(low, other, mine)
    dw_ref[...] = all_ref[:, 0:KDIM]
    dk_ref[...] = all_ref[:, KDIM : KDIM + COUT]
    dv_ref[...] = all_ref[:, KDIM + COUT : KDIM + 2 * COUT]
    small = all_ref[0:32, KDIM + 2 * COUT : WIDE]
    dq_ref[...] = jnp.concatenate([small[0:8], small[8:16]], axis=1)
    dbias_ref[...] = jnp.concatenate([small[16:17], small[24:25]], axis=1)


def spread_kernel(
    near_ref, w_hbm, db_ref, xr_ref, yr_ref, xyr_ref, occ_ref, out_ref,
    ext_ref, even_ref, odd_ref, rows_ref, slot_ref, w_ref, wp_ref, sem,
):
    fetch = pltpu.make_async_copy(w_hbm, w_ref, sem)
    fetch.start()
    wp_ref[...] = jnp.zeros_like(wp_ref)
    find_slots(near_ref, slot_ref)
    edge = yr_ref[...].astype(F32)
    for jx in range(8):
        ext_ref[pl.ds(72 * jx, 64), :] = db_ref[pl.ds(64 * jx, 64), :].astype(F32)
        ext_ref[pl.ds(72 * jx + 64, 8), :] = edge[8 * jx : 8 * jx + 8]
    ext_ref[pl.ds(576, 64), :] = xr_ref[...].astype(F32)
    ext_ref[pl.ds(640, 8), :] = xyr_ref[...].astype(F32)[0:8]
    low = ext_ref[0:576, :].astype(BF16)
    high = ext_ref[72:648, :].astype(BF16)
    fetch.wait()
    for number in range(27):
        wp_ref[:, pl.ds(number * LANES, CIN)] = w_ref[:, pl.ds(number * CIN, CIN)]
    even_ref[...] = nn(low, wp_ref[:, SLOTS9 : 2 * SLOTS9])
    odd_ref[...] = nn(low, wp_ref[:, 2 * SLOTS9 : 3 * SLOTS9]) + nn(high, wp_ref[:, 0:SLOTS9])
    last = lax.broadcasted_iota(jnp.int32, (32, LANES), 0) % 8 == 7

    def up(piece):
        return jnp.where(last, 0.0, pltpu.roll(piece, 31, 0))

    for by in range(2):
        for bx in range(2):
            for xl in range(8):
                x = 8 * bx + xl
                src_ref = even_ref if x % 2 == 0 else odd_ref
                start = 72 * (x // 2) + 32 * by

                def tap(b, c, later, src_ref=src_ref, start=start):
                    return src_ref[pl.ds(start + 8 * later, 32), pl.ds((3 * b + c) * LANES, LANES)]

                e00 = tap(1, 1, 0)
                e01 = tap(1, 2, 0) + up(tap(1, 0, 0))
                e10 = tap(2, 1, 0) + tap(0, 1, 1)
                e11 = tap(2, 2, 0) + tap(0, 2, 1) + up(tap(2, 0, 0) + tap(0, 0, 1))
                for pz, (ye, yo) in enumerate(((e00, e10), (e01, e11))):
                    both = jnp.stack([ye.reshape(4, 8, LANES), yo.reshape(4, 8, LANES)], axis=1)
                    rows_ref[pl.ds(128 * xl + pz, 64, stride=2), :] = both.reshape(64, LANES)
            tile = rows_ref[...].reshape(64, 2, 8, LANES)
            for bz in range(2):
                place = bx + 2 * by + 4 * bz
                slot = slot_ref[place]
                block = tile[:, bz].reshape(512, LANES).T[0:CIN]
                block = jnp.where(occ_ref[pl.ds(slot, 1), :] > 0, block, 0.0)
                out_ref[slot] = block.astype(BF16)


def vm():
    return pl.BlockSpec(memory_space=pltpu.VMEM)


def like(shape, dtype=F32):
    return jax.ShapeDtypeStruct(shape, dtype)


def call(kernel, kinds, outs, scratch, *args):
    spaces = {"s": pltpu.SMEM, "h": pltpu.HBM, "v": pltpu.VMEM}
    kinds = kinds + "v" * (len(args) - len(kinds))
    in_specs = [pl.BlockSpec(memory_space=spaces[kind]) for kind in kinds]
    args = [
        pltpu.with_memory_space_constraint(arg, pltpu.HBM) if kind == "h" else arg
        for arg, kind in zip(args, kinds, strict=True)
    ]
    return pl.pallas_call(
        kernel,
        out_shape=outs,
        in_specs=in_specs,
        out_specs=jax.tree.map(lambda _: vm(), outs),
        scratch_shapes=scratch,
        compiler_params=params(),
        name=kernel.__name__,
    )(*args)


def shift(shard, by_x, by_y):
    pairs = []
    for index in range(32):
        tx, ty = index % 8 + by_x, index // 8 + by_y
        if 0 <= tx < 8 and 0 <= ty < 4:
            pairs.append((index, ty * 8 + tx))
    return lax.ppermute(shard, SPACE, pairs)


def on_device(
    features, occupancy, neighbors, routes, cotangent, conv_weight, conv_bias,
    key_weight, value_weight, queries,
):
    features, occupancy = jnp.swapaxes(features[0], 1, 2), occupancy[0]
    slots = pltpu.SMEM((8,), jnp.int32)
    v, xs, ys, early = call(
        place_kernel, "hhhh",
        [
            like((16, 4, 64, LANES), BF16), like((256, LANES), BF16), like((256, LANES), BF16),
            like((32, 16, 3 * LANES), BF16),
        ],
        [
            pltpu.SMEM((6, 8), jnp.int32), pltpu.VMEM((8, CIN, 512), BF16),
            pltpu.VMEM((8, 512), jnp.int32), pltpu.VMEM((16, COUT), F32),
            pltpu.VMEM((1024, LANES), F32), slots, pltpu.SemaphoreType.DMA((4,)),
        ],
        neighbors, features, occupancy, cotangent.reshape(16, COUT),
    )
    early = lax.all_to_all(early, SPACE, 0, 0, tiled=True).reshape(512, 3 * LANES)
    xr = shift(xs, 1, 0)
    yr = shift(ys, 0, 1)
    wp, group = call(
        prepare_kernel, "sh",
        [
            like((COUT, 27 * LANES), BF16), like((8, 512)),
        ],
        [
            slots, pltpu.VMEM((8, 64), jnp.int32), pltpu.VMEM((COUT, KDIM), BF16),
            pltpu.SemaphoreType.DMA,
        ],
        neighbors, conv_weight.T, routes.reshape(1, 512),
    )
    podd, peven, slope, hidt, cott, kut, knt, wt, tt, kt, vw, send = call(
        forward_kernel, "hhh",
        [
            like((576, SLOTS9), BF16), like((512, SLOTS9), BF16), like((COUT, 512)),
            like((COUT, 512), BF16), like((COUT, 512), BF16), like((COUT, 512)), like((8, 512)),
            like((8, 512)), like((8, 512)), like((2 * COUT, COUT), BF16),
            like((2 * COUT, COUT), BF16), like((512, 256), BF16),
        ],
        [
            pltpu.VMEM((COUT, COUT), F32), pltpu.VMEM((COUT, COUT), F32),
            pltpu.VMEM((NQ, COUT), F32), pltpu.SemaphoreType.DMA((3,)),
        ],
        key_weight, value_weight, queries, v, xr, yr, conv_bias.reshape(1, COUT), wp, group, early,
    )
    recv = lax.all_to_all(send.reshape(32, 16, 256), SPACE, 0, 0, tiled=True).reshape(512, 256)
    pooled, db, bxs, bys, keep, give = call(
        backward_kernel, "",
        [
            like((16, COUT)), like((512, COUT), BF16), like((64, COUT), BF16),
            like((64, COUT), BF16), like((HALF, LANES)), like((HALF, LANES), BF16),
        ],
        [pltpu.VMEM((COUT, WIDE), F32)],
        recv, podd, peven, slope, hidt, kut, knt, wt, tt, group, cott, kt, vw, queries,
    )
    swap = [(0, 1), (1, 0)]
    taken = lax.ppermute(give, "core", swap)
    half = call(add_kernel, "", like((HALF, LANES), BF16), [], keep, taken)
    pieces = lax.all_to_all(half.reshape(64, SHARD, LANES), CHIPS, 0, 0, tiled=True)
    bxr = shift(bxs, -1, 0)
    byr = shift(bys, 0, -1)
    bxyr = shift(bys[0:16], -1, -1)
    copies = call(total_kernel, "", like((64, SHARD, LANES), BF16), [], pieces)
    bxr, byr, bxyr, copies = lax.optimization_barrier((bxr, byr, bxyr, copies))
    mine = lax.all_to_all(copies, CHIPS, 0, 0, tiled=True).reshape(HALF, LANES)
    d_features = call(
        spread_kernel, "sh", like((8, CIN, 512), BF16),
        [
            pltpu.VMEM((648, COUT), F32), pltpu.VMEM((576, SLOTS9), F32),
            pltpu.VMEM((576, SLOTS9), F32), pltpu.VMEM((1024, LANES), F32), slots,
            pltpu.VMEM((COUT, KDIM), BF16), pltpu.VMEM((COUT, 27 * LANES), BF16),
            pltpu.SemaphoreType.DMA,
        ],
        neighbors, conv_weight.T, db, bxr, byr, bxyr, occupancy,
    )
    mine, d_features = lax.optimization_barrier((mine, d_features))
    other = lax.ppermute(mine, "core", swap)
    d_weight, d_key, d_value, d_query, d_bias = call(
        final_kernel, "",
        [
            like((COUT, KDIM)), like((COUT, COUT)), like((COUT, COUT)), like((NQ, COUT)),
            like((1, COUT)),
        ],
        [pltpu.VMEM((COUT, WIDE), F32)],
        mine, other,
    )
    return (
        pooled.reshape(1, 2, NQ, COUT), jnp.swapaxes(d_features, 1, 2)[None], d_weight.T,
        d_bias.reshape(COUT), d_key, d_value, d_query,
    )


def solution(mesh):
    fine = Mesh(mesh.devices.reshape(4, 16, 2), ("section", "chip", "core"))
    in_specs = (
        P("section", SPACE, None, None),
        P("section", SPACE, None),
        P(None, SPACE),
        P("section", SPACE, None),
        P("section", SPACE, None, None),
        P(),
        P(),
        P(),
        P(),
        P(),
    )
    out_specs = (
        P("section", SPACE, None, None),
        P("section", SPACE, None, None),
        P(),
        P(),
        P(),
        P(),
        P(),
    )
    return jax.shard_map(
        on_device, mesh=fine, in_specs=in_specs, out_specs=out_specs, check_vma=False
    )
```

```python
import functools

import jax
import jax.numpy as jnp
from jax import lax
from jax.experimental import pallas as pl
from jax.experimental.pallas import tpu as pltpu
from jax.sharding import Mesh, PartitionSpec as P

EPS = 1e-06
TEMPER = 8.0
CIN, COUT = 96, 192
LANES = 128
SLOTS9 = 9 * LANES
GROUPS, NQ = 64, 8
KDIM = 27 * CIN
SHARD = 40
HALF = 64 * SHARD
USED = 12 * COUT
WIDE = 24 * LANES
F32, BF16 = jnp.float32, jnp.bfloat16
SPACE = ("chip", "core")
CHIPS = ("section", "chip")
ROOT, CUBIC = 0.7978845608028654, 0.044715
VMEM_LIMIT = 44 * 1024 * 1024


def params():
    return pltpu.CompilerParams(vmem_limit_bytes=VMEM_LIMIT)


def nn(a, b):
    return lax.dot_general(a, b, (((1,), (0,)), ((), ())), preferred_element_type=F32)


def nt(a, b):
    return lax.dot_general(a, b, (((1,), (1,)), ((), ())), preferred_element_type=F32)


def tn(a, b):
    return lax.dot_general(a, b, (((0,), (0,)), ((), ())), preferred_element_type=F32)


def split(a):
    high = a.astype(BF16)
    return high, (a - high.astype(F32)).astype(BF16)


def find_slots(near_ref, slot_ref):
    here = lax.axis_index("chip") * 2 + lax.axis_index("core")
    for place in range(8):
        slot_ref[place] = 0
    for slot in range(8):
        place = 0
        for axis in range(3):
            beside = near_ref[axis, slot]
            inner = jnp.logical_and(beside >= 0, lax.shift_right_arithmetic(beside, 3) == here)
            place = place + jnp.where(inner, 0, 1 << axis)
        slot_ref[place] = slot


def place_kernel(
    near_hbm, feat_hbm, occ_hbm, cot_hbm, v_ref, xs_ref, ys_ref, early_ref,
    near_ref, feat_ref, occ_ref, cot_ref, rows_ref, slot_ref, sems,
):
    pairs = [(near_hbm, near_ref), (occ_hbm, occ_ref), (cot_hbm, cot_ref)]
    pairs += [(feat_hbm.at[slot], feat_ref.at[slot]) for slot in range(8)]
    copies = [
        pltpu.make_async_copy(source, target, sems.at[i])
        for i, (source, target) in enumerate(pairs)
    ]
    for copy in copies:
        copy.start()
    rows_ref[...] = jnp.zeros_like(rows_ref)
    for copy in copies:
        copy.wait()
    find_slots(near_ref, slot_ref)
    for by in range(2):
        for bx in range(2):
            pair = []
            for bz in range(2):
                place = bx + 2 * by + 4 * bz
                slot = slot_ref[place]
                block = feat_ref[slot].astype(F32)
                block = jnp.where(occ_ref[pl.ds(slot, 1), :] > 0, block, 0.0).T
                pair.append(block.reshape(64, 8, CIN))
            rows_ref[:, 0:CIN] = jnp.stack(pair, axis=1).reshape(1024, CIN)
            for pz in range(2):
                part = rows_ref[pl.ds(pz, 512, stride=2), :].reshape(8, 4, 2, 8, LANES)
                for py in range(2):
                    piece = part[:, :, py].reshape(8, 32, LANES).astype(BF16)
                    v_ref[pl.ds(8 * bx, 8), 2 * py + pz, pl.ds(32 * by, 32), :] = piece
            if by == 1:
                edge = [
                    rows_ref[pl.ds(pz, 512, stride=2), :].reshape(8, 8, 8, LANES)[:, 7]
                    for pz in range(2)
                ]
                ys_ref[pl.ds(128 * bx, 128), :] = (
                    jnp.stack(edge, axis=1).reshape(128, LANES).astype(BF16)
                )
    xs_ref[...] = v_ref[15].reshape(256, LANES)
    early = jnp.concatenate(
        [cot_ref[...].astype(BF16), jnp.zeros((16, 64), BF16), ys_ref[240:256, :]], axis=1
    )
    early_ref[...] = jnp.broadcast_to(early[None], early_ref.shape)


def prepare_kernel(
    near_ref, w_hbm, routes_ref,
    wp_ref, group_ref,
    slot_ref, routes8_ref, w_ref, sems,
):
    fetches = [
        pltpu.make_async_copy(w_hbm.at[pl.ds(48 * i, 48)], w_ref.at[pl.ds(48 * i, 48)], sems.at[i])
        for i in range(4)
    ]
    for fetch in fetches:
        fetch.start()
    find_slots(near_ref, slot_ref)
    wp_ref[...] = jnp.zeros_like(wp_ref)
    for slot in range(8):
        routes8_ref[slot : slot + 1, :] = routes_ref[:, 64 * slot : 64 * slot + 64]
    routes = jnp.concatenate(
        [routes8_ref[pl.ds(slot_ref[p], 1), :] for p in range(8)], axis=0
    ).astype(BF16)
    row = lax.broadcasted_iota(jnp.int32, (64, 512), 1)
    inside = ((row >> 6) & 3) * 16 + ((row >> 3) & 3) * 4 + (row & 3)
    pick = (inside == lax.broadcasted_iota(jnp.int32, (64, 512), 0)).astype(F32).astype(BF16)
    spread = nn(routes, pick)
    row = lax.broadcasted_iota(jnp.int32, (8, 512), 1)
    place = (row >> 8) + ((row >> 5) & 1) * 2 + ((row >> 2) & 1) * 4
    mine = place == lax.broadcasted_iota(jnp.int32, (8, 512), 0)
    group = jnp.sum(jnp.where(mine, spread, 0.0), axis=0, keepdims=True)
    group_ref[...] = jnp.broadcast_to(group, (8, 512))

    for i, fetch in enumerate(fetches):
        fetch.wait()
        for tap in range(27):
            piece = w_ref[48 * i : 48 * i + 48, tap * CIN : tap * CIN + CIN]
            wp_ref[48 * i : 48 * i + 48, tap * LANES : tap * LANES + CIN] = piece


def shared_out(group, amounts):
    return jnp.concatenate(
        [jnp.where(group == float(g), amounts, 0.0) for g in range(GROUPS)], axis=0
    ).astype(BF16)


def forward_kernel(
    key_hbm, val_hbm, query_hbm, v_ref, xr_ref, yr_ref, bias_ref, wp_ref, group_ref, early_ref,
    podd_ref, peven_ref, slope_ref, hidt_ref, cott_ref, kut_ref, knt_ref, wt_ref, tt_ref, kt_ref,
    vw_ref, send_ref,
    key_ref, val_ref, query_ref, sems,
):
    copies = [
        pltpu.make_async_copy(source, target, sems.at[i])
        for i, (source, target) in enumerate(
            ((key_hbm, key_ref), (val_hbm, val_ref), (query_hbm, query_ref))
        )
    ]
    for copy in copies:
        copy.start()
    here = lax.axis_index("chip") * 2 + lax.axis_index("core")
    inner = jnp.logical_and(here >= 8, lax.rem(here, 8) > 0)
    corner = early_ref[pl.ds(pl.multiple_of(16 * jnp.maximum(here - 9, 0), 16), 16), 256:384]
    corner = jnp.where(inner, corner.astype(F32), 0.0)
    first = lax.broadcasted_iota(jnp.int32, (64, LANES), 0) % 8 == 0
    for x in range(-1, 16):
        if x < 0:
            planes, edge = xr_ref[...].astype(F32).reshape(4, 64, LANES), corner
        else:
            planes, edge = v_ref[x].astype(F32), yr_ref[pl.ds(16 * x, 16), :].astype(F32)
        if x % 2 == 0:
            out_ref, row = peven_ref, 32 * x
        else:
            out_ref, row = podd_ref, 32 * (x + 1)
        for b in range(3):
            for c in range(3):
                py, pz = (b + 1) % 2, (c + 1) % 2
                piece = planes[2 * py + pz]
                if b == 0:
                    piece = jnp.concatenate([edge[8 * pz : 8 * pz + 8], piece[0:56]], axis=0)
                if c == 0:
                    piece = jnp.where(first, 0.0, pltpu.roll(piece, 1, 0))
                column = (3 * b + c) * LANES
                out_ref[pl.ds(row, 64), pl.ds(column, LANES)] = piece.astype(BF16)
    before = (
        nt(podd_ref[0:512, :], wp_ref[:, 0:SLOTS9])
        + nt(peven_ref[...], wp_ref[:, SLOTS9 : 2 * SLOTS9])
        + nt(podd_ref[64:576, :], wp_ref[:, 2 * SLOTS9 : 3 * SLOTS9])
        + bias_ref[...]
    )
    square = before * before
    tanh = jnp.tanh(ROOT * before * (1.0 + CUBIC * square))
    hidden = (0.5 * before * (1.0 + tanh)).astype(BF16)
    slope = 0.5 * (1.0 + tanh) + 0.5 * before * (1.0 - tanh * tanh) * ROOT * (
        1.0 + 3.0 * CUBIC * square
    )
    slope_ref[...] = slope.T
    hidt_ref[...] = hidden.astype(F32).T.astype(BF16)

    for copy in copies:
        copy.wait()
    kh, kl = split(key_ref[...].T)
    vh, vl = split(val_ref[...])
    kt_ref[...] = kh
    vw_ref[...] = vh
    keys = nt(kh, hidden) + nt(kl, hidden)
    values = nn(hidden, vh) + nn(hidden, vl)
    queries = query_ref[...]
    qu = queries * lax.rsqrt(jnp.sum(queries * queries, axis=-1, keepdims=True) + EPS)
    key_norm = lax.rsqrt(jnp.sum(keys * keys, axis=0, keepdims=True) + EPS)
    kut = keys * key_norm
    kut_ref[...] = kut
    knt_ref[...] = jnp.broadcast_to(key_norm, (8, 512))
    weights = jnp.exp(TEMPER * nn(qu.astype(BF16), kut.astype(BF16)))
    wt_ref[...] = weights
    group = group_ref[...]
    shares = shared_out(group, weights)
    vb = values.astype(BF16)
    sums = nn(shares, jnp.concatenate([vb, jnp.ones((512, 64), BF16)], axis=1))
    cot = early_ref[:, 0:COUT]
    cott_ref[...] = cot.astype(F32).T.astype(BF16)
    meets = nt(cot, vb)
    total = jnp.zeros((8, 512), F32)
    for g in range(GROUPS):
        total = total + jnp.where(group == float(g), meets[8 * g : 8 * g + 8], 0.0)
    tt_ref[...] = total
    inner = jnp.sum(sums[:, 0:COUT] * cot.astype(F32), axis=-1, keepdims=True)
    lane = lax.broadcasted_iota(jnp.int32, (8, 64), 1)
    mass = jnp.zeros((8, 64), F32)
    dots = jnp.zeros((8, 64), F32)
    for g in range(GROUPS):
        mass = jnp.where(lane == g, sums[8 * g : 8 * g + 8, COUT:256], mass)
        dots = jnp.where(lane == g, inner[8 * g : 8 * g + 8], dots)
    table = jnp.concatenate([mass, dots], axis=0)
    send_ref[:, 0:COUT] = sums[:, 0:COUT].astype(BF16)
    send_ref[:, COUT:256] = jnp.concatenate([table.astype(BF16)] * 32, axis=0)


def backward_kernel(
    recv_ref, podd_ref, peven_ref, slope_ref, hidt_ref, kut_ref, knt_ref, wt_ref, tt_ref,
    group_ref, cott_ref, kt_ref, vw_ref, query_ref,
    pooled_ref, db_ref, xs_ref, ys_ref, keep_ref, give_ref, sum_ref,
):
    got = jnp.sum(recv_ref[...].reshape(32, 16, 256).astype(F32), axis=0)
    mass = got[0:8, COUT:256]
    dots = got[8:16, COUT:256]
    here = lax.axis_index("chip") * 2 + lax.axis_index("core")
    lane = lax.broadcasted_iota(jnp.int32, (8, 64), 1)
    own = [
        jnp.sum(jnp.where(lane == 2 * here + i, mass, 0.0), axis=-1, keepdims=True)
        for i in range(2)
    ]
    pooled_ref[...] = got[:, 0:COUT] / (1.0 + jnp.concatenate(own, axis=0))

    inverse = 1.0 / (1.0 + mass)
    d_mass = -dots * inverse * inverse
    ih, il = split(inverse)
    mh, ml = split(d_mass)
    group = group_ref[...]
    rows = lax.broadcasted_iota(jnp.int32, (64, 512), 0).astype(F32)
    member = (rows == jnp.broadcast_to(group[0:1], (64, 512))).astype(F32).astype(BF16)
    inv_row = nn(ih, member) + nn(il, member)
    dm_row = nn(mh, member) + nn(ml, member)
    weights = wt_ref[...]
    d_cos = TEMPER * weights * (tt_ref[...] * inv_row + dm_row)
    d_value = nn(cott_ref[...], shared_out(group, weights * inv_row))

    kut = kut_ref[...]
    queries = query_ref[...]
    qn = lax.rsqrt(jnp.sum(queries * queries, axis=-1, keepdims=True) + EPS)
    qu = queries * qn
    ch = d_cos.astype(BF16)
    d_ku = nn(qu.T.astype(BF16), ch)
    d_key = knt_ref[0:1, :] * (d_ku - kut * jnp.sum(kut * d_ku, axis=0, keepdims=True))
    d_qu = nt(ch, kut.astype(BF16))
    d_query = qn * (d_qu - qu * jnp.sum(qu * d_qu, axis=-1, keepdims=True))

    kh, vh = d_key.astype(BF16), d_value.astype(BF16)
    d_hidden = tn(kt_ref[...], kh) + nn(vw_ref[...], vh)
    d_before = d_hidden * slope_ref[...]
    dbt = d_before.astype(BF16)
    d_rows = d_before.T
    db = d_rows.astype(BF16)
    db_ref[...] = db
    xs_ref[...] = db[0:64]
    ys_ref[...] = d_rows.reshape(8, 64, COUT)[:, 0:8].reshape(64, COUT).astype(BF16)

    parts = (podd_ref[0:512, :], peven_ref[...], podd_ref[64:576, :])
    for a in range(3):
        grad = nn(dbt, parts[a])
        for tap in range(9):
            piece = grad[:, tap * LANES : tap * LANES + CIN]
            sum_ref[:, pl.ds((9 * a + tap) * CIN, CIN)] = piece
    sum_ref[:, KDIM : KDIM + COUT] = nt(hidt_ref[...], kh)
    sum_ref[:, KDIM + COUT : KDIM + 2 * COUT] = nt(hidt_ref[...], vh)
    bias = jnp.broadcast_to(jnp.sum(d_rows, axis=0, keepdims=True), (8, COUT))
    small = [d_query[:, 0:CIN], d_query[:, CIN:COUT], bias[:, 0:CIN], bias[:, CIN:COUT]]
    small = jnp.concatenate(small + [jnp.zeros((COUT - 32, CIN), F32)], axis=0)
    sum_ref[:, KDIM + 2 * COUT : WIDE] = small
    low = lax.axis_index("core") == 0
    for t in range(12):
        left = sum_ref[:, LANES * t : LANES * (t + 1)]
        right = sum_ref[:, LANES * (t + 12) : LANES * (t + 13)]
        keep_ref[COUT * t : COUT * (t + 1), :] = jnp.where(low, left, right)
        give_ref[COUT * t : COUT * (t + 1), :] = jnp.where(low, right, left).astype(BF16)


def add_kernel(a_ref, b_ref, out_ref):
    out_ref[0:USED, :] = (a_ref[...] + b_ref[...].astype(F32)).astype(BF16)
    out_ref[USED:HALF, :] = jnp.zeros((HALF - USED, LANES), BF16)


def total_kernel(recv_ref, out_ref):
    total = jnp.sum(recv_ref[...].astype(F32), axis=0).astype(BF16)
    out_ref[...] = jnp.broadcast_to(total[None], out_ref.shape)


def final_kernel(
    mine_ref, other_ref, dw_hbm, dk_ref, dv_ref, dq_ref, dbias_ref, dw_ref, tail_ref, sems
):
    low = lax.axis_index("core") == 0

    def tile(t, start, rows):
        place = COUT * (t % 12) + start
        mine = mine_ref[place : place + rows, :].astype(F32)
        other = other_ref[place : place + rows, :].astype(F32)
        return jnp.where(low, mine, other) if t < 12 else jnp.where(low, other, mine)

    copies = []
    for i in range(4):
        start = 48 * i
        for t in range(20):
            dw_ref[start : start + 48, LANES * t : LANES * (t + 1)] = tile(t, start, 48)
        for t in range(20, 24):
            tail_ref[start : start + 48, LANES * (t - 20) : LANES * (t - 19)] = tile(t, start, 48)
        dw_ref[start : start + 48, 20 * LANES : KDIM] = tail_ref[
            start : start + 48, 0 : KDIM - 20 * LANES
        ]
        copy = pltpu.make_async_copy(
            dw_ref.at[pl.ds(start, 48)], dw_hbm.at[pl.ds(start, 48)], sems.at[i]
        )
        copy.start()
        copies.append(copy)
    base = KDIM - 20 * LANES
    dk_ref[...] = tail_ref[:, base : base + COUT]
    dv_ref[...] = tail_ref[:, base + COUT : base + 2 * COUT]
    small = tail_ref[0:32, base + 2 * COUT : 4 * LANES]
    dq_ref[...] = jnp.concatenate([small[0:8], small[8:16]], axis=1)
    dbias_ref[...] = jnp.concatenate([small[16:17], small[24:25]], axis=1)
    for copy in copies:
        copy.wait()


def spread_kernel(
    near_ref, w_hbm, db_ref, xr_ref, yr_ref, xyr_ref, occ_ref, out_ref,
    ext_ref, even_ref, odd_ref, rows_ref, slot_ref, w_ref, wp_ref, sem,
):
    fetch = pltpu.make_async_copy(w_hbm, w_ref, sem)
    fetch.start()
    wp_ref[...] = jnp.zeros_like(wp_ref)
    find_slots(near_ref, slot_ref)
    edge = yr_ref[...].astype(F32)
    for jx in range(8):
        ext_ref[pl.ds(72 * jx, 64), :] = db_ref[pl.ds(64 * jx, 64), :].astype(F32)
        ext_ref[pl.ds(72 * jx + 64, 8), :] = edge[8 * jx : 8 * jx + 8]
    ext_ref[pl.ds(576, 64), :] = xr_ref[...].astype(F32)
    ext_ref[pl.ds(640, 8), :] = xyr_ref[...].astype(F32)[0:8]
    low = ext_ref[0:576, :].astype(BF16)
    high = ext_ref[72:648, :].astype(BF16)
    fetch.wait()
    for number in range(27):
        wp_ref[:, pl.ds(number * LANES, CIN)] = w_ref[:, pl.ds(number * CIN, CIN)]
    even_ref[...] = nn(low, wp_ref[:, SLOTS9 : 2 * SLOTS9])
    odd_ref[...] = nn(low, wp_ref[:, 2 * SLOTS9 : 3 * SLOTS9]) + nn(high, wp_ref[:, 0:SLOTS9])
    last = lax.broadcasted_iota(jnp.int32, (32, LANES), 0) % 8 == 7

    def up(piece):
        return jnp.where(last, 0.0, pltpu.roll(piece, 31, 0))

    for by in range(2):
        for bx in range(2):
            for xl in range(8):
                x = 8 * bx + xl
                src_ref = even_ref if x % 2 == 0 else odd_ref
                start = 72 * (x // 2) + 32 * by

                def tap(b, c, later, src_ref=src_ref, start=start):
                    return src_ref[pl.ds(start + 8 * later, 32), pl.ds((3 * b + c) * LANES, LANES)]

                e00 = tap(1, 1, 0)
                e01 = tap(1, 2, 0) + up(tap(1, 0, 0))
                e10 = tap(2, 1, 0) + tap(0, 1, 1)
                e11 = tap(2, 2, 0) + tap(0, 2, 1) + up(tap(2, 0, 0) + tap(0, 0, 1))
                for pz, (ye, yo) in enumerate(((e00, e10), (e01, e11))):
                    both = jnp.stack([ye.reshape(4, 8, LANES), yo.reshape(4, 8, LANES)], axis=1)
                    rows_ref[pl.ds(128 * xl + pz, 64, stride=2), :] = both.reshape(64, LANES)
            tile = rows_ref[...].reshape(64, 2, 8, LANES)
            for bz in range(2):
                place = bx + 2 * by + 4 * bz
                slot = slot_ref[place]
                block = tile[:, bz].reshape(512, LANES).T[0:CIN]
                block = jnp.where(occ_ref[pl.ds(slot, 1), :] > 0, block, 0.0)
                out_ref[slot] = block.astype(BF16)


def vm():
    return pl.BlockSpec(memory_space=pltpu.VMEM)


def like(shape, dtype=F32):
    return jax.ShapeDtypeStruct(shape, dtype)


def call(kernel, kinds, outs, scratch, *args, first_out=None):
    spaces = {"s": pltpu.SMEM, "h": pltpu.HBM, "v": pltpu.VMEM}
    kinds = kinds + "v" * (len(args) - len(kinds))
    in_specs = [pl.BlockSpec(memory_space=spaces[kind]) for kind in kinds]
    args = [
        pltpu.with_memory_space_constraint(arg, pltpu.HBM) if kind == "h" else arg
        for arg, kind in zip(args, kinds, strict=True)
    ]
    out_specs = jax.tree.map(lambda _: vm(), outs)
    if first_out is not None:
        out_specs[0] = pl.BlockSpec(memory_space=first_out)
    return pl.pallas_call(
        kernel,
        out_shape=outs,
        in_specs=in_specs,
        out_specs=out_specs,
        scratch_shapes=scratch,
        compiler_params=params(),
        name=kernel.__name__,
    )(*args)


def shift(shard, by_x, by_y):
    pairs = []
    for index in range(32):
        tx, ty = index % 8 + by_x, index // 8 + by_y
        if 0 <= tx < 8 and 0 <= ty < 4:
            pairs.append((index, ty * 8 + tx))
    return lax.ppermute(shard, SPACE, pairs)


def on_device(
    features, occupancy, neighbors, routes, cotangent, conv_weight, conv_bias,
    key_weight, value_weight, queries,
):
    features, occupancy = jnp.swapaxes(features[0], 1, 2), occupancy[0]
    slots = pltpu.SMEM((8,), jnp.int32)
    v, xs, ys, early = call(
        place_kernel, "hhhh",
        [
            like((16, 4, 64, LANES), BF16), like((256, LANES), BF16), like((256, LANES), BF16),
            like((32, 16, 3 * LANES), BF16),
        ],
        [
            pltpu.SMEM((6, 8), jnp.int32), pltpu.VMEM((8, CIN, 512), BF16),
            pltpu.VMEM((8, 512), jnp.int32), pltpu.VMEM((16, COUT), F32),
            pltpu.VMEM((1024, LANES), F32), slots, pltpu.SemaphoreType.DMA((11,)),
        ],
        neighbors, features, occupancy, cotangent.reshape(16, COUT),
    )
    early = lax.all_to_all(early, SPACE, 0, 0, tiled=True).reshape(512, 3 * LANES)
    xr = shift(xs, 1, 0)
    yr = shift(ys, 0, 1)
    wp, group = call(
        prepare_kernel, "sh",
        [
            like((COUT, 27 * LANES), BF16), like((8, 512)),
        ],
        [
            slots, pltpu.VMEM((8, 64), jnp.int32), pltpu.VMEM((COUT, KDIM), BF16),
            pltpu.SemaphoreType.DMA((4,)),
        ],
        neighbors, conv_weight.T, routes.reshape(1, 512),
    )
    podd, peven, slope, hidt, cott, kut, knt, wt, tt, kt, vw, send = call(
        forward_kernel, "hhh",
        [
            like((576, SLOTS9), BF16), like((512, SLOTS9), BF16), like((COUT, 512)),
            like((COUT, 512), BF16), like((COUT, 512), BF16), like((COUT, 512)), like((8, 512)),
            like((8, 512)), like((8, 512)), like((COUT, COUT), BF16),
            like((COUT, COUT), BF16), like((512, 256), BF16),
        ],
        [
            pltpu.VMEM((COUT, COUT), F32), pltpu.VMEM((COUT, COUT), F32),
            pltpu.VMEM((NQ, COUT), F32), pltpu.SemaphoreType.DMA((3,)),
        ],
        key_weight, value_weight, queries, v, xr, yr, conv_bias.reshape(1, COUT), wp, group, early,
    )
    recv = lax.all_to_all(send.reshape(32, 16, 256), SPACE, 0, 0, tiled=True).reshape(512, 256)
    pooled, db, bxs, bys, keep, give = call(
        backward_kernel, "",
        [
            like((16, COUT)), like((512, COUT), BF16), like((64, COUT), BF16),
            like((64, COUT), BF16), like((USED, LANES)), like((USED, LANES), BF16),
        ],
        [pltpu.VMEM((COUT, WIDE), F32)],
        recv, podd, peven, slope, hidt, kut, knt, wt, tt, group, cott, kt, vw, queries,
    )
    swap = [(0, 1), (1, 0)]
    taken = lax.ppermute(give, "core", swap)
    half = call(add_kernel, "", like((HALF, LANES), BF16), [], keep, taken)
    pieces = lax.all_to_all(half.reshape(64, SHARD, LANES), CHIPS, 0, 0, tiled=True)
    bxr = shift(bxs, -1, 0)
    byr = shift(bys, 0, -1)
    bxyr = shift(bys[0:16], -1, -1)
    copies = call(total_kernel, "", like((64, SHARD, LANES), BF16), [], pieces)
    bxr, byr, bxyr, copies = lax.optimization_barrier((bxr, byr, bxyr, copies))
    mine = lax.all_to_all(copies, CHIPS, 0, 0, tiled=True).reshape(HALF, LANES)
    d_features = call(
        spread_kernel, "sh", like((8, CIN, 512), BF16),
        [
            pltpu.VMEM((648, COUT), F32), pltpu.VMEM((576, SLOTS9), F32),
            pltpu.VMEM((576, SLOTS9), F32), pltpu.VMEM((1024, LANES), F32), slots,
            pltpu.VMEM((COUT, KDIM), BF16), pltpu.VMEM((COUT, 27 * LANES), BF16),
            pltpu.SemaphoreType.DMA,
        ],
        neighbors, conv_weight.T, db, bxr, byr, bxyr, occupancy,
    )
    mine, d_features = lax.optimization_barrier((mine, d_features))
    other = lax.ppermute(mine, "core", swap)
    d_weight, d_key, d_value, d_query, d_bias = call(
        final_kernel, "",
        [
            like((COUT, KDIM)), like((COUT, COUT)), like((COUT, COUT)), like((NQ, COUT)),
            like((1, COUT)),
        ],
        [
            pltpu.VMEM((COUT, KDIM), F32), pltpu.VMEM((COUT, 4 * LANES), F32),
            pltpu.SemaphoreType.DMA((4,)),
        ],
        mine, other, first_out=pltpu.HBM,
    )
    return (
        pooled.reshape(1, 2, NQ, COUT), jnp.swapaxes(d_features, 1, 2)[None], d_weight.T,
        d_bias.reshape(COUT), d_key, d_value, d_query,
    )


def solution(mesh):
    fine = Mesh(mesh.devices.reshape(4, 16, 2), ("section", "chip", "core"))
    in_specs = (
        P("section", SPACE, None, None),
        P("section", SPACE, None),
        P(None, SPACE),
        P("section", SPACE, None),
        P("section", SPACE, None, None),
        P(),
        P(),
        P(),
        P(),
        P(),
    )
    out_specs = (
        P("section", SPACE, None, None),
        P("section", SPACE, None, None),
        P(),
        P(),
        P(),
        P(),
        P(),
    )
    return jax.shard_map(
        on_device, mesh=fine, in_specs=in_specs, out_specs=out_specs, check_vma=False
    )
```

```python
import functools

import jax
import jax.numpy as jnp
from jax import lax
from jax.experimental import pallas as pl
from jax.experimental.pallas import tpu as pltpu
from jax.sharding import Mesh, PartitionSpec as P

EPS = 1e-06
TEMPER = 8.0
CIN, COUT = 96, 192
LANES = 128
SLOTS9 = 9 * LANES
GROUPS, NQ = 64, 8
KDIM = 27 * CIN
SHARD = 40
PACKED, PACKS = 9 * CIN, 7 * LANES
HALF = 64 * SHARD
USED = 12 * COUT
WIDE = 24 * LANES
F32, BF16 = jnp.float32, jnp.bfloat16
SPACE = ("chip", "core")
CHIPS = ("section", "chip")
ROOT, CUBIC = 0.7978845608028654, 0.044715
VMEM_LIMIT = 44 * 1024 * 1024


def params():
    return pltpu.CompilerParams(vmem_limit_bytes=VMEM_LIMIT)


def nn(a, b):
    return lax.dot_general(a, b, (((1,), (0,)), ((), ())), preferred_element_type=F32)


def nt(a, b):
    return lax.dot_general(a, b, (((1,), (1,)), ((), ())), preferred_element_type=F32)


def tn(a, b):
    return lax.dot_general(a, b, (((0,), (0,)), ((), ())), preferred_element_type=F32)


def split(a):
    high = a.astype(BF16)
    return high, (a - high.astype(F32)).astype(BF16)


def find_slots(near_ref, slot_ref):
    here = lax.axis_index("chip") * 2 + lax.axis_index("core")
    for place in range(8):
        slot_ref[place] = 0
    for slot in range(8):
        place = 0
        for axis in range(3):
            beside = near_ref[axis, slot]
            inner = jnp.logical_and(beside >= 0, lax.shift_right_arithmetic(beside, 3) == here)
            place = place + jnp.where(inner, 0, 1 << axis)
        slot_ref[place] = slot


def place_kernel(
    near_hbm, feat_hbm, occ_hbm, cot_hbm, v_ref, xs_ref, ys_ref, early_ref,
    near_ref, feat_ref, occ_ref, cot_ref, rows_ref, slot_ref, sems,
):
    pairs = [
        (near_hbm, near_ref), (feat_hbm, feat_ref), (occ_hbm, occ_ref), (cot_hbm, cot_ref),
    ]
    copies = [
        pltpu.make_async_copy(source, target, sems.at[i])
        for i, (source, target) in enumerate(pairs)
    ]
    for copy in copies:
        copy.start()
    rows_ref[...] = jnp.zeros_like(rows_ref)
    for copy in copies:
        copy.wait()
    find_slots(near_ref, slot_ref)
    for by in range(2):
        for bx in range(2):
            pair = []
            for bz in range(2):
                place = bx + 2 * by + 4 * bz
                slot = slot_ref[place]
                block = feat_ref[slot].astype(F32)
                block = jnp.where(occ_ref[pl.ds(slot, 1), :] > 0, block, 0.0).T
                pair.append(block.reshape(64, 8, CIN))
            rows_ref[:, 0:CIN] = jnp.stack(pair, axis=1).reshape(1024, CIN)
            for pz in range(2):
                part = rows_ref[pl.ds(pz, 512, stride=2), :].reshape(8, 4, 2, 8, LANES)
                for py in range(2):
                    piece = part[:, :, py].reshape(8, 32, LANES).astype(BF16)
                    v_ref[pl.ds(8 * bx, 8), 2 * py + pz, pl.ds(32 * by, 32), :] = piece
            if by == 1:
                edge = [
                    rows_ref[pl.ds(pz, 512, stride=2), :].reshape(8, 8, 8, LANES)[:, 7]
                    for pz in range(2)
                ]
                ys_ref[pl.ds(128 * bx, 128), :] = (
                    jnp.stack(edge, axis=1).reshape(128, LANES).astype(BF16)
                )
    xs_ref[...] = v_ref[15].reshape(256, LANES)
    early = jnp.concatenate(
        [cot_ref[...].astype(BF16), jnp.zeros((16, 64), BF16), ys_ref[240:256, :]], axis=1
    )
    early_ref[...] = jnp.broadcast_to(early[None], early_ref.shape)


def row_groups(routes_ref, routes8_ref, slot_ref):
    for slot in range(8):
        routes8_ref[slot : slot + 1, :] = routes_ref[:, 64 * slot : 64 * slot + 64]
    routes = jnp.concatenate(
        [routes8_ref[pl.ds(slot_ref[p], 1), :] for p in range(8)], axis=0
    ).astype(BF16)
    row = lax.broadcasted_iota(jnp.int32, (64, 512), 1)
    inside = ((row >> 6) & 3) * 16 + ((row >> 3) & 3) * 4 + (row & 3)
    pick = (inside == lax.broadcasted_iota(jnp.int32, (64, 512), 0)).astype(F32).astype(BF16)
    spread = nn(routes, pick)
    row = lax.broadcasted_iota(jnp.int32, (8, 512), 1)
    place = (row >> 8) + ((row >> 5) & 1) * 2 + ((row >> 2) & 1) * 4
    mine = place == lax.broadcasted_iota(jnp.int32, (8, 512), 0)
    group = jnp.sum(jnp.where(mine, spread, 0.0), axis=0, keepdims=True)
    return jnp.broadcast_to(group, (8, 512))


def pad_weights(w_ref, wp_ref):
    for a in range(3):
        wp_ref[:, PACKS * a : PACKS * a + PACKED] = w_ref[:, PACKED * a : PACKED * (a + 1)]
        wp_ref[:, PACKS * a + PACKED : PACKS * (a + 1)] = jnp.zeros((COUT, PACKS - PACKED), BF16)


def shared_out(group, amounts):
    return jnp.concatenate(
        [jnp.where(group == float(g), amounts, 0.0) for g in range(GROUPS)], axis=0
    ).astype(BF16)


def forward_kernel(
    near_hbm, key_hbm, val_hbm, query_hbm, bias_hbm, routes_hbm, v_ref, xr_ref, yr_ref, w_ref,
    early_ref,
    podd_ref, peven_ref, slope_ref, hidt_ref, cott_ref, kut_ref, knt_ref, wt_ref, tt_ref, kt_ref,
    vw_ref, group_ref, send_ref,
    near_ref, key_ref, val_ref, query_ref, bias_ref, routes_ref, sems, slot_ref, routes8_ref, wp_ref,
):
    copies = [
        pltpu.make_async_copy(source, target, sems.at[i])
        for i, (source, target) in enumerate(
            (
                (near_hbm, near_ref), (key_hbm, key_ref), (val_hbm, val_ref),
                (query_hbm, query_ref), (bias_hbm, bias_ref), (routes_hbm, routes_ref),
            )
        )
    ]
    for copy in copies:
        copy.start()
    pad_weights(w_ref, wp_ref)
    here = lax.axis_index("chip") * 2 + lax.axis_index("core")
    inner = jnp.logical_and(here >= 8, lax.rem(here, 8) > 0)
    corner = early_ref[pl.ds(pl.multiple_of(16 * jnp.maximum(here - 9, 0), 16), 16), 256:384]
    corner = jnp.where(inner, corner.astype(F32), 0.0)
    first = lax.broadcasted_iota(jnp.int32, (64, LANES), 0) % 8 == 0
    for x in range(-1, 16):
        if x < 0:
            planes, edge = xr_ref[...].astype(F32).reshape(4, 64, LANES), corner
        else:
            planes, edge = v_ref[x].astype(F32), yr_ref[pl.ds(16 * x, 16), :].astype(F32)
        if x % 2 == 0:
            out_ref, row = peven_ref, 32 * x
        else:
            out_ref, row = podd_ref, 32 * (x + 1)
        for b in range(3):
            for c in range(3):
                py, pz = (b + 1) % 2, (c + 1) % 2
                piece = planes[2 * py + pz]
                if b == 0:
                    piece = jnp.concatenate([edge[8 * pz : 8 * pz + 8], piece[0:56]], axis=0)
                if c == 0:
                    piece = jnp.where(first, 0.0, pltpu.roll(piece, 1, 0))
                column = (3 * b + c) * CIN
                out_ref[pl.ds(row, 64), pl.ds(column, CIN)] = piece[:, 0:CIN].astype(BF16)
        out_ref[pl.ds(row, 64), PACKED:PACKS] = jnp.zeros((64, PACKS - PACKED), BF16)
    for copy in copies:
        copy.wait()
    find_slots(near_ref, slot_ref)
    group = row_groups(routes_ref, routes8_ref, slot_ref)
    group_ref[...] = group
    before = (
        nt(podd_ref[0:512, :], wp_ref[:, 0:PACKS])
        + nt(peven_ref[...], wp_ref[:, PACKS : 2 * PACKS])
        + nt(podd_ref[64:576, :], wp_ref[:, 2 * PACKS : 3 * PACKS])
        + bias_ref[...]
    )
    square = before * before
    tanh = jnp.tanh(ROOT * before * (1.0 + CUBIC * square))
    hidden = (0.5 * before * (1.0 + tanh)).astype(BF16)
    slope = 0.5 * (1.0 + tanh) + 0.5 * before * (1.0 - tanh * tanh) * ROOT * (
        1.0 + 3.0 * CUBIC * square
    )
    slope_ref[...] = slope.T
    hidt_ref[...] = hidden.astype(F32).T.astype(BF16)

    kh, kl = split(key_ref[...].T)
    vh, vl = split(val_ref[...])
    kt_ref[...] = kh
    vw_ref[...] = vh
    keys = nt(kh, hidden) + nt(kl, hidden)
    values = nn(hidden, vh) + nn(hidden, vl)
    queries = query_ref[...]
    qu = queries * lax.rsqrt(jnp.sum(queries * queries, axis=-1, keepdims=True) + EPS)
    key_norm = lax.rsqrt(jnp.sum(keys * keys, axis=0, keepdims=True) + EPS)
    kut = keys * key_norm
    kut_ref[...] = kut
    knt_ref[...] = jnp.broadcast_to(key_norm, (8, 512))
    weights = jnp.exp(TEMPER * nn(qu.astype(BF16), kut.astype(BF16)))
    wt_ref[...] = weights
    shares = shared_out(group, weights)
    vb = values.astype(BF16)
    sums = nn(shares, jnp.concatenate([vb, jnp.ones((512, 64), BF16)], axis=1))
    cot = early_ref[:, 0:COUT]
    cott_ref[...] = cot.astype(F32).T.astype(BF16)
    meets = nt(cot, vb)
    total = jnp.zeros((8, 512), F32)
    for g in range(GROUPS):
        total = total + jnp.where(group == float(g), meets[8 * g : 8 * g + 8], 0.0)
    tt_ref[...] = total
    inner = jnp.sum(sums[:, 0:COUT] * cot.astype(F32), axis=-1, keepdims=True)
    lane = lax.broadcasted_iota(jnp.int32, (8, 64), 1)
    mass = jnp.zeros((8, 64), F32)
    dots = jnp.zeros((8, 64), F32)
    for g in range(GROUPS):
        mass = jnp.where(lane == g, sums[8 * g : 8 * g + 8, COUT:256], mass)
        dots = jnp.where(lane == g, inner[8 * g : 8 * g + 8], dots)
    table = jnp.concatenate([mass, dots], axis=0)
    send_ref[:, 0:COUT] = sums[:, 0:COUT].astype(BF16)
    send_ref[:, COUT:256] = jnp.concatenate([table.astype(BF16)] * 32, axis=0)


def backward_kernel(
    recv_ref, podd_ref, peven_ref, slope_ref, hidt_ref, kut_ref, knt_ref, wt_ref, tt_ref,
    group_ref, cott_ref, kt_ref, vw_ref, query_ref,
    pooled_ref, db_ref, xs_ref, ys_ref, keep_ref, give_ref, sum_ref,
):
    got = jnp.sum(recv_ref[...].reshape(32, 16, 256).astype(F32), axis=0)
    mass = got[0:8, COUT:256]
    dots = got[8:16, COUT:256]
    here = lax.axis_index("chip") * 2 + lax.axis_index("core")
    lane = lax.broadcasted_iota(jnp.int32, (8, 64), 1)
    own = [
        jnp.sum(jnp.where(lane == 2 * here + i, mass, 0.0), axis=-1, keepdims=True)
        for i in range(2)
    ]
    pooled_ref[...] = got[:, 0:COUT] / (1.0 + jnp.concatenate(own, axis=0))

    inverse = 1.0 / (1.0 + mass)
    d_mass = -dots * inverse * inverse
    ih, il = split(inverse)
    mh, ml = split(d_mass)
    group = group_ref[...]
    rows = lax.broadcasted_iota(jnp.int32, (64, 512), 0).astype(F32)
    member = (rows == jnp.broadcast_to(group[0:1], (64, 512))).astype(F32).astype(BF16)
    inv_row = nn(ih, member) + nn(il, member)
    dm_row = nn(mh, member) + nn(ml, member)
    weights = wt_ref[...]
    d_cos = TEMPER * weights * (tt_ref[...] * inv_row + dm_row)
    d_value = nn(cott_ref[...], shared_out(group, weights * inv_row))

    kut = kut_ref[...]
    queries = query_ref[...]
    qn = lax.rsqrt(jnp.sum(queries * queries, axis=-1, keepdims=True) + EPS)
    qu = queries * qn
    ch = d_cos.astype(BF16)
    d_ku = nn(qu.T.astype(BF16), ch)
    d_key = knt_ref[0:1, :] * (d_ku - kut * jnp.sum(kut * d_ku, axis=0, keepdims=True))
    d_qu = nt(ch, kut.astype(BF16))
    d_query = qn * (d_qu - qu * jnp.sum(qu * d_qu, axis=-1, keepdims=True))

    kh, vh = d_key.astype(BF16), d_value.astype(BF16)
    d_hidden = tn(kt_ref[...], kh) + nn(vw_ref[...], vh)
    d_before = d_hidden * slope_ref[...]
    dbt = d_before.astype(BF16)
    d_rows = d_before.T
    db = d_rows.astype(BF16)
    db_ref[...] = db
    xs_ref[...] = db[0:64]
    ys_ref[...] = d_rows.reshape(8, 64, COUT)[:, 0:8].reshape(64, COUT).astype(BF16)

    parts = (podd_ref[0:512, :], peven_ref[...], podd_ref[64:576, :])
    for a in range(3):
        sum_ref[:, PACKED * a : PACKED * (a + 1)] = nn(dbt, parts[a])[:, 0:PACKED]
    sum_ref[:, KDIM : KDIM + COUT] = nt(hidt_ref[...], kh)
    sum_ref[:, KDIM + COUT : KDIM + 2 * COUT] = nt(hidt_ref[...], vh)
    bias = jnp.broadcast_to(jnp.sum(d_rows, axis=0, keepdims=True), (8, COUT))
    small = [d_query[:, 0:CIN], d_query[:, CIN:COUT], bias[:, 0:CIN], bias[:, CIN:COUT]]
    small = jnp.concatenate(small + [jnp.zeros((COUT - 32, CIN), F32)], axis=0)
    sum_ref[:, KDIM + 2 * COUT : WIDE] = small
    low = lax.axis_index("core") == 0
    for t in range(12):
        left = sum_ref[:, LANES * t : LANES * (t + 1)]
        right = sum_ref[:, LANES * (t + 12) : LANES * (t + 13)]
        keep_ref[COUT * t : COUT * (t + 1), :] = jnp.where(low, left, right)
        give_ref[COUT * t : COUT * (t + 1), :] = jnp.where(low, right, left).astype(BF16)


def add_kernel(a_ref, b_ref, out_ref):
    out_ref[0:USED, :] = (a_ref[...] + b_ref[...].astype(F32)).astype(BF16)
    out_ref[USED:HALF, :] = jnp.zeros((HALF - USED, LANES), BF16)


def total_kernel(recv_ref, out_ref):
    total = jnp.sum(recv_ref[...].astype(F32), axis=0).astype(BF16)
    out_ref[...] = jnp.broadcast_to(total[None], out_ref.shape)


def final_kernel(mine_ref, other_ref, dw_ref, dk_ref, dv_ref, dq_ref, dbias_ref, all_ref):
    low = lax.axis_index("core") == 0
    for t in range(12):
        mine = mine_ref[COUT * t : COUT * (t + 1), :].astype(F32)
        other = other_ref[COUT * t : COUT * (t + 1), :].astype(F32)
        all_ref[:, LANES * t : LANES * (t + 1)] = jnp.where(low, mine, other)
        all_ref[:, LANES * (t + 12) : LANES * (t + 13)] = jnp.where(low, other, mine)
    dw_ref[...] = all_ref[:, 0:KDIM]
    dk_ref[...] = all_ref[:, KDIM : KDIM + COUT]
    dv_ref[...] = all_ref[:, KDIM + COUT : KDIM + 2 * COUT]
    small = all_ref[0:32, KDIM + 2 * COUT : WIDE]
    dq_ref[...] = jnp.concatenate([small[0:8], small[8:16]], axis=1)
    dbias_ref[...] = jnp.concatenate([small[16:17], small[24:25]], axis=1)


def spread_kernel(
    near_ref, w_hbm, db_ref, xr_ref, yr_ref, xyr_ref, occ_ref, out_ref,
    ext_ref, even_ref, odd_ref, rows_ref, slot_ref, w_ref, wp_ref, sem,
):
    fetch = pltpu.make_async_copy(w_hbm, w_ref, sem)
    fetch.start()
    wp_ref[...] = jnp.zeros_like(wp_ref)
    find_slots(near_ref, slot_ref)
    edge = yr_ref[...].astype(F32)
    for jx in range(8):
        ext_ref[pl.ds(72 * jx, 64), :] = db_ref[pl.ds(64 * jx, 64), :].astype(F32)
        ext_ref[pl.ds(72 * jx + 64, 8), :] = edge[8 * jx : 8 * jx + 8]
    ext_ref[pl.ds(576, 64), :] = xr_ref[...].astype(F32)
    ext_ref[pl.ds(640, 8), :] = xyr_ref[...].astype(F32)[0:8]
    low = ext_ref[0:576, :].astype(BF16)
    high = ext_ref[72:648, :].astype(BF16)
    fetch.wait()
    for number in range(27):
        wp_ref[:, pl.ds(number * LANES, CIN)] = w_ref[:, pl.ds(number * CIN, CIN)]
    even_ref[...] = nn(low, wp_ref[:, SLOTS9 : 2 * SLOTS9])
    odd_ref[...] = nn(low, wp_ref[:, 2 * SLOTS9 : 3 * SLOTS9]) + nn(high, wp_ref[:, 0:SLOTS9])
    last = lax.broadcasted_iota(jnp.int32, (32, LANES), 0) % 8 == 7

    def up(piece):
        return jnp.where(last, 0.0, pltpu.roll(piece, 31, 0))

    for by in range(2):
        for bx in range(2):
            for xl in range(8):
                x = 8 * bx + xl
                src_ref = even_ref if x % 2 == 0 else odd_ref
                start = 72 * (x // 2) + 32 * by

                def tap(b, c, later, src_ref=src_ref, start=start):
                    return src_ref[pl.ds(start + 8 * later, 32), pl.ds((3 * b + c) * LANES, LANES)]

                e00 = tap(1, 1, 0)
                e01 = tap(1, 2, 0) + up(tap(1, 0, 0))
                e10 = tap(2, 1, 0) + tap(0, 1, 1)
                e11 = tap(2, 2, 0) + tap(0, 2, 1) + up(tap(2, 0, 0) + tap(0, 0, 1))
                for pz, (ye, yo) in enumerate(((e00, e10), (e01, e11))):
                    both = jnp.stack([ye.reshape(4, 8, LANES), yo.reshape(4, 8, LANES)], axis=1)
                    rows_ref[pl.ds(128 * xl + pz, 64, stride=2), :] = both.reshape(64, LANES)
            tile = rows_ref[...].reshape(64, 2, 8, LANES)
            for bz in range(2):
                place = bx + 2 * by + 4 * bz
                slot = slot_ref[place]
                block = tile[:, bz].reshape(512, LANES).T[0:CIN]
                block = jnp.where(occ_ref[pl.ds(slot, 1), :] > 0, block, 0.0)
                out_ref[slot] = block.astype(BF16)


def vm():
    return pl.BlockSpec(memory_space=pltpu.VMEM)


def like(shape, dtype=F32):
    return jax.ShapeDtypeStruct(shape, dtype)


def call(kernel, kinds, outs, scratch, *args):
    spaces = {"s": pltpu.SMEM, "h": pltpu.HBM, "v": pltpu.VMEM}
    kinds = kinds + "v" * (len(args) - len(kinds))
    in_specs = [pl.BlockSpec(memory_space=spaces[kind]) for kind in kinds]
    args = [
        pltpu.with_memory_space_constraint(arg, pltpu.HBM) if kind == "h" else arg
        for arg, kind in zip(args, kinds, strict=True)
    ]
    return pl.pallas_call(
        kernel,
        out_shape=outs,
        in_specs=in_specs,
        out_specs=jax.tree.map(lambda _: vm(), outs),
        scratch_shapes=scratch,
        compiler_params=params(),
        name=kernel.__name__,
    )(*args)


def shift(shard, by_x, by_y):
    pairs = []
    for index in range(32):
        tx, ty = index % 8 + by_x, index // 8 + by_y
        if 0 <= tx < 8 and 0 <= ty < 4:
            pairs.append((index, ty * 8 + tx))
    return lax.ppermute(shard, SPACE, pairs)


def on_device(
    features, occupancy, neighbors, routes, cotangent, conv_weight, conv_bias,
    key_weight, value_weight, queries,
):
    features, occupancy = jnp.swapaxes(features[0], 1, 2), occupancy[0]
    slots = pltpu.SMEM((8,), jnp.int32)
    v, xs, ys, early = call(
        place_kernel, "hhhh",
        [
            like((16, 4, 64, LANES), BF16), like((256, LANES), BF16), like((256, LANES), BF16),
            like((32, 16, 3 * LANES), BF16),
        ],
        [
            pltpu.SMEM((6, 8), jnp.int32), pltpu.VMEM((8, CIN, 512), BF16),
            pltpu.VMEM((8, 512), jnp.int32), pltpu.VMEM((16, COUT), F32),
            pltpu.VMEM((1024, LANES), F32), slots, pltpu.SemaphoreType.DMA((4,)),
        ],
        neighbors, features, occupancy, cotangent.reshape(16, COUT),
    )
    early = lax.all_to_all(early, SPACE, 0, 0, tiled=True).reshape(512, 3 * LANES)
    xr = shift(xs, 1, 0)
    yr = shift(ys, 0, 1)
    podd, peven, slope, hidt, cott, kut, knt, wt, tt, kt, vw, group, send = call(
        forward_kernel, "hhhhhh",
        [
            like((576, PACKS), BF16), like((512, PACKS), BF16), like((COUT, 512)),
            like((COUT, 512), BF16), like((COUT, 512), BF16), like((COUT, 512)), like((8, 512)),
            like((8, 512)), like((8, 512)), like((COUT, COUT), BF16),
            like((COUT, COUT), BF16), like((8, 512)), like((512, 256), BF16),
        ],
        [
            pltpu.SMEM((6, 8), jnp.int32), pltpu.VMEM((COUT, COUT), F32),
            pltpu.VMEM((COUT, COUT), F32), pltpu.VMEM((NQ, COUT), F32), pltpu.VMEM((1, COUT), F32),
            pltpu.VMEM((1, 512), jnp.int32), pltpu.SemaphoreType.DMA((6,)), slots,
            pltpu.VMEM((8, 64), jnp.int32), pltpu.VMEM((COUT, 3 * PACKS), BF16),
        ],
        neighbors, key_weight, value_weight, queries, conv_bias.reshape(1, COUT),
        routes.reshape(1, 512), v, xr, yr, conv_weight.T, early,
    )
    recv = lax.all_to_all(send.reshape(32, 16, 256), SPACE, 0, 0, tiled=True).reshape(512, 256)
    pooled, db, bxs, bys, keep, give = call(
        backward_kernel, "",
        [
            like((16, COUT)), like((512, COUT), BF16), like((64, COUT), BF16),
            like((64, COUT), BF16), like((USED, LANES)), like((USED, LANES), BF16),
        ],
        [pltpu.VMEM((COUT, WIDE), F32)],
        recv, podd, peven, slope, hidt, kut, knt, wt, tt, group, cott, kt, vw, queries,
    )
    swap = [(0, 1), (1, 0)]
    taken = lax.ppermute(give, "core", swap)
    half = call(add_kernel, "", like((HALF, LANES), BF16), [], keep, taken)
    pieces = lax.all_to_all(half.reshape(64, SHARD, LANES), CHIPS, 0, 0, tiled=True)
    bxr = shift(bxs, -1, 0)
    byr = shift(bys, 0, -1)
    bxyr = shift(bys[0:16], -1, -1)
    copies = call(total_kernel, "", like((64, SHARD, LANES), BF16), [], pieces)
    bxr, byr, bxyr, copies = lax.optimization_barrier((bxr, byr, bxyr, copies))
    mine = lax.all_to_all(copies, CHIPS, 0, 0, tiled=True).reshape(HALF, LANES)
    d_features = call(
        spread_kernel, "sh", like((8, CIN, 512), BF16),
        [
            pltpu.VMEM((648, COUT), F32), pltpu.VMEM((576, SLOTS9), F32),
            pltpu.VMEM((576, SLOTS9), F32), pltpu.VMEM((1024, LANES), F32), slots,
            pltpu.VMEM((COUT, KDIM), BF16), pltpu.VMEM((COUT, 27 * LANES), BF16),
            pltpu.SemaphoreType.DMA,
        ],
        neighbors, conv_weight.T, db, bxr, byr, bxyr, occupancy,
    )
    mine, d_features = lax.optimization_barrier((mine, d_features))
    other = lax.ppermute(mine, "core", swap)
    d_weight, d_key, d_value, d_query, d_bias = call(
        final_kernel, "",
        [
            like((COUT, KDIM)), like((COUT, COUT)), like((COUT, COUT)), like((NQ, COUT)),
            like((1, COUT)),
        ],
        [pltpu.VMEM((COUT, WIDE), F32)],
        mine, other,
    )
    return (
        pooled.reshape(1, 2, NQ, COUT), jnp.swapaxes(d_features, 1, 2)[None], d_weight.T,
        d_bias.reshape(COUT), d_key, d_value, d_query,
    )


def solution(mesh):
    fine = Mesh(mesh.devices.reshape(4, 16, 2), ("section", "chip", "core"))
    in_specs = (
        P("section", SPACE, None, None),
        P("section", SPACE, None),
        P(None, SPACE),
        P("section", SPACE, None),
        P("section", SPACE, None, None),
        P(),
        P(),
        P(),
        P(),
        P(),
    )
    out_specs = (
        P("section", SPACE, None, None),
        P("section", SPACE, None, None),
        P(),
        P(),
        P(),
        P(),
        P(),
    )
    return jax.shard_map(
        on_device, mesh=fine, in_specs=in_specs, out_specs=out_specs, check_vma=False
    )
```

```python
import functools

import jax
import jax.numpy as jnp
from jax import lax
from jax.experimental import pallas as pl
from jax.experimental.pallas import tpu as pltpu
from jax.sharding import Mesh, PartitionSpec as P

EPS = 1e-06
TEMPER = 8.0
CIN, COUT = 96, 192
LANES = 128
SLOTS9 = 9 * LANES
GROUPS, NQ = 64, 8
KDIM = 27 * CIN
SHARD = 40
HALF = 64 * SHARD
USED = 12 * COUT
WIDE = 24 * LANES
F32, BF16 = jnp.float32, jnp.bfloat16
SPACE = ("chip", "core")
CHIPS = ("section", "chip")
ROOT, CUBIC = 0.7978845608028654, 0.044715
VMEM_LIMIT = 44 * 1024 * 1024


def params():
    return pltpu.CompilerParams(vmem_limit_bytes=VMEM_LIMIT)


def nn(a, b):
    return lax.dot_general(a, b, (((1,), (0,)), ((), ())), preferred_element_type=F32)


def nt(a, b):
    return lax.dot_general(a, b, (((1,), (1,)), ((), ())), preferred_element_type=F32)


def tn(a, b):
    return lax.dot_general(a, b, (((0,), (0,)), ((), ())), preferred_element_type=F32)


def split(a):
    high = a.astype(BF16)
    return high, (a - high.astype(F32)).astype(BF16)


def find_slots(near_ref, slot_ref):
    here = lax.axis_index("chip") * 2 + lax.axis_index("core")
    for place in range(8):
        slot_ref[place] = 0
    for slot in range(8):
        place = 0
        for axis in range(3):
            beside = near_ref[axis, slot]
            inner = jnp.logical_and(beside >= 0, lax.shift_right_arithmetic(beside, 3) == here)
            place = place + jnp.where(inner, 0, 1 << axis)
        slot_ref[place] = slot


def place_kernel(
    near_hbm, feat_hbm, occ_hbm, cot_hbm, v_ref, xs_ref, ys_ref, early_ref,
    near_ref, feat_ref, occ_ref, cot_ref, rows_ref, slot_ref, sems,
):
    copies = [
        pltpu.make_async_copy(source, target, sems.at[i])
        for i, (source, target) in enumerate(
            (
                (near_hbm, near_ref), (feat_hbm, feat_ref), (occ_hbm, occ_ref), (cot_hbm, cot_ref),
            )
        )
    ]
    for copy in copies:
        copy.start()
    rows_ref[...] = jnp.zeros_like(rows_ref)
    for copy in copies:
        copy.wait()
    find_slots(near_ref, slot_ref)
    for by in range(2):
        for bx in range(2):
            pair = []
            for bz in range(2):
                place = bx + 2 * by + 4 * bz
                slot = slot_ref[place]
                block = feat_ref[slot].astype(F32)
                block = jnp.where(occ_ref[pl.ds(slot, 1), :] > 0, block, 0.0).T
                pair.append(block.reshape(64, 8, CIN))
            rows_ref[:, 0:CIN] = jnp.stack(pair, axis=1).reshape(1024, CIN)
            for pz in range(2):
                part = rows_ref[pl.ds(pz, 512, stride=2), :].reshape(8, 4, 2, 8, LANES)
                for py in range(2):
                    piece = part[:, :, py].reshape(8, 32, LANES).astype(BF16)
                    v_ref[pl.ds(8 * bx, 8), 2 * py + pz, pl.ds(32 * by, 32), :] = piece
            if by == 1:
                edge = [
                    rows_ref[pl.ds(pz, 512, stride=2), :].reshape(8, 8, 8, LANES)[:, 7]
                    for pz in range(2)
                ]
                ys_ref[pl.ds(128 * bx, 128), :] = (
                    jnp.stack(edge, axis=1).reshape(128, LANES).astype(BF16)
                )
    xs_ref[...] = v_ref[15].reshape(256, LANES)
    early = jnp.concatenate(
        [cot_ref[...].astype(BF16), jnp.zeros((16, 64), BF16), ys_ref[240:256, :]], axis=1
    )
    early_ref[...] = jnp.broadcast_to(early[None], early_ref.shape)


def prepare_kernel(
    near_ref, w_hbm, routes_ref,
    wp_ref, group_ref,
    slot_ref, routes8_ref, w_ref, sems,
):
    fetches = [
        pltpu.make_async_copy(w_hbm.at[pl.ds(48 * i, 48)], w_ref.at[pl.ds(48 * i, 48)], sems.at[i])
        for i in range(4)
    ]
    for fetch in fetches:
        fetch.start()
    find_slots(near_ref, slot_ref)
    wp_ref[...] = jnp.zeros_like(wp_ref)
    for slot in range(8):
        routes8_ref[slot : slot + 1, :] = routes_ref[:, 64 * slot : 64 * slot + 64]
    routes = jnp.concatenate(
        [routes8_ref[pl.ds(slot_ref[p], 1), :] for p in range(8)], axis=0
    ).astype(BF16)
    row = lax.broadcasted_iota(jnp.int32, (64, 512), 1)
    inside = ((row >> 6) & 3) * 16 + ((row >> 3) & 3) * 4 + (row & 3)
    pick = (inside == lax.broadcasted_iota(jnp.int32, (64, 512), 0)).astype(F32).astype(BF16)
    spread = nn(routes, pick)
    row = lax.broadcasted_iota(jnp.int32, (8, 512), 1)
    place = (row >> 8) + ((row >> 5) & 1) * 2 + ((row >> 2) & 1) * 4
    mine = place == lax.broadcasted_iota(jnp.int32, (8, 512), 0)
    group = jnp.sum(jnp.where(mine, spread, 0.0), axis=0, keepdims=True)
    group_ref[...] = jnp.broadcast_to(group, (8, 512))

    for i, fetch in enumerate(fetches):
        fetch.wait()
        for tap in range(27):
            piece = w_ref[48 * i : 48 * i + 48, tap * CIN : tap * CIN + CIN]
            wp_ref[48 * i : 48 * i + 48, tap * LANES : tap * LANES + CIN] = piece


def shared_out(group, amounts):
    return jnp.concatenate(
        [jnp.where(group == float(g), amounts, 0.0) for g in range(GROUPS)], axis=0
    ).astype(BF16)


def forward_kernel(
    key_hbm, val_hbm, query_hbm, v_ref, xr_ref, yr_ref, bias_ref, wp_ref, group_ref, early_ref,
    podd_ref, peven_ref, slope_ref, hidt_ref, cott_ref, kut_ref, knt_ref, wt_ref, tt_ref, kt_ref,
    vw_ref, send_ref,
    key_ref, val_ref, query_ref, sems,
):
    copies = [
        pltpu.make_async_copy(source, target, sems.at[i])
        for i, (source, target) in enumerate(
            ((key_hbm, key_ref), (val_hbm, val_ref), (query_hbm, query_ref))
        )
    ]
    for copy in copies:
        copy.start()
    here = lax.axis_index("chip") * 2 + lax.axis_index("core")
    inner = jnp.logical_and(here >= 8, lax.rem(here, 8) > 0)
    corner = early_ref[pl.ds(pl.multiple_of(16 * jnp.maximum(here - 9, 0), 16), 16), 256:384]
    corner = jnp.where(inner, corner.astype(F32), 0.0)
    first = lax.broadcasted_iota(jnp.int32, (64, LANES), 0) % 8 == 0
    for x in range(-1, 16):
        if x < 0:
            planes, edge = xr_ref[...].astype(F32).reshape(4, 64, LANES), corner
        else:
            planes, edge = v_ref[x].astype(F32), yr_ref[pl.ds(16 * x, 16), :].astype(F32)
        if x % 2 == 0:
            out_ref, row = peven_ref, 32 * x
        else:
            out_ref, row = podd_ref, 32 * (x + 1)
        for b in range(3):
            for c in range(3):
                py, pz = (b + 1) % 2, (c + 1) % 2
                piece = planes[2 * py + pz]
                if b == 0:
                    piece = jnp.concatenate([edge[8 * pz : 8 * pz + 8], piece[0:56]], axis=0)
                if c == 0:
                    piece = jnp.where(first, 0.0, pltpu.roll(piece, 1, 0))
                column = (3 * b + c) * LANES
                out_ref[pl.ds(row, 64), pl.ds(column, LANES)] = piece.astype(BF16)
    before = (
        nt(podd_ref[0:512, :], wp_ref[:, 0:SLOTS9])
        + nt(peven_ref[...], wp_ref[:, SLOTS9 : 2 * SLOTS9])
        + nt(podd_ref[64:576, :], wp_ref[:, 2 * SLOTS9 : 3 * SLOTS9])
        + bias_ref[...]
    )
    square = before * before
    tanh = jnp.tanh(ROOT * before * (1.0 + CUBIC * square))
    hidden = (0.5 * before * (1.0 + tanh)).astype(BF16)
    slope = 0.5 * (1.0 + tanh) + 0.5 * before * (1.0 - tanh * tanh) * ROOT * (
        1.0 + 3.0 * CUBIC * square
    )
    slope_ref[...] = slope.T
    hidt_ref[...] = hidden.astype(F32).T.astype(BF16)

    for copy in copies:
        copy.wait()
    kh, kl = split(key_ref[...].T)
    vh, vl = split(val_ref[...])
    kt_ref[...] = kh
    vw_ref[...] = vh
    keys = nt(kh, hidden) + nt(kl, hidden)
    values = nn(hidden, vh) + nn(hidden, vl)
    queries = query_ref[...]
    qu = queries * lax.rsqrt(jnp.sum(queries * queries, axis=-1, keepdims=True) + EPS)
    key_norm = lax.rsqrt(jnp.sum(keys * keys, axis=0, keepdims=True) + EPS)
    kut = keys * key_norm
    kut_ref[...] = kut
    knt_ref[...] = jnp.broadcast_to(key_norm, (8, 512))
    weights = jnp.exp(TEMPER * nn(qu.astype(BF16), kut.astype(BF16)))
    wt_ref[...] = weights
    group = group_ref[...]
    shares = shared_out(group, weights)
    vb = values.astype(BF16)
    sums = nn(shares, jnp.concatenate([vb, jnp.ones((512, 64), BF16)], axis=1))
    cot = early_ref[:, 0:COUT]
    cott_ref[...] = cot.astype(F32).T.astype(BF16)
    meets = nt(cot, vb)
    total = jnp.zeros((8, 512), F32)
    for g in range(GROUPS):
        total = total + jnp.where(group == float(g), meets[8 * g : 8 * g + 8], 0.0)
    tt_ref[...] = total
    inner = jnp.sum(sums[:, 0:COUT] * cot.astype(F32), axis=-1, keepdims=True)
    lane = lax.broadcasted_iota(jnp.int32, (8, 64), 1)
    mass = jnp.zeros((8, 64), F32)
    dots = jnp.zeros((8, 64), F32)
    for g in range(GROUPS):
        mass = jnp.where(lane == g, sums[8 * g : 8 * g + 8, COUT:256], mass)
        dots = jnp.where(lane == g, inner[8 * g : 8 * g + 8], dots)
    table = jnp.concatenate([mass, dots], axis=0)
    send_ref[:, 0:COUT] = sums[:, 0:COUT].astype(BF16)
    send_ref[:, COUT:256] = jnp.concatenate([table.astype(BF16)] * 32, axis=0)


def backward_kernel(
    recv_ref, podd_ref, peven_ref, slope_ref, hidt_ref, kut_ref, knt_ref, wt_ref, tt_ref,
    group_ref, cott_ref, kt_ref, vw_ref, query_ref,
    pooled_ref, db_ref, xs_ref, ys_ref, keep_ref, give_ref, sum_ref,
):
    got = jnp.sum(recv_ref[...].reshape(32, 16, 256).astype(F32), axis=0)
    mass = got[0:8, COUT:256]
    dots = got[8:16, COUT:256]
    here = lax.axis_index("chip") * 2 + lax.axis_index("core")
    lane = lax.broadcasted_iota(jnp.int32, (8, 64), 1)
    own = [
        jnp.sum(jnp.where(lane == 2 * here + i, mass, 0.0), axis=-1, keepdims=True)
        for i in range(2)
    ]
    pooled_ref[...] = got[:, 0:COUT] / (1.0 + jnp.concatenate(own, axis=0))

    inverse = 1.0 / (1.0 + mass)
    d_mass = -dots * inverse * inverse
    ih, il = split(inverse)
    mh, ml = split(d_mass)
    group = group_ref[...]
    rows = lax.broadcasted_iota(jnp.int32, (64, 512), 0).astype(F32)
    member = (rows == jnp.broadcast_to(group[0:1], (64, 512))).astype(F32).astype(BF16)
    inv_row = nn(ih, member) + nn(il, member)
    dm_row = nn(mh, member) + nn(ml, member)
    weights = wt_ref[...]
    d_cos = TEMPER * weights * (tt_ref[...] * inv_row + dm_row)
    d_value = nn(cott_ref[...], shared_out(group, weights * inv_row))

    kut = kut_ref[...]
    queries = query_ref[...]
    qn = lax.rsqrt(jnp.sum(queries * queries, axis=-1, keepdims=True) + EPS)
    qu = queries * qn
    ch = d_cos.astype(BF16)
    d_ku = nn(qu.T.astype(BF16), ch)
    d_key = knt_ref[0:1, :] * (d_ku - kut * jnp.sum(kut * d_ku, axis=0, keepdims=True))
    d_qu = nt(ch, kut.astype(BF16))
    d_query = qn * (d_qu - qu * jnp.sum(qu * d_qu, axis=-1, keepdims=True))

    kh, vh = d_key.astype(BF16), d_value.astype(BF16)
    d_hidden = tn(kt_ref[...], kh) + nn(vw_ref[...], vh)
    d_before = d_hidden * slope_ref[...]
    dbt = d_before.astype(BF16)
    d_rows = d_before.T
    db = d_rows.astype(BF16)
    db_ref[...] = db
    xs_ref[...] = db[0:64]
    ys_ref[...] = d_rows.reshape(8, 64, COUT)[:, 0:8].reshape(64, COUT).astype(BF16)

    parts = (podd_ref[0:512, :], peven_ref[...], podd_ref[64:576, :])
    for a in range(3):
        grad = nn(dbt, parts[a])
        for tap in range(9):
            piece = grad[:, tap * LANES : tap * LANES + CIN]
            sum_ref[:, pl.ds((9 * a + tap) * CIN, CIN)] = piece
    sum_ref[:, KDIM : KDIM + COUT] = nt(hidt_ref[...], kh)
    sum_ref[:, KDIM + COUT : KDIM + 2 * COUT] = nt(hidt_ref[...], vh)
    bias = jnp.broadcast_to(jnp.sum(d_rows, axis=0, keepdims=True), (8, COUT))
    small = [d_query[:, 0:CIN], d_query[:, CIN:COUT], bias[:, 0:CIN], bias[:, CIN:COUT]]
    small = jnp.concatenate(small + [jnp.zeros((COUT - 32, CIN), F32)], axis=0)
    sum_ref[:, KDIM + 2 * COUT : WIDE] = small
    low = lax.axis_index("core") == 0
    for t in range(12):
        left = sum_ref[:, LANES * t : LANES * (t + 1)]
        right = sum_ref[:, LANES * (t + 12) : LANES * (t + 13)]
        keep_ref[COUT * t : COUT * (t + 1), :] = jnp.where(low, left, right)
        give_ref[COUT * t : COUT * (t + 1), :] = jnp.where(low, right, left).astype(BF16)


def add_kernel(a_ref, b_ref, out_ref):
    out_ref[0:USED, :] = (a_ref[...] + b_ref[...].astype(F32)).astype(BF16)
    out_ref[USED:HALF, :] = jnp.zeros((HALF - USED, LANES), BF16)


def total_kernel(recv_ref, out_ref):
    total = jnp.sum(recv_ref[...].astype(F32), axis=0).astype(BF16)
    out_ref[...] = jnp.broadcast_to(total[None], out_ref.shape)


def final_kernel(mine_ref, other_ref, dw_ref, dk_ref, dv_ref, dq_ref, dbias_ref, all_ref):
    low = lax.axis_index("core") == 0
    for t in range(12):
        mine = mine_ref[COUT * t : COUT * (t + 1), :].astype(F32)
        other = other_ref[COUT * t : COUT * (t + 1), :].astype(F32)
        all_ref[:, LANES * t : LANES * (t + 1)] = jnp.where(low, mine, other)
        all_ref[:, LANES * (t + 12) : LANES * (t + 13)] = jnp.where(low, other, mine)
    dw_ref[...] = all_ref[:, 0:KDIM]
    dk_ref[...] = all_ref[:, KDIM : KDIM + COUT]
    dv_ref[...] = all_ref[:, KDIM + COUT : KDIM + 2 * COUT]
    small = all_ref[0:32, KDIM + 2 * COUT : WIDE]
    dq_ref[...] = jnp.concatenate([small[0:8], small[8:16]], axis=1)
    dbias_ref[...] = jnp.concatenate([small[16:17], small[24:25]], axis=1)


def spread_kernel(
    near_ref, w_hbm, db_ref, xr_ref, yr_ref, xyr_ref, occ_ref, out_ref,
    ext_ref, even_ref, odd_ref, rows_ref, slot_ref, w_ref, wp_ref, sem,
):
    fetch = pltpu.make_async_copy(w_hbm, w_ref, sem)
    fetch.start()
    wp_ref[...] = jnp.zeros_like(wp_ref)
    find_slots(near_ref, slot_ref)
    edge = yr_ref[...].astype(F32)
    for jx in range(8):
        ext_ref[pl.ds(72 * jx, 64), :] = db_ref[pl.ds(64 * jx, 64), :].astype(F32)
        ext_ref[pl.ds(72 * jx + 64, 8), :] = edge[8 * jx : 8 * jx + 8]
    ext_ref[pl.ds(576, 64), :] = xr_ref[...].astype(F32)
    ext_ref[pl.ds(640, 8), :] = xyr_ref[...].astype(F32)[0:8]
    low = ext_ref[0:576, :].astype(BF16)
    high = ext_ref[72:648, :].astype(BF16)
    fetch.wait()
    for number in range(27):
        wp_ref[:, pl.ds(number * LANES, CIN)] = w_ref[:, pl.ds(number * CIN, CIN)]
    even_ref[...] = nn(low, wp_ref[:, SLOTS9 : 2 * SLOTS9])
    odd_ref[...] = nn(low, wp_ref[:, 2 * SLOTS9 : 3 * SLOTS9]) + nn(high, wp_ref[:, 0:SLOTS9])
    last = lax.broadcasted_iota(jnp.int32, (32, LANES), 0) % 8 == 7

    def up(piece):
        return jnp.where(last, 0.0, pltpu.roll(piece, 31, 0))

    for by in range(2):
        for bx in range(2):
            for xl in range(8):
                x = 8 * bx + xl
                src_ref = even_ref if x % 2 == 0 else odd_ref
                start = 72 * (x // 2) + 32 * by

                def tap(b, c, later, src_ref=src_ref, start=start):
                    return src_ref[pl.ds(start + 8 * later, 32), pl.ds((3 * b + c) * LANES, LANES)]

                e00 = tap(1, 1, 0)
                e01 = tap(1, 2, 0) + up(tap(1, 0, 0))
                e10 = tap(2, 1, 0) + tap(0, 1, 1)
                e11 = tap(2, 2, 0) + tap(0, 2, 1) + up(tap(2, 0, 0) + tap(0, 0, 1))
                for pz, (ye, yo) in enumerate(((e00, e10), (e01, e11))):
                    both = jnp.stack([ye.reshape(4, 8, LANES), yo.reshape(4, 8, LANES)], axis=1)
                    rows_ref[pl.ds(128 * xl + pz, 64, stride=2), :] = both.reshape(64, LANES)
            tile = rows_ref[...].reshape(64, 2, 8, LANES)
            for bz in range(2):
                place = bx + 2 * by + 4 * bz
                slot = slot_ref[place]
                block = tile[:, bz].reshape(512, LANES).T[0:CIN]
                block = jnp.where(occ_ref[pl.ds(slot, 1), :] > 0, block, 0.0)
                out_ref[slot] = block.astype(BF16)


def vm():
    return pl.BlockSpec(memory_space=pltpu.VMEM)


def like(shape, dtype=F32):
    return jax.ShapeDtypeStruct(shape, dtype)


def call(kernel, kinds, outs, scratch, *args):
    spaces = {"s": pltpu.SMEM, "h": pltpu.HBM, "v": pltpu.VMEM}
    kinds = kinds + "v" * (len(args) - len(kinds))
    in_specs = [pl.BlockSpec(memory_space=spaces[kind]) for kind in kinds]
    args = [
        pltpu.with_memory_space_constraint(arg, pltpu.HBM) if kind == "h" else arg
        for arg, kind in zip(args, kinds, strict=True)
    ]
    return pl.pallas_call(
        kernel,
        out_shape=outs,
        in_specs=in_specs,
        out_specs=jax.tree.map(lambda _: vm(), outs),
        scratch_shapes=scratch,
        compiler_params=params(),
        name=kernel.__name__,
    )(*args)


def shift(shard, by_x, by_y):
    pairs = []
    for index in range(32):
        tx, ty = index % 8 + by_x, index // 8 + by_y
        if 0 <= tx < 8 and 0 <= ty < 4:
            pairs.append((index, ty * 8 + tx))
    return lax.ppermute(shard, SPACE, pairs)


def on_device(
    features, occupancy, neighbors, routes, cotangent, conv_weight, conv_bias,
    key_weight, value_weight, queries,
):
    features, occupancy = jnp.swapaxes(features[0], 1, 2), occupancy[0]
    slots = pltpu.SMEM((8,), jnp.int32)
    v, xs, ys, early = call(
        place_kernel, "hhhh",
        [
            like((16, 4, 64, LANES), BF16), like((256, LANES), BF16), like((256, LANES), BF16),
            like((32, 16, 3 * LANES), BF16),
        ],
        [
            pltpu.SMEM((6, 8), jnp.int32), pltpu.VMEM((8, CIN, 512), BF16),
            pltpu.VMEM((8, 512), jnp.int32), pltpu.VMEM((16, COUT), F32),
            pltpu.VMEM((1024, LANES), F32), slots, pltpu.SemaphoreType.DMA((4,)),
        ],
        neighbors, features, occupancy, cotangent.reshape(16, COUT),
    )
    early = lax.all_to_all(early, SPACE, 0, 0, tiled=True).reshape(512, 3 * LANES)
    xr = shift(xs, 1, 0)
    yr = shift(ys, 0, 1)
    wp, group = call(
        prepare_kernel, "sh",
        [
            like((COUT, 27 * LANES), BF16), like((8, 512)),
        ],
        [
            slots, pltpu.VMEM((8, 64), jnp.int32), pltpu.VMEM((COUT, KDIM), BF16),
            pltpu.SemaphoreType.DMA((4,)),
        ],
        neighbors, conv_weight.T, routes.reshape(1, 512),
    )
    podd, peven, slope, hidt, cott, kut, knt, wt, tt, kt, vw, send = call(
        forward_kernel, "hhh",
        [
            like((576, SLOTS9), BF16), like((512, SLOTS9), BF16), like((COUT, 512)),
            like((COUT, 512), BF16), like((COUT, 512), BF16), like((COUT, 512)), like((8, 512)),
            like((8, 512)), like((8, 512)), like((COUT, COUT), BF16),
            like((COUT, COUT), BF16), like((512, 256), BF16),
        ],
        [
            pltpu.VMEM((COUT, COUT), F32), pltpu.VMEM((COUT, COUT), F32),
            pltpu.VMEM((NQ, COUT), F32), pltpu.SemaphoreType.DMA((3,)),
        ],
        key_weight, value_weight, queries, v, xr, yr, conv_bias.reshape(1, COUT), wp, group, early,
    )
    recv = lax.all_to_all(send.reshape(32, 16, 256), SPACE, 0, 0, tiled=True).reshape(512, 256)
    pooled, db, bxs, bys, keep, give = call(
        backward_kernel, "",
        [
            like((16, COUT)), like((512, COUT), BF16), like((64, COUT), BF16),
            like((64, COUT), BF16), like((USED, LANES)), like((USED, LANES), BF16),
        ],
        [pltpu.VMEM((COUT, WIDE), F32)],
        recv, podd, peven, slope, hidt, kut, knt, wt, tt, group, cott, kt, vw, queries,
    )
    swap = [(0, 1), (1, 0)]
    taken = lax.ppermute(give, "core", swap)
    half = call(add_kernel, "", like((HALF, LANES), BF16), [], keep, taken)
    pieces = lax.all_to_all(half.reshape(64, SHARD, LANES), CHIPS, 0, 0, tiled=True)
    bxr = shift(bxs, -1, 0)
    byr = shift(bys, 0, -1)
    bxyr = shift(bys[0:16], -1, -1)
    copies = call(total_kernel, "", like((64, SHARD, LANES), BF16), [], pieces)
    bxr, byr, bxyr, copies = lax.optimization_barrier((bxr, byr, bxyr, copies))
    mine = lax.all_to_all(copies, CHIPS, 0, 0, tiled=True).reshape(HALF, LANES)
    d_features = call(
        spread_kernel, "sh", like((8, CIN, 512), BF16),
        [
            pltpu.VMEM((648, COUT), F32), pltpu.VMEM((576, SLOTS9), F32),
            pltpu.VMEM((576, SLOTS9), F32), pltpu.VMEM((1024, LANES), F32), slots,
            pltpu.VMEM((COUT, KDIM), BF16), pltpu.VMEM((COUT, 27 * LANES), BF16),
            pltpu.SemaphoreType.DMA,
        ],
        neighbors, conv_weight.T, db, bxr, byr, bxyr, occupancy,
    )
    mine, d_features = lax.optimization_barrier((mine, d_features))
    other = lax.ppermute(mine, "core", swap)
    d_weight, d_key, d_value, d_query, d_bias = call(
        final_kernel, "",
        [
            like((COUT, KDIM)), like((COUT, COUT)), like((COUT, COUT)), like((NQ, COUT)),
            like((1, COUT)),
        ],
        [pltpu.VMEM((COUT, WIDE), F32)],
        mine, other,
    )
    return (
        pooled.reshape(1, 2, NQ, COUT), jnp.swapaxes(d_features, 1, 2)[None], d_weight.T,
        d_bias.reshape(COUT), d_key, d_value, d_query,
    )


def solution(mesh):
    fine = Mesh(mesh.devices.reshape(4, 16, 2), ("section", "chip", "core"))
    in_specs = (
        P("section", SPACE, None, None),
        P("section", SPACE, None),
        P(None, SPACE),
        P("section", SPACE, None),
        P("section", SPACE, None, None),
        P(),
        P(),
        P(),
        P(),
        P(),
    )
    out_specs = (
        P("section", SPACE, None, None),
        P("section", SPACE, None, None),
        P(),
        P(),
        P(),
        P(),
        P(),
    )
    return jax.shard_map(
        on_device, mesh=fine, in_specs=in_specs, out_specs=out_specs, check_vma=False
    )
```

```python
import functools

import jax
import jax.numpy as jnp
from jax import lax
from jax.experimental import pallas as pl
from jax.experimental.pallas import tpu as pltpu
from jax.sharding import Mesh, PartitionSpec as P

EPS = 1e-06
TEMPER = 8.0
CIN, COUT = 96, 192
LANES = 128
SLOTS9 = 9 * LANES
GROUPS, NQ = 64, 8
KDIM = 27 * CIN
SHARD = 40
HALF = 64 * SHARD
USED = 12 * COUT
WIDE = 24 * LANES
F32, BF16 = jnp.float32, jnp.bfloat16
SPACE = ("chip", "core")
CHIPS = ("section", "chip")
ROOT, CUBIC = 0.7978845608028654, 0.044715
VMEM_LIMIT = 44 * 1024 * 1024


def params():
    return pltpu.CompilerParams(vmem_limit_bytes=VMEM_LIMIT)


def nn(a, b):
    return lax.dot_general(a, b, (((1,), (0,)), ((), ())), preferred_element_type=F32)


def nt(a, b):
    return lax.dot_general(a, b, (((1,), (1,)), ((), ())), preferred_element_type=F32)


def tn(a, b):
    return lax.dot_general(a, b, (((0,), (0,)), ((), ())), preferred_element_type=F32)


def split(a):
    high = a.astype(BF16)
    return high, (a - high.astype(F32)).astype(BF16)


def find_slots(near_ref, slot_ref):
    here = lax.axis_index("chip") * 2 + lax.axis_index("core")
    for place in range(8):
        slot_ref[place] = 0
    for slot in range(8):
        place = 0
        for axis in range(3):
            beside = near_ref[axis, slot]
            inner = jnp.logical_and(beside >= 0, lax.shift_right_arithmetic(beside, 3) == here)
            place = place + jnp.where(inner, 0, 1 << axis)
        slot_ref[place] = slot


def place_kernel(
    near_hbm, feat_hbm, occ_hbm, cot_hbm, v_ref, xs_ref, ys_ref, early_ref,
    near_ref, feat_ref, occ_ref, cot_ref, rows_ref, slot_ref, sems,
):
    copies = [
        pltpu.make_async_copy(source, target, sems.at[i])
        for i, (source, target) in enumerate(
            (
                (near_hbm, near_ref), (feat_hbm, feat_ref), (occ_hbm, occ_ref), (cot_hbm, cot_ref),
            )
        )
    ]
    for copy in copies:
        copy.start()
    rows_ref[...] = jnp.zeros_like(rows_ref)
    for copy in copies:
        copy.wait()
    find_slots(near_ref, slot_ref)
    for by in range(2):
        for bx in range(2):
            pair = []
            for bz in range(2):
                place = bx + 2 * by + 4 * bz
                slot = slot_ref[place]
                block = feat_ref[slot].astype(F32)
                block = jnp.where(occ_ref[pl.ds(slot, 1), :] > 0, block, 0.0).T
                pair.append(block.reshape(64, 8, CIN))
            rows_ref[:, 0:CIN] = jnp.stack(pair, axis=1).reshape(1024, CIN)
            for pz in range(2):
                part = rows_ref[pl.ds(pz, 512, stride=2), :].reshape(8, 4, 2, 8, LANES)
                for py in range(2):
                    piece = part[:, :, py].reshape(8, 32, LANES).astype(BF16)
                    v_ref[pl.ds(8 * bx, 8), 2 * py + pz, pl.ds(32 * by, 32), :] = piece
            if by == 1:
                edge = [
                    rows_ref[pl.ds(pz, 512, stride=2), :].reshape(8, 8, 8, LANES)[:, 7]
                    for pz in range(2)
                ]
                ys_ref[pl.ds(128 * bx, 128), :] = (
                    jnp.stack(edge, axis=1).reshape(128, LANES).astype(BF16)
                )
    xs_ref[...] = v_ref[15].reshape(256, LANES)
    early = jnp.concatenate(
        [cot_ref[...].astype(BF16), jnp.zeros((16, 64), BF16), ys_ref[240:256, :]], axis=1
    )
    early_ref[...] = jnp.broadcast_to(early[None], early_ref.shape)


def prepare_kernel(
    near_ref, w_hbm, routes_ref,
    wp_ref, group_ref,
    slot_ref, routes8_ref, w_ref, sems,
):
    fetches = [
        pltpu.make_async_copy(w_hbm.at[pl.ds(48 * i, 48)], w_ref.at[pl.ds(48 * i, 48)], sems.at[i])
        for i in range(4)
    ]
    for fetch in fetches:
        fetch.start()
    find_slots(near_ref, slot_ref)
    wp_ref[...] = jnp.zeros_like(wp_ref)
    for slot in range(8):
        routes8_ref[slot : slot + 1, :] = routes_ref[:, 64 * slot : 64 * slot + 64]
    routes = jnp.concatenate(
        [routes8_ref[pl.ds(slot_ref[p], 1), :] for p in range(8)], axis=0
    ).astype(BF16)
    row = lax.broadcasted_iota(jnp.int32, (64, 512), 1)
    inside = ((row >> 6) & 3) * 16 + ((row >> 3) & 3) * 4 + (row & 3)
    pick = (inside == lax.broadcasted_iota(jnp.int32, (64, 512), 0)).astype(F32).astype(BF16)
    spread = nn(routes, pick)
    row = lax.broadcasted_iota(jnp.int32, (8, 512), 1)
    place = (row >> 8) + ((row >> 5) & 1) * 2 + ((row >> 2) & 1) * 4
    mine = place == lax.broadcasted_iota(jnp.int32, (8, 512), 0)
    group = jnp.sum(jnp.where(mine, spread, 0.0), axis=0, keepdims=True)
    group_ref[...] = jnp.broadcast_to(group, (8, 512))

    for i, fetch in enumerate(fetches):
        fetch.wait()
        for tap in range(27):
            piece = w_ref[48 * i : 48 * i + 48, tap * CIN : tap * CIN + CIN]
            wp_ref[48 * i : 48 * i + 48, tap * LANES : tap * LANES + CIN] = piece


def shared_out(group, amounts):
    return jnp.concatenate(
        [jnp.where(group == float(g), amounts, 0.0) for g in range(GROUPS)], axis=0
    ).astype(BF16)


def forward_kernel(
    key_hbm, val_hbm, query_hbm, v_ref, xr_ref, yr_ref, bias_ref, wp_ref, group_ref, early_ref,
    podd_ref, peven_ref, slope_ref, hidt_ref, cott_ref, kut_ref, knt_ref, wt_ref, tt_ref, kt_ref,
    vw_ref, send_ref,
    key_ref, val_ref, query_ref, sems,
):
    copies = [
        pltpu.make_async_copy(source, target, sems.at[i])
        for i, (source, target) in enumerate(
            ((key_hbm, key_ref), (val_hbm, val_ref), (query_hbm, query_ref))
        )
    ]
    for copy in copies:
        copy.start()
    here = lax.axis_index("chip") * 2 + lax.axis_index("core")
    inner = jnp.logical_and(here >= 8, lax.rem(here, 8) > 0)
    corner = early_ref[pl.ds(pl.multiple_of(16 * jnp.maximum(here - 9, 0), 16), 16), 256:384]
    corner = jnp.where(inner, corner.astype(F32), 0.0)
    first = lax.broadcasted_iota(jnp.int32, (64, LANES), 0) % 8 == 0
    for x in range(-1, 16):
        if x < 0:
            planes, edge = xr_ref[...].astype(F32).reshape(4, 64, LANES), corner
        else:
            planes, edge = v_ref[x].astype(F32), yr_ref[pl.ds(16 * x, 16), :].astype(F32)
        if x % 2 == 0:
            out_ref, row = peven_ref, 32 * x
        else:
            out_ref, row = podd_ref, 32 * (x + 1)
        for b in range(3):
            for c in range(3):
                py, pz = (b + 1) % 2, (c + 1) % 2
                piece = planes[2 * py + pz]
                if b == 0:
                    piece = jnp.concatenate([edge[8 * pz : 8 * pz + 8], piece[0:56]], axis=0)
                if c == 0:
                    piece = jnp.where(first, 0.0, pltpu.roll(piece, 1, 0))
                column = (3 * b + c) * LANES
                out_ref[pl.ds(row, 64), pl.ds(column, LANES)] = piece.astype(BF16)
    before = (
        nt(podd_ref[0:512, :], wp_ref[:, 0:SLOTS9])
        + nt(peven_ref[...], wp_ref[:, SLOTS9 : 2 * SLOTS9])
        + nt(podd_ref[64:576, :], wp_ref[:, 2 * SLOTS9 : 3 * SLOTS9])
        + bias_ref[...]
    )
    square = before * before
    tanh = jnp.tanh(ROOT * before * (1.0 + CUBIC * square))
    hidden = (0.5 * before * (1.0 + tanh)).astype(BF16)
    slope = 0.5 * (1.0 + tanh) + 0.5 * before * (1.0 - tanh * tanh) * ROOT * (
        1.0 + 3.0 * CUBIC * square
    )
    slope_ref[...] = slope.T
    hidt_ref[...] = hidden.astype(F32).T.astype(BF16)

    for copy in copies:
        copy.wait()
    kh, kl = split(key_ref[...].T)
    vh, vl = split(val_ref[...])
    kt_ref[...] = kh
    vw_ref[...] = vh
    keys = nt(kh, hidden) + nt(kl, hidden)
    values = nn(hidden, vh) + nn(hidden, vl)
    queries = query_ref[...]
    qu = queries * lax.rsqrt(jnp.sum(queries * queries, axis=-1, keepdims=True) + EPS)
    key_norm = lax.rsqrt(jnp.sum(keys * keys, axis=0, keepdims=True) + EPS)
    kut = keys * key_norm
    kut_ref[...] = kut
    knt_ref[...] = jnp.broadcast_to(key_norm, (8, 512))
    weights = jnp.exp(TEMPER * nn(qu.astype(BF16), kut.astype(BF16)))
    wt_ref[...] = weights
    group = group_ref[...]
    shares = shared_out(group, weights)
    vb = values.astype(BF16)
    sums = nn(shares, jnp.concatenate([vb, jnp.ones((512, 64), BF16)], axis=1))
    cot = early_ref[:, 0:COUT]
    cott_ref[...] = cot.astype(F32).T.astype(BF16)
    meets = nt(cot, vb)
    total = jnp.zeros((8, 512), F32)
    for g in range(GROUPS):
        total = total + jnp.where(group == float(g), meets[8 * g : 8 * g + 8], 0.0)
    tt_ref[...] = total
    inner = jnp.sum(sums[:, 0:COUT] * cot.astype(F32), axis=-1, keepdims=True)
    lane = lax.broadcasted_iota(jnp.int32, (8, 64), 1)
    mass = jnp.zeros((8, 64), F32)
    dots = jnp.zeros((8, 64), F32)
    for g in range(GROUPS):
        mass = jnp.where(lane == g, sums[8 * g : 8 * g + 8, COUT:256], mass)
        dots = jnp.where(lane == g, inner[8 * g : 8 * g + 8], dots)
    table = jnp.concatenate([mass, dots], axis=0)
    send_ref[:, 0:COUT] = sums[:, 0:COUT].astype(BF16)
    send_ref[:, COUT:256] = jnp.concatenate([table.astype(BF16)] * 32, axis=0)


def backward_kernel(
    recv_ref, podd_ref, peven_ref, slope_ref, hidt_ref, kut_ref, knt_ref, wt_ref, tt_ref,
    group_ref, cott_ref, kt_ref, vw_ref, query_ref,
    pooled_ref, db_ref, xs_ref, ys_ref, keep_ref, give_ref, sum_ref,
):
    got = jnp.sum(recv_ref[...].reshape(32, 16, 256).astype(F32), axis=0)
    mass = got[0:8, COUT:256]
    dots = got[8:16, COUT:256]
    here = lax.axis_index("chip") * 2 + lax.axis_index("core")
    lane = lax.broadcasted_iota(jnp.int32, (8, 64), 1)
    own = [
        jnp.sum(jnp.where(lane == 2 * here + i, mass, 0.0), axis=-1, keepdims=True)
        for i in range(2)
    ]
    pooled_ref[...] = got[:, 0:COUT] / (1.0 + jnp.concatenate(own, axis=0))

    inverse = 1.0 / (1.0 + mass)
    d_mass = -dots * inverse * inverse
    ih, il = split(inverse)
    mh, ml = split(d_mass)
    group = group_ref[...]
    rows = lax.broadcasted_iota(jnp.int32, (64, 512), 0).astype(F32)
    member = (rows == jnp.broadcast_to(group[0:1], (64, 512))).astype(F32).astype(BF16)
    inv_row = nn(ih, member) + nn(il, member)
    dm_row = nn(mh, member) + nn(ml, member)
    weights = wt_ref[...]
    d_cos = TEMPER * weights * (tt_ref[...] * inv_row + dm_row)
    d_value = nn(cott_ref[...], shared_out(group, weights * inv_row))

    kut = kut_ref[...]
    queries = query_ref[...]
    qn = lax.rsqrt(jnp.sum(queries * queries, axis=-1, keepdims=True) + EPS)
    qu = queries * qn
    ch = d_cos.astype(BF16)
    d_ku = nn(qu.T.astype(BF16), ch)
    d_key = knt_ref[0:1, :] * (d_ku - kut * jnp.sum(kut * d_ku, axis=0, keepdims=True))
    d_qu = nt(ch, kut.astype(BF16))
    d_query = qn * (d_qu - qu * jnp.sum(qu * d_qu, axis=-1, keepdims=True))

    kh, vh = d_key.astype(BF16), d_value.astype(BF16)
    d_hidden = tn(kt_ref[...], kh) + nn(vw_ref[...], vh)
    d_before = d_hidden * slope_ref[...]
    dbt = d_before.astype(BF16)
    d_rows = d_before.T
    db = d_rows.astype(BF16)
    db_ref[...] = db
    xs_ref[...] = db[0:64]
    ys_ref[...] = d_rows.reshape(8, 64, COUT)[:, 0:8].reshape(64, COUT).astype(BF16)

    parts = (podd_ref[0:512, :], peven_ref[...], podd_ref[64:576, :])
    for a in range(3):
        grad = nn(dbt, parts[a])
        for tap in range(9):
            piece = grad[:, tap * LANES : tap * LANES + CIN]
            sum_ref[:, pl.ds((9 * a + tap) * CIN, CIN)] = piece
    sum_ref[:, KDIM : KDIM + COUT] = nt(hidt_ref[...], kh)
    sum_ref[:, KDIM + COUT : KDIM + 2 * COUT] = nt(hidt_ref[...], vh)
    bias = jnp.broadcast_to(jnp.sum(d_rows, axis=0, keepdims=True), (8, COUT))
    small = [d_query[:, 0:CIN], d_query[:, CIN:COUT], bias[:, 0:CIN], bias[:, CIN:COUT]]
    small = jnp.concatenate(small + [jnp.zeros((COUT - 32, CIN), F32)], axis=0)
    sum_ref[:, KDIM + 2 * COUT : WIDE] = small
    low = lax.axis_index("core") == 0
    for t in range(12):
        left = sum_ref[:, LANES * t : LANES * (t + 1)]
        right = sum_ref[:, LANES * (t + 12) : LANES * (t + 13)]
        keep_ref[COUT * t : COUT * (t + 1), :] = jnp.where(low, left, right)
        give_ref[COUT * t : COUT * (t + 1), :] = jnp.where(low, right, left).astype(BF16)


def add_kernel(a_ref, b_ref, out_ref):
    out_ref[0:USED, :] = (a_ref[...] + b_ref[...].astype(F32)).astype(BF16)
    out_ref[USED:HALF, :] = jnp.zeros((HALF - USED, LANES), BF16)


def total_kernel(recv_ref, out_ref):
    total = jnp.sum(recv_ref[...].astype(F32), axis=0).astype(BF16)
    out_ref[...] = jnp.broadcast_to(total[None], out_ref.shape)


def final_kernel(mine_ref, other_ref, dw_ref, dk_ref, dv_ref, dq_ref, dbias_ref, all_ref):
    low = lax.axis_index("core") == 0
    for t in range(12):
        mine = mine_ref[COUT * t : COUT * (t + 1), :].astype(F32)
        other = other_ref[COUT * t : COUT * (t + 1), :].astype(F32)
        all_ref[:, LANES * t : LANES * (t + 1)] = jnp.where(low, mine, other)
        all_ref[:, LANES * (t + 12) : LANES * (t + 13)] = jnp.where(low, other, mine)
    dw_ref[...] = all_ref[:, 0:KDIM]
    dk_ref[...] = all_ref[:, KDIM : KDIM + COUT]
    dv_ref[...] = all_ref[:, KDIM + COUT : KDIM + 2 * COUT]
    small = all_ref[0:32, KDIM + 2 * COUT : WIDE]
    dq_ref[...] = jnp.concatenate([small[0:8], small[8:16]], axis=1)
    dbias_ref[...] = jnp.concatenate([small[16:17], small[24:25]], axis=1)


def spread_kernel(
    near_ref, w_hbm, db_ref, xr_ref, yr_ref, xyr_ref, occ_ref, out_ref,
    ext_ref, even_ref, odd_ref, rows_ref, slot_ref, w_ref, wp_ref, sem,
):
    fetch = pltpu.make_async_copy(w_hbm, w_ref, sem)
    fetch.start()
    wp_ref[...] = jnp.zeros_like(wp_ref)
    find_slots(near_ref, slot_ref)
    edge = yr_ref[...].astype(F32)
    for jx in range(8):
        ext_ref[pl.ds(72 * jx, 64), :] = db_ref[pl.ds(64 * jx, 64), :].astype(F32)
        ext_ref[pl.ds(72 * jx + 64, 8), :] = edge[8 * jx : 8 * jx + 8]
    ext_ref[pl.ds(576, 64), :] = xr_ref[...].astype(F32)
    ext_ref[pl.ds(640, 8), :] = xyr_ref[...].astype(F32)[0:8]
    low = ext_ref[0:576, :].astype(BF16)
    high = ext_ref[72:648, :].astype(BF16)
    fetch.wait()
    for number in range(27):
        wp_ref[:, pl.ds(number * LANES, CIN)] = w_ref[:, pl.ds(number * CIN, CIN)]
    even_ref[...] = nn(low, wp_ref[:, SLOTS9 : 2 * SLOTS9])
    odd_ref[...] = nn(low, wp_ref[:, 2 * SLOTS9 : 3 * SLOTS9]) + nn(high, wp_ref[:, 0:SLOTS9])
    last = lax.broadcasted_iota(jnp.int32, (32, LANES), 0) % 8 == 7

    def up(piece):
        return jnp.where(last, 0.0, pltpu.roll(piece, 31, 0))

    for by in range(2):
        for bx in range(2):
            for xl in range(8):
                x = 8 * bx + xl
                src_ref = even_ref if x % 2 == 0 else odd_ref
                start = 72 * (x // 2) + 32 * by

                def tap(b, c, later, src_ref=src_ref, start=start):
                    return src_ref[pl.ds(start + 8 * later, 32), pl.ds((3 * b + c) * LANES, LANES)]

                e00 = tap(1, 1, 0)
                e01 = tap(1, 2, 0) + up(tap(1, 0, 0))
                e10 = tap(2, 1, 0) + tap(0, 1, 1)
                e11 = tap(2, 2, 0) + tap(0, 2, 1) + up(tap(2, 0, 0) + tap(0, 0, 1))
                for pz, (ye, yo) in enumerate(((e00, e10), (e01, e11))):
                    both = jnp.stack([ye.reshape(4, 8, LANES), yo.reshape(4, 8, LANES)], axis=1)
                    rows_ref[pl.ds(128 * xl + pz, 64, stride=2), :] = both.reshape(64, LANES)
            tile = rows_ref[...].reshape(64, 2, 8, LANES)
            for bz in range(2):
                place = bx + 2 * by + 4 * bz
                slot = slot_ref[place]
                block = tile[:, bz].reshape(512, LANES).T[0:CIN]
                block = jnp.where(occ_ref[pl.ds(slot, 1), :] > 0, block, 0.0)
                out_ref[slot] = block.astype(BF16)


def vm():
    return pl.BlockSpec(memory_space=pltpu.VMEM)


def like(shape, dtype=F32):
    return jax.ShapeDtypeStruct(shape, dtype)


def call(kernel, kinds, outs, scratch, *args):
    spaces = {"s": pltpu.SMEM, "h": pltpu.HBM, "v": pltpu.VMEM}
    kinds = kinds + "v" * (len(args) - len(kinds))
    in_specs = [pl.BlockSpec(memory_space=spaces[kind]) for kind in kinds]
    args = [
        pltpu.with_memory_space_constraint(arg, pltpu.HBM) if kind == "h" else arg
        for arg, kind in zip(args, kinds, strict=True)
    ]
    return pl.pallas_call(
        kernel,
        out_shape=outs,
        in_specs=in_specs,
        out_specs=jax.tree.map(lambda _: vm(), outs),
        scratch_shapes=scratch,
        compiler_params=params(),
        name=kernel.__name__,
    )(*args)


def shift(shard, by_x, by_y):
    pairs = []
    for index in range(32):
        tx, ty = index % 8 + by_x, index // 8 + by_y
        if 0 <= tx < 8 and 0 <= ty < 4:
            pairs.append((index, ty * 8 + tx))
    return lax.ppermute(shard, SPACE, pairs)


def on_device(
    features, occupancy, neighbors, routes, cotangent, conv_weight, conv_bias,
    key_weight, value_weight, queries,
):
    features, occupancy = jnp.swapaxes(features[0], 1, 2), occupancy[0]
    slots = pltpu.SMEM((8,), jnp.int32)
    v, xs, ys, early = call(
        place_kernel, "hhhh",
        [
            like((16, 4, 64, LANES), BF16), like((256, LANES), BF16), like((256, LANES), BF16),
            like((32, 16, 3 * LANES), BF16),
        ],
        [
            pltpu.SMEM((6, 8), jnp.int32), pltpu.VMEM((8, CIN, 512), BF16),
            pltpu.VMEM((8, 512), jnp.int32), pltpu.VMEM((16, COUT), F32),
            pltpu.VMEM((1024, LANES), F32), slots, pltpu.SemaphoreType.DMA((4,)),
        ],
        neighbors, features, occupancy, cotangent.reshape(16, COUT),
    )
    early = lax.all_to_all(early, SPACE, 0, 0, tiled=True).reshape(512, 3 * LANES)
    xr = shift(xs, 1, 0)
    yr = shift(ys, 0, 1)
    wp, group = call(
        prepare_kernel, "sh",
        [
            like((COUT, 27 * LANES), BF16), like((8, 512)),
        ],
        [
            slots, pltpu.VMEM((8, 64), jnp.int32), pltpu.VMEM((COUT, KDIM), BF16),
            pltpu.SemaphoreType.DMA((4,)),
        ],
        neighbors, conv_weight.T, routes.reshape(1, 512),
    )
    podd, peven, slope, hidt, cott, kut, knt, wt, tt, kt, vw, send = call(
        forward_kernel, "hhh",
        [
            like((576, SLOTS9), BF16), like((512, SLOTS9), BF16), like((COUT, 512)),
            like((COUT, 512), BF16), like((COUT, 512), BF16), like((COUT, 512)), like((8, 512)),
            like((8, 512)), like((8, 512)), like((COUT, COUT), BF16),
            like((COUT, COUT), BF16), like((512, 256), BF16),
        ],
        [
            pltpu.VMEM((COUT, COUT), F32), pltpu.VMEM((COUT, COUT), F32),
            pltpu.VMEM((NQ, COUT), F32), pltpu.SemaphoreType.DMA((3,)),
        ],
        key_weight, value_weight, queries, v, xr, yr, conv_bias.reshape(1, COUT), wp, group, early,
    )
    recv = lax.all_to_all(send.reshape(32, 16, 256), SPACE, 0, 0, tiled=True).reshape(512, 256)
    pooled, db, bxs, bys, keep, give = call(
        backward_kernel, "",
        [
            like((16, COUT)), like((512, COUT), BF16), like((64, COUT), BF16),
            like((64, COUT), BF16), like((USED, LANES)), like((USED, LANES), BF16),
        ],
        [pltpu.VMEM((COUT, WIDE), F32)],
        recv, podd, peven, slope, hidt, kut, knt, wt, tt, group, cott, kt, vw, queries,
    )
    swap = [(0, 1), (1, 0)]
    taken = lax.ppermute(give, "core", swap)
    half = call(add_kernel, "", like((HALF, LANES), BF16), [], keep, taken)
    pieces = lax.all_to_all(half.reshape(64, SHARD, LANES), CHIPS, 0, 0, tiled=True)
    bxr = shift(bxs, -1, 0)
    byr = shift(bys, 0, -1)
    bxyr = shift(bys[0:16], -1, -1)
    copies = call(total_kernel, "", like((64, SHARD, LANES), BF16), [], pieces)
    db, bxr, byr, copies = lax.optimization_barrier((db, bxr, byr, copies))
    mine = lax.all_to_all(copies, CHIPS, 0, 0, tiled=True).reshape(HALF, LANES)
    d_features = call(
        spread_kernel, "sh", like((8, CIN, 512), BF16),
        [
            pltpu.VMEM((648, COUT), F32), pltpu.VMEM((576, SLOTS9), F32),
            pltpu.VMEM((576, SLOTS9), F32), pltpu.VMEM((1024, LANES), F32), slots,
            pltpu.VMEM((COUT, KDIM), BF16), pltpu.VMEM((COUT, 27 * LANES), BF16),
            pltpu.SemaphoreType.DMA,
        ],
        neighbors, conv_weight.T, db, bxr, byr, bxyr, occupancy,
    )
    mine, d_features = lax.optimization_barrier((mine, d_features))
    other = lax.ppermute(mine, "core", swap)
    d_weight, d_key, d_value, d_query, d_bias = call(
        final_kernel, "",
        [
            like((COUT, KDIM)), like((COUT, COUT)), like((COUT, COUT)), like((NQ, COUT)),
            like((1, COUT)),
        ],
        [pltpu.VMEM((COUT, WIDE), F32)],
        mine, other,
    )
    return (
        pooled.reshape(1, 2, NQ, COUT), jnp.swapaxes(d_features, 1, 2)[None], d_weight.T,
        d_bias.reshape(COUT), d_key, d_value, d_query,
    )


def solution(mesh):
    fine = Mesh(mesh.devices.reshape(4, 16, 2), ("section", "chip", "core"))
    in_specs = (
        P("section", SPACE, None, None),
        P("section", SPACE, None),
        P(None, SPACE),
        P("section", SPACE, None),
        P("section", SPACE, None, None),
        P(),
        P(),
        P(),
        P(),
        P(),
    )
    out_specs = (
        P("section", SPACE, None, None),
        P("section", SPACE, None, None),
        P(),
        P(),
        P(),
        P(),
        P(),
    )
    return jax.shard_map(
        on_device, mesh=fine, in_specs=in_specs, out_specs=out_specs, check_vma=False
    )
```

```python
import functools

import jax
import jax.numpy as jnp
from jax import lax
from jax.experimental import pallas as pl
from jax.experimental.pallas import tpu as pltpu
from jax.sharding import Mesh, PartitionSpec as P

EPS = 1e-06
TEMPER = 8.0
CIN, COUT = 96, 192
LANES = 128
SLOTS9 = 9 * LANES
GROUPS, NQ = 64, 8
KDIM = 27 * CIN
SHARD = 40
HALF = 64 * SHARD
USED = 12 * COUT
WIDE = 24 * LANES
F32, BF16 = jnp.float32, jnp.bfloat16
SPACE = ("chip", "core")
CHIPS = ("section", "chip")
ROOT, CUBIC = 0.7978845608028654, 0.044715
VMEM_LIMIT = 44 * 1024 * 1024


def params():
    return pltpu.CompilerParams(vmem_limit_bytes=VMEM_LIMIT)


def nn(a, b):
    return lax.dot_general(a, b, (((1,), (0,)), ((), ())), preferred_element_type=F32)


def nt(a, b):
    return lax.dot_general(a, b, (((1,), (1,)), ((), ())), preferred_element_type=F32)


def tn(a, b):
    return lax.dot_general(a, b, (((0,), (0,)), ((), ())), preferred_element_type=F32)


def split(a):
    high = a.astype(BF16)
    return high, (a - high.astype(F32)).astype(BF16)


def find_slots(near_ref, slot_ref):
    here = lax.axis_index("chip") * 2 + lax.axis_index("core")
    for place in range(8):
        slot_ref[place] = 0
    for slot in range(8):
        place = 0
        for axis in range(3):
            beside = near_ref[axis, slot]
            inner = jnp.logical_and(beside >= 0, lax.shift_right_arithmetic(beside, 3) == here)
            place = place + jnp.where(inner, 0, 1 << axis)
        slot_ref[place] = slot


def place_kernel(
    near_hbm, feat_hbm, occ_hbm, cot_hbm, v_ref, xs_ref, ys_ref, early_ref,
    near_ref, feat_ref, occ_ref, cot_ref, rows_ref, slot_ref, sems,
):
    copies = [
        pltpu.make_async_copy(source, target, sems.at[i])
        for i, (source, target) in enumerate(
            (
                (near_hbm, near_ref), (feat_hbm, feat_ref), (occ_hbm, occ_ref), (cot_hbm, cot_ref),
            )
        )
    ]
    for copy in copies:
        copy.start()
    rows_ref[...] = jnp.zeros_like(rows_ref)
    for copy in copies:
        copy.wait()
    find_slots(near_ref, slot_ref)
    for by in range(2):
        for bx in range(2):
            pair = []
            for bz in range(2):
                place = bx + 2 * by + 4 * bz
                slot = slot_ref[place]
                block = feat_ref[slot].astype(F32)
                block = jnp.where(occ_ref[pl.ds(slot, 1), :] > 0, block, 0.0).T
                pair.append(block.reshape(64, 8, CIN))
            rows_ref[:, 0:CIN] = jnp.stack(pair, axis=1).reshape(1024, CIN)
            for pz in range(2):
                part = rows_ref[pl.ds(pz, 512, stride=2), :].reshape(8, 4, 2, 8, LANES)
                for py in range(2):
                    piece = part[:, :, py].reshape(8, 32, LANES).astype(BF16)
                    v_ref[pl.ds(8 * bx, 8), 2 * py + pz, pl.ds(32 * by, 32), :] = piece
            if by == 1:
                edge = [
                    rows_ref[pl.ds(pz, 512, stride=2), :].reshape(8, 8, 8, LANES)[:, 7]
                    for pz in range(2)
                ]
                ys_ref[pl.ds(128 * bx, 128), :] = (
                    jnp.stack(edge, axis=1).reshape(128, LANES).astype(BF16)
                )
    xs_ref[...] = v_ref[15].reshape(256, LANES)
    early = jnp.concatenate(
        [cot_ref[...].astype(BF16), jnp.zeros((16, 64), BF16), ys_ref[240:256, :]], axis=1
    )
    early_ref[...] = jnp.broadcast_to(early[None], early_ref.shape)


def prepare_kernel(
    near_ref, w_hbm, routes_ref,
    wp_ref, group_ref,
    slot_ref, routes8_ref, w_ref, sems,
):
    fetches = [
        pltpu.make_async_copy(w_hbm.at[pl.ds(48 * i, 48)], w_ref.at[pl.ds(48 * i, 48)], sems.at[i])
        for i in range(4)
    ]
    for fetch in fetches:
        fetch.start()
    find_slots(near_ref, slot_ref)
    wp_ref[...] = jnp.zeros_like(wp_ref)
    for slot in range(8):
        routes8_ref[slot : slot + 1, :] = routes_ref[:, 64 * slot : 64 * slot + 64]
    routes = jnp.concatenate(
        [routes8_ref[pl.ds(slot_ref[p], 1), :] for p in range(8)], axis=0
    ).astype(BF16)
    row = lax.broadcasted_iota(jnp.int32, (64, 512), 1)
    inside = ((row >> 6) & 3) * 16 + ((row >> 3) & 3) * 4 + (row & 3)
    pick = (inside == lax.broadcasted_iota(jnp.int32, (64, 512), 0)).astype(F32).astype(BF16)
    spread = nn(routes, pick)
    row = lax.broadcasted_iota(jnp.int32, (8, 512), 1)
    place = (row >> 8) + ((row >> 5) & 1) * 2 + ((row >> 2) & 1) * 4
    mine = place == lax.broadcasted_iota(jnp.int32, (8, 512), 0)
    group = jnp.sum(jnp.where(mine, spread, 0.0), axis=0, keepdims=True)
    group_ref[...] = jnp.broadcast_to(group, (8, 512))

    for i, fetch in enumerate(fetches):
        fetch.wait()
        for tap in range(27):
            piece = w_ref[48 * i : 48 * i + 48, tap * CIN : tap * CIN + CIN]
            wp_ref[48 * i : 48 * i + 48, tap * LANES : tap * LANES + CIN] = piece


def shared_out(group, amounts):
    return jnp.concatenate(
        [jnp.where(group == float(g), amounts, 0.0) for g in range(GROUPS)], axis=0
    ).astype(BF16)


def forward_kernel(
    key_hbm, val_hbm, query_hbm, v_ref, xr_ref, yr_ref, bias_ref, wp_ref, group_ref, early_ref,
    podd_ref, peven_ref, slope_ref, hidt_ref, cott_ref, kut_ref, knt_ref, wt_ref, tt_ref, kt_ref,
    vw_ref, send_ref,
    key_ref, val_ref, query_ref, sems,
):
    copies = [
        pltpu.make_async_copy(source, target, sems.at[i])
        for i, (source, target) in enumerate(
            ((key_hbm, key_ref), (val_hbm, val_ref), (query_hbm, query_ref))
        )
    ]
    for copy in copies:
        copy.start()
    here = lax.axis_index("chip") * 2 + lax.axis_index("core")
    inner = jnp.logical_and(here >= 8, lax.rem(here, 8) > 0)
    corner = early_ref[pl.ds(pl.multiple_of(16 * jnp.maximum(here - 9, 0), 16), 16), 256:384]
    corner = jnp.where(inner, corner.astype(F32), 0.0)
    first = lax.broadcasted_iota(jnp.int32, (64, LANES), 0) % 8 == 0
    for x in range(-1, 16):
        if x < 0:
            planes, edge = xr_ref[...].astype(F32).reshape(4, 64, LANES), corner
        else:
            planes, edge = v_ref[x].astype(F32), yr_ref[pl.ds(16 * x, 16), :].astype(F32)
        if x % 2 == 0:
            out_ref, row = peven_ref, 32 * x
        else:
            out_ref, row = podd_ref, 32 * (x + 1)
        for b in range(3):
            for c in range(3):
                py, pz = (b + 1) % 2, (c + 1) % 2
                piece = planes[2 * py + pz]
                if b == 0:
                    piece = jnp.concatenate([edge[8 * pz : 8 * pz + 8], piece[0:56]], axis=0)
                if c == 0:
                    piece = jnp.where(first, 0.0, pltpu.roll(piece, 1, 0))
                column = (3 * b + c) * LANES
                out_ref[pl.ds(row, 64), pl.ds(column, LANES)] = piece.astype(BF16)
    before = (
        nt(podd_ref[0:512, :], wp_ref[:, 0:SLOTS9])
        + nt(peven_ref[...], wp_ref[:, SLOTS9 : 2 * SLOTS9])
        + nt(podd_ref[64:576, :], wp_ref[:, 2 * SLOTS9 : 3 * SLOTS9])
        + bias_ref[...]
    )
    square = before * before
    tanh = jnp.tanh(ROOT * before * (1.0 + CUBIC * square))
    hidden = (0.5 * before * (1.0 + tanh)).astype(BF16)
    slope = 0.5 * (1.0 + tanh) + 0.5 * before * (1.0 - tanh * tanh) * ROOT * (
        1.0 + 3.0 * CUBIC * square
    )
    slope_ref[...] = slope.T
    hidt_ref[...] = hidden.astype(F32).T.astype(BF16)

    for copy in copies:
        copy.wait()
    kh, kl = split(key_ref[...].T)
    vh, vl = split(val_ref[...])
    kt_ref[...] = kh
    vw_ref[...] = vh
    keys = nt(kh, hidden) + nt(kl, hidden)
    values = nn(hidden, vh) + nn(hidden, vl)
    queries = query_ref[...]
    qu = queries * lax.rsqrt(jnp.sum(queries * queries, axis=-1, keepdims=True) + EPS)
    key_norm = lax.rsqrt(jnp.sum(keys * keys, axis=0, keepdims=True) + EPS)
    kut = keys * key_norm
    kut_ref[...] = kut
    knt_ref[...] = jnp.broadcast_to(key_norm, (8, 512))
    weights = jnp.exp(TEMPER * nn(qu.astype(BF16), kut.astype(BF16)))
    wt_ref[...] = weights
    group = group_ref[...]
    shares = shared_out(group, weights)
    vb = values.astype(BF16)
    sums = nn(shares, jnp.concatenate([vb, jnp.ones((512, 64), BF16)], axis=1))
    cot = early_ref[:, 0:COUT]
    cott_ref[...] = cot.astype(F32).T.astype(BF16)
    meets = nt(cot, vb)
    total = jnp.zeros((8, 512), F32)
    for g in range(GROUPS):
        total = total + jnp.where(group == float(g), meets[8 * g : 8 * g + 8], 0.0)
    tt_ref[...] = total
    inner = jnp.sum(sums[:, 0:COUT] * cot.astype(F32), axis=-1, keepdims=True)
    lane = lax.broadcasted_iota(jnp.int32, (8, 64), 1)
    mass = jnp.zeros((8, 64), F32)
    dots = jnp.zeros((8, 64), F32)
    for g in range(GROUPS):
        mass = jnp.where(lane == g, sums[8 * g : 8 * g + 8, COUT:256], mass)
        dots = jnp.where(lane == g, inner[8 * g : 8 * g + 8], dots)
    table = jnp.concatenate([mass, dots], axis=0)
    send_ref[:, 0:COUT] = sums[:, 0:COUT].astype(BF16)
    send_ref[:, COUT:256] = jnp.concatenate([table.astype(BF16)] * 32, axis=0)


def backward_kernel(
    recv_ref, podd_ref, peven_ref, slope_ref, hidt_ref, kut_ref, knt_ref, wt_ref, tt_ref,
    group_ref, cott_ref, kt_ref, vw_ref, query_ref,
    pooled_ref, db_ref, xs_ref, ys_ref, keep_ref, give_ref, sum_ref,
):
    got = jnp.sum(recv_ref[...].reshape(32, 16, 256).astype(F32), axis=0)
    mass = got[0:8, COUT:256]
    dots = got[8:16, COUT:256]
    here = lax.axis_index("chip") * 2 + lax.axis_index("core")
    lane = lax.broadcasted_iota(jnp.int32, (8, 64), 1)
    own = [
        jnp.sum(jnp.where(lane == 2 * here + i, mass, 0.0), axis=-1, keepdims=True)
        for i in range(2)
    ]
    pooled_ref[...] = got[:, 0:COUT] / (1.0 + jnp.concatenate(own, axis=0))

    inverse = 1.0 / (1.0 + mass)
    d_mass = -dots * inverse * inverse
    ih, il = split(inverse)
    mh, ml = split(d_mass)
    group = group_ref[...]
    rows = lax.broadcasted_iota(jnp.int32, (64, 512), 0).astype(F32)
    member = (rows == jnp.broadcast_to(group[0:1], (64, 512))).astype(F32).astype(BF16)
    inv_row = nn(ih, member) + nn(il, member)
    dm_row = nn(mh, member) + nn(ml, member)
    weights = wt_ref[...]
    d_cos = TEMPER * weights * (tt_ref[...] * inv_row + dm_row)
    d_value = nn(cott_ref[...], shared_out(group, weights * inv_row))

    kut = kut_ref[...]
    queries = query_ref[...]
    qn = lax.rsqrt(jnp.sum(queries * queries, axis=-1, keepdims=True) + EPS)
    qu = queries * qn
    ch = d_cos.astype(BF16)
    d_ku = nn(qu.T.astype(BF16), ch)
    d_key = knt_ref[0:1, :] * (d_ku - kut * jnp.sum(kut * d_ku, axis=0, keepdims=True))
    d_qu = nt(ch, kut.astype(BF16))
    d_query = qn * (d_qu - qu * jnp.sum(qu * d_qu, axis=-1, keepdims=True))

    kh, vh = d_key.astype(BF16), d_value.astype(BF16)
    d_hidden = tn(kt_ref[...], kh) + nn(vw_ref[...], vh)
    d_before = d_hidden * slope_ref[...]
    dbt = d_before.astype(BF16)
    d_rows = d_before.T
    db = d_rows.astype(BF16)
    db_ref[...] = db
    xs_ref[...] = db[0:64]
    ys_ref[...] = d_rows.reshape(8, 64, COUT)[:, 0:8].reshape(64, COUT).astype(BF16)

    parts = (podd_ref[0:512, :], peven_ref[...], podd_ref[64:576, :])
    for a in range(3):
        grad = nn(dbt, parts[a])
        for tap in range(9):
            piece = grad[:, tap * LANES : tap * LANES + CIN]
            sum_ref[:, pl.ds((9 * a + tap) * CIN, CIN)] = piece
    sum_ref[:, KDIM : KDIM + COUT] = nt(hidt_ref[...], kh)
    sum_ref[:, KDIM + COUT : KDIM + 2 * COUT] = nt(hidt_ref[...], vh)
    bias = jnp.broadcast_to(jnp.sum(d_rows, axis=0, keepdims=True), (8, COUT))
    small = [d_query[:, 0:CIN], d_query[:, CIN:COUT], bias[:, 0:CIN], bias[:, CIN:COUT]]
    small = jnp.concatenate(small + [jnp.zeros((COUT - 32, CIN), F32)], axis=0)
    sum_ref[:, KDIM + 2 * COUT : WIDE] = small
    low = lax.axis_index("core") == 0
    for t in range(12):
        left = sum_ref[:, LANES * t : LANES * (t + 1)]
        right = sum_ref[:, LANES * (t + 12) : LANES * (t + 13)]
        keep_ref[COUT * t : COUT * (t + 1), :] = jnp.where(low, left, right)
        give_ref[COUT * t : COUT * (t + 1), :] = jnp.where(low, right, left).astype(BF16)


def add_kernel(a_ref, b_ref, out_ref):
    out_ref[0:USED, :] = (a_ref[...] + b_ref[...].astype(F32)).astype(BF16)
    out_ref[USED:HALF, :] = jnp.zeros((HALF - USED, LANES), BF16)


def total_kernel(recv_ref, out_ref):
    total = jnp.sum(recv_ref[...].astype(F32), axis=0).astype(BF16)
    out_ref[...] = jnp.broadcast_to(total[None], out_ref.shape)


def final_kernel(mine_ref, other_ref, dw_ref, dk_ref, dv_ref, dq_ref, dbias_ref, all_ref):
    low = lax.axis_index("core") == 0
    for t in range(12):
        mine = mine_ref[COUT * t : COUT * (t + 1), :].astype(F32)
        other = other_ref[COUT * t : COUT * (t + 1), :].astype(F32)
        all_ref[:, LANES * t : LANES * (t + 1)] = jnp.where(low, mine, other)
        all_ref[:, LANES * (t + 12) : LANES * (t + 13)] = jnp.where(low, other, mine)
    dw_ref[...] = all_ref[:, 0:KDIM]
    dk_ref[...] = all_ref[:, KDIM : KDIM + COUT]
    dv_ref[...] = all_ref[:, KDIM + COUT : KDIM + 2 * COUT]
    small = all_ref[0:32, KDIM + 2 * COUT : WIDE]
    dq_ref[...] = jnp.concatenate([small[0:8], small[8:16]], axis=1)
    dbias_ref[...] = jnp.concatenate([small[16:17], small[24:25]], axis=1)


def spread_kernel(
    near_ref, w_ref, db_ref, xr_ref, yr_ref, xyr_ref, occ_ref, out_ref,
    ext_ref, even_ref, odd_ref, rows_ref, slot_ref, wp_ref,
):
    wp_ref[...] = jnp.zeros_like(wp_ref)
    find_slots(near_ref, slot_ref)
    edge = yr_ref[...].astype(F32)
    for jx in range(8):
        ext_ref[pl.ds(72 * jx, 64), :] = db_ref[pl.ds(64 * jx, 64), :].astype(F32)
        ext_ref[pl.ds(72 * jx + 64, 8), :] = edge[8 * jx : 8 * jx + 8]
    ext_ref[pl.ds(576, 64), :] = xr_ref[...].astype(F32)
    ext_ref[pl.ds(640, 8), :] = xyr_ref[...].astype(F32)[0:8]
    low = ext_ref[0:576, :].astype(BF16)
    high = ext_ref[72:648, :].astype(BF16)
    for number in range(27):
        wp_ref[:, pl.ds(number * LANES, CIN)] = w_ref[:, pl.ds(number * CIN, CIN)]
    even_ref[...] = nn(low, wp_ref[:, SLOTS9 : 2 * SLOTS9])
    odd_ref[...] = nn(low, wp_ref[:, 2 * SLOTS9 : 3 * SLOTS9]) + nn(high, wp_ref[:, 0:SLOTS9])
    last = lax.broadcasted_iota(jnp.int32, (32, LANES), 0) % 8 == 7

    def up(piece):
        return jnp.where(last, 0.0, pltpu.roll(piece, 31, 0))

    for by in range(2):
        for bx in range(2):
            for xl in range(8):
                x = 8 * bx + xl
                src_ref = even_ref if x % 2 == 0 else odd_ref
                start = 72 * (x // 2) + 32 * by

                def tap(b, c, later, src_ref=src_ref, start=start):
                    return src_ref[pl.ds(start + 8 * later, 32), pl.ds((3 * b + c) * LANES, LANES)]

                e00 = tap(1, 1, 0)
                e01 = tap(1, 2, 0) + up(tap(1, 0, 0))
                e10 = tap(2, 1, 0) + tap(0, 1, 1)
                e11 = tap(2, 2, 0) + tap(0, 2, 1) + up(tap(2, 0, 0) + tap(0, 0, 1))
                for pz, (ye, yo) in enumerate(((e00, e10), (e01, e11))):
                    both = jnp.stack([ye.reshape(4, 8, LANES), yo.reshape(4, 8, LANES)], axis=1)
                    rows_ref[pl.ds(128 * xl + pz, 64, stride=2), :] = both.reshape(64, LANES)
            tile = rows_ref[...].reshape(64, 2, 8, LANES)
            for bz in range(2):
                place = bx + 2 * by + 4 * bz
                slot = slot_ref[place]
                block = tile[:, bz].reshape(512, LANES).T[0:CIN]
                block = jnp.where(occ_ref[pl.ds(slot, 1), :] > 0, block, 0.0)
                out_ref[slot] = block.astype(BF16)


def vm():
    return pl.BlockSpec(memory_space=pltpu.VMEM)


def like(shape, dtype=F32):
    return jax.ShapeDtypeStruct(shape, dtype)


def call(kernel, kinds, outs, scratch, *args):
    spaces = {"s": pltpu.SMEM, "h": pltpu.HBM, "v": pltpu.VMEM}
    kinds = kinds + "v" * (len(args) - len(kinds))
    in_specs = [pl.BlockSpec(memory_space=spaces[kind]) for kind in kinds]
    args = [
        pltpu.with_memory_space_constraint(arg, pltpu.HBM) if kind == "h" else arg
        for arg, kind in zip(args, kinds, strict=True)
    ]
    return pl.pallas_call(
        kernel,
        out_shape=outs,
        in_specs=in_specs,
        out_specs=jax.tree.map(lambda _: vm(), outs),
        scratch_shapes=scratch,
        compiler_params=params(),
        name=kernel.__name__,
    )(*args)


def shift(shard, by_x, by_y):
    pairs = []
    for index in range(32):
        tx, ty = index % 8 + by_x, index // 8 + by_y
        if 0 <= tx < 8 and 0 <= ty < 4:
            pairs.append((index, ty * 8 + tx))
    return lax.ppermute(shard, SPACE, pairs)


def on_device(
    features, occupancy, neighbors, routes, cotangent, conv_weight, conv_bias,
    key_weight, value_weight, queries,
):
    features, occupancy = jnp.swapaxes(features[0], 1, 2), occupancy[0]
    slots = pltpu.SMEM((8,), jnp.int32)
    v, xs, ys, early = call(
        place_kernel, "hhhh",
        [
            like((16, 4, 64, LANES), BF16), like((256, LANES), BF16), like((256, LANES), BF16),
            like((32, 16, 3 * LANES), BF16),
        ],
        [
            pltpu.SMEM((6, 8), jnp.int32), pltpu.VMEM((8, CIN, 512), BF16),
            pltpu.VMEM((8, 512), jnp.int32), pltpu.VMEM((16, COUT), F32),
            pltpu.VMEM((1024, LANES), F32), slots, pltpu.SemaphoreType.DMA((4,)),
        ],
        neighbors, features, occupancy, cotangent.reshape(16, COUT),
    )
    early = lax.all_to_all(early, SPACE, 0, 0, tiled=True).reshape(512, 3 * LANES)
    xr = shift(xs, 1, 0)
    yr = shift(ys, 0, 1)
    wp, group = call(
        prepare_kernel, "sh",
        [
            like((COUT, 27 * LANES), BF16), like((8, 512)),
        ],
        [
            slots, pltpu.VMEM((8, 64), jnp.int32), pltpu.VMEM((COUT, KDIM), BF16),
            pltpu.SemaphoreType.DMA((4,)),
        ],
        neighbors, conv_weight.T, routes.reshape(1, 512),
    )
    podd, peven, slope, hidt, cott, kut, knt, wt, tt, kt, vw, send = call(
        forward_kernel, "hhh",
        [
            like((576, SLOTS9), BF16), like((512, SLOTS9), BF16), like((COUT, 512)),
            like((COUT, 512), BF16), like((COUT, 512), BF16), like((COUT, 512)), like((8, 512)),
            like((8, 512)), like((8, 512)), like((COUT, COUT), BF16),
            like((COUT, COUT), BF16), like((512, 256), BF16),
        ],
        [
            pltpu.VMEM((COUT, COUT), F32), pltpu.VMEM((COUT, COUT), F32),
            pltpu.VMEM((NQ, COUT), F32), pltpu.SemaphoreType.DMA((3,)),
        ],
        key_weight, value_weight, queries, v, xr, yr, conv_bias.reshape(1, COUT), wp, group, early,
    )
    recv = lax.all_to_all(send.reshape(32, 16, 256), SPACE, 0, 0, tiled=True).reshape(512, 256)
    pooled, db, bxs, bys, keep, give = call(
        backward_kernel, "",
        [
            like((16, COUT)), like((512, COUT), BF16), like((64, COUT), BF16),
            like((64, COUT), BF16), like((USED, LANES)), like((USED, LANES), BF16),
        ],
        [pltpu.VMEM((COUT, WIDE), F32)],
        recv, podd, peven, slope, hidt, kut, knt, wt, tt, group, cott, kt, vw, queries,
    )
    swap = [(0, 1), (1, 0)]
    taken = lax.ppermute(give, "core", swap)
    half = call(add_kernel, "", like((HALF, LANES), BF16), [], keep, taken)
    pieces = lax.all_to_all(half.reshape(64, SHARD, LANES), CHIPS, 0, 0, tiled=True)
    bxr = shift(bxs, -1, 0)
    byr = shift(bys, 0, -1)
    bxyr = shift(bys[0:16], -1, -1)
    copies = call(total_kernel, "", like((64, SHARD, LANES), BF16), [], pieces)
    db, bxr, byr, copies = lax.optimization_barrier((db, bxr, byr, copies))
    mine = lax.all_to_all(copies, CHIPS, 0, 0, tiled=True).reshape(HALF, LANES)
    d_features = call(
        spread_kernel, "s", like((8, CIN, 512), BF16),
        [
            pltpu.VMEM((648, COUT), F32), pltpu.VMEM((576, SLOTS9), F32),
            pltpu.VMEM((576, SLOTS9), F32), pltpu.VMEM((1024, LANES), F32), slots,
            pltpu.VMEM((COUT, 27 * LANES), BF16),
        ],
        neighbors, conv_weight.T, db, bxr, byr, bxyr, occupancy,
    )
    mine, d_features = lax.optimization_barrier((mine, d_features))
    other = lax.ppermute(mine, "core", swap)
    d_weight, d_key, d_value, d_query, d_bias = call(
        final_kernel, "",
        [
            like((COUT, KDIM)), like((COUT, COUT)), like((COUT, COUT)), like((NQ, COUT)),
            like((1, COUT)),
        ],
        [pltpu.VMEM((COUT, WIDE), F32)],
        mine, other,
    )
    return (
        pooled.reshape(1, 2, NQ, COUT), jnp.swapaxes(d_features, 1, 2)[None], d_weight.T,
        d_bias.reshape(COUT), d_key, d_value, d_query,
    )


def solution(mesh):
    fine = Mesh(mesh.devices.reshape(4, 16, 2), ("section", "chip", "core"))
    in_specs = (
        P("section", SPACE, None, None),
        P("section", SPACE, None),
        P(None, SPACE),
        P("section", SPACE, None),
        P("section", SPACE, None, None),
        P(),
        P(),
        P(),
        P(),
        P(),
    )
    out_specs = (
        P("section", SPACE, None, None),
        P("section", SPACE, None, None),
        P(),
        P(),
        P(),
        P(),
        P(),
    )
    return jax.shard_map(
        on_device, mesh=fine, in_specs=in_specs, out_specs=out_specs, check_vma=False
    )
```
